512 devices in a mesh: kstr: 16 (over y, z_lo), pw: 32 (over x, z_hi, core).
Axes of the slice: x: 4, y: 8, z: 8 (z_hi: 4, z_lo: 2; z = z_hi * 2 + z_lo), core: 2. Of those that a mesh axis runs over, the one named last changes fastest.
Arguments:
- states_re: bfloat16 [16, 256, 16384], P('kstr', None, 'pw'), may hold values from -8 to 8
- states_im: bfloat16 [16, 256, 16384], P('kstr', None, 'pw'), may hold values from -8 to 8
- gmap: int32 [16384], P('pw'), may hold values from 0 to 16383, as said below
Outputs:
- new_re: bfloat16 [16, 256, 16384], P('kstr', None, 'pw')
- new_im: bfloat16 [16, 256, 16384], P('kstr', None, 'pw')
The draws below stay inside these ranges and needn't reach their ends.
Inputs may be any that keep to these rules, and one draw needn't show every extreme that they name: gmap[G] = (G + o) mod 16384 for one offset o with 1 <= o < 16384.
All inputs are finite; a program needn't handle non-finite values.
Results may differ from the reference program's by a relative error of at most 0.008.
Values may be sent and summed in bfloat16 or wider, within the bound.
No kernel may reach another device: no remote copies, remote signals or barrier semaphores. Data moves between devices by JAX's collectives and lax.ppermute only.
A program may use at most 64 MiB of HBM per device.

```python
import jax
import jax.numpy as jnp
from jax import lax

NB = 256
NPW = 16384
NEWTON = 4
STEPS = 2
NK = 16


def state_parts(key):
    base_key = jax.random.fold_in(key, 7)
    noise_key = jax.random.fold_in(key, 8)
    kpos = jnp.arange(NK, dtype=jnp.float32) / max(NK - 1, 1)
    base = jax.random.normal(base_key, (2, 1, NB, NPW), jnp.float32) * 0.7071
    noise = jax.random.normal(noise_key, (2, NK, NB, NPW), jnp.float32) * 0.7071
    bands = jnp.ones((1, 1, NB, 1), jnp.float32)
    amplitude = 1.0 / (1.0 + 2.0 * kpos)
    level = (0.15 * (1.0 + 2.0 * kpos))[None, :, None, None]
    gpos = jnp.arange(NPW, dtype=jnp.float32) / NPW
    column = (0.6 + 0.8 * gpos)[None, None, None, :]
    field = jnp.clip(amplitude[None, :, None, None] * (base + level * column * bands * noise), -8.0, 8.0)
    return (field[0], field[1])


def draw_states_re(key, part):
    return state_parts(key)[0].astype(jnp.bfloat16)


def draw_states_im(key, part):
    return state_parts(key)[1].astype(jnp.bfloat16)


def draw_gmap(key, part):
    offset = jax.random.randint(jax.random.fold_in(key, 11), (), 1, NPW)
    index = jnp.arange(NPW, dtype=jnp.int32)
    return jnp.mod(index + offset, NPW).astype(jnp.int32)


def setup_inputs(seed: int = 0) -> dict:
    key_list = jax.random.split(jax.random.key(seed), 4)
    states_re = draw_states_re(jax.random.fold_in(key_list[3], 71), 0)
    states_im = draw_states_im(jax.random.fold_in(key_list[3], 71), 0)
    gmap = draw_gmap(jax.random.fold_in(key_list[3], 71), 0)
    return {"states_re": states_re, "states_im": states_im, "gmap": gmap}


HIGH = lax.Precision.HIGHEST
EPS_SCALE = 1e-06
EPS_NORM = 1e-06
TAU_STEP = 0.25

def complex_mul(a_re, a_im, b_re, b_im):

    def matmul(left, right):
        return jnp.einsum('kij,kjl->kil', left, right, precision=HIGH)
    return (matmul(a_re, b_re) - matmul(a_im, b_im), matmul(a_re, b_im) + matmul(a_im, b_re))

def invert(s_re, s_im):
    magnitude = jnp.sqrt(s_re * s_re + s_im * s_im)
    colmax = lax.optimization_barrier(jnp.max(lax.optimization_barrier(jnp.sum(magnitude, axis=1)), axis=1))
    rowmax = lax.optimization_barrier(jnp.max(lax.optimization_barrier(jnp.sum(magnitude, axis=2)), axis=1))
    factor = (1.0 / (colmax * rowmax + EPS_SCALE))[:, None, None]
    x_re = jnp.swapaxes(s_re, 1, 2) * factor
    x_im = -jnp.swapaxes(s_im, 1, 2) * factor
    for turn in range(NEWTON):
        p_re, p_im = complex_mul(s_re, s_im, x_re, x_im)
        q_re, q_im = complex_mul(x_re, x_im, p_re, p_im)
        x_re = 2.0 * x_re - q_re
        x_im = 2.0 * x_im - q_im
    return (x_re, x_im)

def product(form, left, right):
    return jnp.einsum(form, left.astype(jnp.float32), right.astype(jnp.float32), precision=HIGH)

def reference(states_re, states_im, gmap):
    field_re, field_im = (states_re, states_im)
    for step in range(STEPS):
        next_re = jnp.concatenate([field_re[1:], field_re[:1][:, :, gmap]], 0)
        next_im = jnp.concatenate([field_im[1:], field_im[:1][:, :, gmap]], 0)
        s_re = (product('kmg,kng->kmn', field_re, next_re) + product('kmg,kng->kmn', field_im, next_im)) / NPW
        s_im = (product('kmg,kng->kmn', field_re, next_im) - product('kmg,kng->kmn', field_im, next_re)) / NPW
        x_re, x_im = invert(s_re, s_im)
        xb_re = x_re.astype(jnp.bfloat16)
        xb_im = x_im.astype(jnp.bfloat16)
        a_re = product('kmn,kmg->kng', xb_re, next_re) - product('kmn,kmg->kng', xb_im, next_im)
        a_im = product('kmn,kmg->kng', xb_re, next_im) + product('kmn,kmg->kng', xb_im, next_re)
        c_re = (product('kmn,kmg->kng', xb_re, field_re) + product('kmn,kmg->kng', xb_im, field_im)).astype(jnp.bfloat16)
        c_im = (product('kmn,kmg->kng', xb_re, field_im) - product('kmn,kmg->kng', xb_im, field_re)).astype(jnp.bfloat16)
        head_re = jnp.zeros_like(c_re[-1]).at[:, gmap].set(c_re[-1])
        head_im = jnp.zeros_like(c_im[-1]).at[:, gmap].set(c_im[-1])
        d_re = jnp.concatenate([head_re[None], c_re[:-1]], 0).astype(jnp.float32)
        d_im = jnp.concatenate([head_im[None], c_im[:-1]], 0).astype(jnp.float32)
        g_re = a_im - d_im
        g_im = d_re - a_re
        total = jnp.sum(g_re * g_re + g_im * g_im)
        rms = jnp.sqrt(total / (2 * NK * NB * NPW) + EPS_NORM)
        field_re = (field_re.astype(jnp.float32) + TAU_STEP * g_re / rms).astype(jnp.bfloat16)
        field_im = (field_im.astype(jnp.float32) + TAU_STEP * g_im / rms).astype(jnp.bfloat16)
    return (field_re, field_im)
```

```python
import jax
import jax.numpy as jnp
from jax import lax
from jax.experimental import pallas as pl
from jax.experimental.pallas import tpu as pltpu
from jax.sharding import PartitionSpec as P

NEWTON = 4
NK = 16
NPW = 16384
NB = 256
PARTS = 32
EPS_SCALE = 1e-06
EPS_NORM = 1e-06
TAU_STEP = 0.25
F32 = jnp.float32
BF16 = jnp.bfloat16


def call(kernel, outs, *args, smem=0, flops=0):
    specs = [pl.BlockSpec(memory_space=pltpu.SMEM)] * smem
    specs += [pl.BlockSpec(memory_space=pltpu.VMEM)] * (len(args) - smem)
    single = not isinstance(outs, (tuple, list))
    outs = (outs,) if single else tuple(outs)
    moved = sum(a.size * a.dtype.itemsize for a in args) + sum(
        o.size * o.dtype.itemsize for o in outs
    )
    result = pl.pallas_call(
        kernel,
        out_shape=outs,
        in_specs=specs,
        out_specs=tuple(pl.BlockSpec(memory_space=pltpu.VMEM) for _ in outs),
        compiler_params=pltpu.CompilerParams(vmem_limit_bytes=36 * 1024 * 1024),
        cost_estimate=pl.CostEstimate(flops=flops, bytes_accessed=moved, transcendentals=0),
    )(*args)
    return result[0] if single else result


def shape(dims, dtype):
    return jax.ShapeDtypeStruct(dims, dtype)


def dot(left, right):
    return jnp.dot(left, right, preferred_element_type=F32)


def margin(left, right, out_ref):
    every = lax.dot_general(left, right, (((1,), (1,)), ((), ())), preferred_element_type=F32)
    out_ref[:NB, :] = (every[:NB, :NB] + every[NB:, NB:]).astype(out_ref.dtype)
    out_ref[NB:, :] = (every[:NB, NB:] - every[NB:, :NB]).astype(out_ref.dtype)


def margin_kernel(state_ref, next_ref, out_ref):
    margin(state_ref[...], next_ref[...], out_ref)


def rotate_kernel(amount_ref, block_ref, out_ref, rolled_ref):
    count, rows, width = block_ref.shape
    amount = amount_ref[0]
    first = amount // width
    rest = amount - first * width
    turn = lax.rem(width - rest, width)

    def roll(index, carry):
        rolled_ref[index] = pltpu.roll(block_ref[index].astype(F32), turn, 1)
        return carry

    lax.fori_loop(0, count, roll, 0, unroll=4)
    lane = lax.broadcasted_iota(jnp.int32, (rows, width), 1)

    def place(index, carry):
        here = lax.rem(index + first, count)
        after = lax.rem(index + first + 1, count)
        value = jnp.where(lane < width - rest, rolled_ref[here], rolled_ref[after])
        out_ref[index] = value.astype(BF16)
        return carry

    lax.fori_loop(0, count, place, 0, unroll=4)


def rotate(amount, block):
    return pl.pallas_call(
        rotate_kernel,
        out_shape=shape(block.shape, BF16),
        in_specs=[
            pl.BlockSpec(memory_space=pltpu.SMEM),
            pl.BlockSpec(memory_space=pltpu.VMEM),
        ],
        out_specs=pl.BlockSpec(memory_space=pltpu.VMEM),
        scratch_shapes=[pltpu.VMEM(block.shape, F32)],
        compiler_params=pltpu.CompilerParams(vmem_limit_bytes=36 * 1024 * 1024),
    )(amount, block)


def collect_kernel(parts_ref, out_ref):
    total = jnp.sum(parts_ref[...].astype(F32), axis=0) * (1.0 / NPW)
    out_ref[...] = jnp.broadcast_to(total.astype(out_ref.dtype)[None], out_ref.shape)


def spread_kernel(parts_ref, out_ref):
    total = jnp.sum(parts_ref[...], axis=0)
    out_ref[...] = jnp.broadcast_to(total[None], out_ref.shape)


def pieces(value, count):
    high = value.astype(BF16)
    if count == 1:
        return [high]
    return [high, (value - high.astype(F32)).astype(BF16)]


def newton_kernel(margin_ref, out_ref):
    stacked = margin_ref[...]
    whole = stacked.astype(F32)
    real, imag = whole[:NB], whole[NB:]
    magnitude = jnp.sqrt(real * real + imag * imag)
    colmax = jnp.max(jnp.sum(magnitude, axis=0, keepdims=True), axis=1, keepdims=True)
    rowmax = jnp.max(jnp.sum(magnitude, axis=1, keepdims=True), axis=0, keepdims=True)
    factor = 1.0 / (colmax * rowmax + EPS_SCALE)
    iterate = jnp.concatenate([real * factor, imag * factor], 1)

    for turn in range(NEWTON):
        parts = pieces(iterate, 2)
        product = None
        for part in parts:
            crossed = jnp.concatenate([part[:, NB:], -part[:, :NB]], 1)
            right = jnp.concatenate([part, crossed], 0)
            term = lax.dot_general(
                stacked, right, (((0,), (0,)), ((), ())), preferred_element_type=F32
            )
            product = term if product is None else product + term
        seconds = pieces(product, 2)
        change = None
        for j, second in enumerate(seconds):
            crossed = jnp.concatenate([-second[:, NB:], second[:, :NB]], 1)
            right = jnp.concatenate([second, crossed], 0)
            for i, part in enumerate(parts):
                if i + j < 2:
                    term = dot(part, right)
                    change = term if change is None else change + term
        iterate = 2.0 * iterate - change
    out_ref[...] = iterate.astype(BF16)


def slope(dual, following, dual_before, before):
    real, imag = dual[:, :NB], dual[:, NB:]
    forward = jnp.concatenate(
        [jnp.concatenate([-imag, real], 1), jnp.concatenate([-real, -imag], 1)], 0
    )
    real, imag = dual_before[:, :NB], dual_before[:, NB:]
    backward = jnp.concatenate(
        [jnp.concatenate([imag, real], 1), jnp.concatenate([-real, imag], 1)], 0
    )
    return dot(forward, following) - dot(backward, before).astype(BF16).astype(F32)


def squares(grad, count):
    part = grad[0:8]
    part = part * part
    for row in range(8, grad.shape[0], 8):
        more = grad[row : row + 8]
        part = part + more * more
    part = part[:, 0:128] + part[:, 128:256] + part[:, 256:384] + part[:, 384:512]
    return jnp.broadcast_to(part[None], (count, 8, 128))


def slopes_kernel(y_2, y_1, y0, y1, p_2, p_1, p0, p1, p2, g_1, g0, g1, total_ref):
    grad = slope(y0[...], p1[...], y_1[...], p_1[...])
    g0[...] = grad
    total_ref[...] = squares(grad, PARTS)
    g_1[...] = slope(y_1[...], p0[...], y_2[...], p_2[...])
    g1[...] = slope(y1[...], p2[...], y0[...], p0[...])


def last_slope_kernel(y_1, y0, p_1, p1, g0, total_ref):
    grad = slope(y0[...], p1[...], y_1[...], p_1[...])
    g0[...] = grad
    total_ref[...] = squares(grad, PARTS)


def step_size(total_ref):
    part = jnp.sum(total_ref[...], axis=0)
    total = jnp.sum(jnp.sum(part, axis=1, keepdims=True), axis=0, keepdims=True)
    return TAU_STEP / jnp.sqrt(total / (2 * NK * NB * NPW) + EPS_NORM)


def advance_kernel(total_ref, p_1, p0, p1, g_1, g0, g1, q_1, q0, q1, out_ref):
    size = step_size(total_ref)
    q_1[...] = (p_1[...].astype(F32) + size * g_1[...]).astype(BF16)
    here = (p0[...].astype(F32) + size * g0[...]).astype(BF16)
    ahead = (p1[...].astype(F32) + size * g1[...]).astype(BF16)
    q0[...] = here
    q1[...] = ahead
    margin(here, ahead, out_ref)


def finish_kernel(total_ref, p0, g0, re_ref, im_ref):
    size = step_size(total_ref)
    value = (p0[...].astype(F32) + size * g0[...]).astype(BF16)
    re_ref[...] = value[:NB]
    im_ref[...] = value[NB:]


def shifted(value, by):
    return lax.ppermute(value, "kstr", [(i, (i + by) % NK) for i in range(NK)])


def exchange(value, axis):
    return lax.all_to_all(value, axis, 0, 0, tiled=True)


def whole_margin(part):
    rows = 2 * NB // PARTS
    parts = exchange(part, "pw").reshape(PARTS, rows, NB)
    own = call(collect_kernel, shape((PARTS, rows, NB), BF16), parts)
    return exchange(own.reshape(2 * NB, NB), "pw")


def whole_total(part):
    parts = exchange(part, "pw")
    own = call(spread_kernel, shape((NK, 8, 128), F32), parts)
    return exchange(own, "kstr")


def inverse(whole):
    return call(newton_kernel, shape((NB, 2 * NB), BF16), whole)


def body(states_re, states_im, gmap):
    width = states_re.shape[2]
    row = lax.axis_index("kstr")
    offset = jnp.mod(gmap[0] - lax.axis_index("pw") * width, NPW)
    amount = jnp.where(row < NK // 2, offset, NPW - offset).astype(jnp.int32)
    state = jnp.concatenate([states_re[0], states_im[0]], 0)
    full = 2 * NB
    duals = shape((NB, full), BF16)
    fields = shape((full, width), BF16)
    grads = shape((full, width), F32)
    margins = shape((full, NB), BF16)
    totals = shape((PARTS, 8, 128), F32)

    blocks = exchange(state, "pw").reshape(PARTS, full // PARTS, width)
    turned = exchange(rotate(amount.reshape(1), blocks).reshape(full, width), "pw")

    p1 = shifted(jnp.where(row == 0, turned, state), -1)
    part = call(margin_kernel, margins, state, p1)
    state, turned, part = lax.optimization_barrier((state, turned, part))
    p_1 = shifted(jnp.where(row == NK - 1, turned, state), 1)
    p2 = shifted(jnp.where(row <= 1, turned, state), -2)
    p_2 = shifted(jnp.where(row >= NK - 2, turned, state), 2)

    y0 = inverse(whole_margin(part))
    y_1 = shifted(y0, 1)
    y1 = shifted(y0, -1)
    y_2 = shifted(y0, 2)
    g_1, g0, g1, total = call(
        slopes_kernel,
        (grads, grads, grads, totals),
        *(y_2, y_1, y0, y1, p_2, p_1, state, p1, p2),
    )
    total = whole_total(total)
    q_1, q0, q1, part = call(
        advance_kernel,
        (fields, fields, fields, margins),
        *(total, p_1, state, p1, g_1, g0, g1),
    )

    y0 = inverse(whole_margin(part))
    y_1 = shifted(y0, 1)
    g0, total = call(last_slope_kernel, (grads, totals), y_1, y0, q_1, q1)
    total = whole_total(total)
    half = shape((NB, width), BF16)
    new_re, new_im = call(finish_kernel, (half, half), total, q0, g0)
    return new_re[None], new_im[None]


def solution(mesh):
    placed = (P("kstr", None, "pw"), P("kstr", None, "pw"), P("pw"))
    return jax.shard_map(
        body,
        mesh=mesh,
        in_specs=placed,
        out_specs=(P("kstr", None, "pw"), P("kstr", None, "pw")),
        check_vma=False,
    )
```

```python
import jax
import jax.numpy as jnp
from jax import lax
from jax.experimental import pallas as pl
from jax.experimental.pallas import tpu as pltpu
from jax.sharding import PartitionSpec as P

NEWTON = 4
NK = 16
NPW = 16384
NB = 256
PARTS = 32
EPS_SCALE = 1e-06
EPS_NORM = 1e-06
TAU_STEP = 0.25
F32 = jnp.float32
BF16 = jnp.bfloat16


def call(kernel, outs, *args, smem=0, flops=0):
    specs = [pl.BlockSpec(memory_space=pltpu.SMEM)] * smem
    specs += [pl.BlockSpec(memory_space=pltpu.VMEM)] * (len(args) - smem)
    single = not isinstance(outs, (tuple, list))
    outs = (outs,) if single else tuple(outs)
    moved = sum(a.size * a.dtype.itemsize for a in args) + sum(
        o.size * o.dtype.itemsize for o in outs
    )
    result = pl.pallas_call(
        kernel,
        out_shape=outs,
        in_specs=specs,
        out_specs=tuple(pl.BlockSpec(memory_space=pltpu.VMEM) for _ in outs),
        compiler_params=pltpu.CompilerParams(vmem_limit_bytes=36 * 1024 * 1024),
        cost_estimate=pl.CostEstimate(flops=flops, bytes_accessed=moved, transcendentals=0),
    )(*args)
    return result[0] if single else result


def shape(dims, dtype):
    return jax.ShapeDtypeStruct(dims, dtype)


def dot(left, right):
    return jnp.dot(left, right, preferred_element_type=F32)


def margin(left, right, out_ref):
    every = lax.dot_general(left, right, (((1,), (1,)), ((), ())), preferred_element_type=F32)
    out_ref[:NB, :] = (every[:NB, :NB] + every[NB:, NB:]).astype(out_ref.dtype)
    out_ref[NB:, :] = (every[:NB, NB:] - every[NB:, :NB]).astype(out_ref.dtype)


def margin_kernel(last_ref, state_ref, next_ref, closing_ref, out_ref, chosen_ref):
    following = next_ref[...]

    @pl.when(last_ref[0] == 1)
    def _():
        chosen_ref[...] = closing_ref[...]

    @pl.when(last_ref[0] != 1)
    def _():
        chosen_ref[...] = following

    margin(state_ref[...], chosen_ref[...], out_ref)


def prepare_kernel(turn_ref, re_ref, im_ref, out_ref, send_ref):
    for part, ref in enumerate((re_ref, im_ref)):
        rows = pl.ds(part * NB, NB)
        value = ref[...]
        out_ref[rows, :] = value
        send_ref[rows, :] = pltpu.roll(value.astype(F32), turn_ref[0], 1).astype(BF16)


def turn_kernel(turn_ref, in_ref, out_ref):
    out_ref[...] = pltpu.roll(in_ref[...].astype(F32), turn_ref[0], 1).astype(BF16)


def closing_pairs(by):
    pairs = []
    for j in range(PARTS):
        down, up = (j - by) % PARTS, (j + by) % PARTS
        last = (NK - 1) * PARTS
        pairs.append((j, last + down))
        pairs.append((PARTS + j, last - PARTS + down))
        pairs.append((last + j, up))
        pairs.append((last - PARTS + j, PARTS + up))
    return pairs


def close_string(send, blocks, rest):
    rows, width = send.shape
    lane = lax.broadcasted_iota(jnp.int32, (rows, width), 1)
    step = width // 4

    def branch(index):
        by, part = divmod(index, 4)
        near, far = width - step * part, step * (part + 1)

        def run(value, rest):
            one = lax.ppermute(value[:, :near], ("kstr", "pw"), closing_pairs(by))
            two = lax.ppermute(value[:, width - far :], ("kstr", "pw"), closing_pairs(by + 1))
            one = jnp.pad(one, ((0, 0), (0, width - near)))
            two = jnp.pad(two, ((0, 0), (width - far, 0)))
            return jnp.where(lane < width - rest, one, two)

        return run

    index = blocks * 4 + rest // step
    return lax.switch(index, [branch(i) for i in range(4 * PARTS)], send, rest)


def collect_kernel(parts_ref, out_ref):
    total = jnp.sum(parts_ref[...].astype(F32), axis=0) * (1.0 / NPW)
    out_ref[...] = jnp.broadcast_to(total.astype(out_ref.dtype)[None], out_ref.shape)


def spread_kernel(parts_ref, out_ref):
    total = jnp.sum(parts_ref[...], axis=0)
    out_ref[...] = jnp.broadcast_to(total[None], out_ref.shape)


def pieces(value, count):
    high = value.astype(BF16)
    if count == 1:
        return [high]
    return [high, (value - high.astype(F32)).astype(BF16)]


def newton_kernel(margin_ref, out_ref):
    stacked = margin_ref[...]
    whole = stacked.astype(F32)
    real, imag = whole[:NB], whole[NB:]
    magnitude = jnp.sqrt(real * real + imag * imag)
    colmax = jnp.max(jnp.sum(magnitude, axis=0, keepdims=True), axis=1, keepdims=True)
    rowmax = jnp.max(jnp.sum(magnitude, axis=1, keepdims=True), axis=0, keepdims=True)
    factor = 1.0 / (colmax * rowmax + EPS_SCALE)
    iterate = jnp.concatenate([real * factor, imag * factor], 1)

    for turn in range(NEWTON):
        parts = pieces(iterate, 2)
        product = None
        for part in parts:
            crossed = jnp.concatenate([part[:, NB:], -part[:, :NB]], 1)
            right = jnp.concatenate([part, crossed], 0)
            term = lax.dot_general(
                stacked, right, (((0,), (0,)), ((), ())), preferred_element_type=F32
            )
            product = term if product is None else product + term
        seconds = pieces(product, 2)
        change = None
        for j, second in enumerate(seconds):
            crossed = jnp.concatenate([-second[:, NB:], second[:, :NB]], 1)
            right = jnp.concatenate([second, crossed], 0)
            for i, part in enumerate(parts):
                if i + j < 2:
                    term = dot(part, right)
                    change = term if change is None else change + term
        iterate = 2.0 * iterate - change
    out_ref[...] = iterate.astype(BF16)


def slope(dual, following, dual_before, before):
    real, imag = dual[:, :NB], dual[:, NB:]
    forward = jnp.concatenate(
        [jnp.concatenate([-imag, real], 1), jnp.concatenate([-real, -imag], 1)], 0
    )
    real, imag = dual_before[:, :NB], dual_before[:, NB:]
    backward = jnp.concatenate(
        [jnp.concatenate([imag, real], 1), jnp.concatenate([-real, imag], 1)], 0
    )
    return dot(forward, following) - dot(backward, before).astype(BF16).astype(F32)


def squares(grad, count):
    part = grad[0:8]
    part = part * part
    for row in range(8, grad.shape[0], 8):
        more = grad[row : row + 8]
        part = part + more * more
    part = part[:, 0:128] + part[:, 128:256] + part[:, 256:384] + part[:, 384:512]
    return jnp.broadcast_to(part[None], (count, 8, 128))


def sides_kernel(y_2, y_1, y0, y1, p_2, p0, p2, g_1, g1):
    g_1[...] = slope(y_1[...], p0[...], y_2[...], p_2[...])
    g1[...] = slope(y1[...], p2[...], y0[...], p0[...])


def slope_kernel(y_1, y0, p_1, p1, g0, total_ref):
    grad = slope(y0[...], p1[...], y_1[...], p_1[...])
    g0[...] = grad
    total_ref[...] = squares(grad, PARTS)


def step_size(total_ref):
    part = jnp.sum(total_ref[...], axis=0)
    total = jnp.sum(jnp.sum(part, axis=1, keepdims=True), axis=0, keepdims=True)
    return TAU_STEP / jnp.sqrt(total / (2 * NK * NB * NPW) + EPS_NORM)


def advance_kernel(total_ref, p_1, p0, p1, g_1, g0, g1, q_1, q0, q1, out_ref):
    size = step_size(total_ref)
    q_1[...] = (p_1[...].astype(F32) + size * g_1[...]).astype(BF16)
    here = (p0[...].astype(F32) + size * g0[...]).astype(BF16)
    ahead = (p1[...].astype(F32) + size * g1[...]).astype(BF16)
    q0[...] = here
    q1[...] = ahead
    margin(here, ahead, out_ref)


def finish_kernel(total_ref, p0, g0, re_ref, im_ref):
    size = step_size(total_ref)
    value = (p0[...].astype(F32) + size * g0[...]).astype(BF16)
    re_ref[...] = value[:NB]
    im_ref[...] = value[NB:]


def shifted(value, by):
    return lax.ppermute(value, "kstr", [(i, (i + by) % NK) for i in range(NK)])


def exchange(value, axis):
    return lax.all_to_all(value, axis, 0, 0, tiled=True)


def whole_margin(part):
    rows = 2 * NB // PARTS
    parts = exchange(part, "pw").reshape(PARTS, rows, NB)
    own = call(collect_kernel, shape((PARTS, rows, NB), BF16), parts)
    return exchange(own.reshape(2 * NB, NB), "pw")


def whole_total(part):
    parts = exchange(part, "pw")
    own = call(spread_kernel, shape((NK, 8, 128), F32), parts)
    return exchange(own, "kstr")


def inverse(whole):
    return call(newton_kernel, shape((NB, 2 * NB), BF16), whole)


def body(states_re, states_im, gmap):
    width = states_re.shape[2]
    row = lax.axis_index("kstr")
    offset = jnp.mod(gmap[0] - lax.axis_index("pw") * width, NPW)
    blocks = offset // width
    rest = offset - blocks * width
    full = 2 * NB
    duals = shape((NB, full), BF16)
    fields = shape((full, width), BF16)
    grads = shape((full, width), F32)
    margins = shape((full, NB), BF16)
    totals = shape((PARTS, 8, 128), F32)

    first = row < NK // 2
    send_turn = jnp.where(first, jnp.mod(width - rest, width), 0).astype(jnp.int32)
    back_turn = jnp.where(first, rest, 0).astype(jnp.int32)
    is_last = (row == NK - 1).astype(jnp.int32)
    state, send = call(
        prepare_kernel, (fields, fields), send_turn.reshape(1), states_re[0], states_im[0], smem=1
    )
    p1 = shifted(state, -1)
    closing = close_string(send, blocks, rest)
    part, p1 = call(margin_kernel, (margins, fields), is_last.reshape(1), state, p1, closing, smem=1)
    state, closing, part = lax.optimization_barrier((state, closing, part))
    closing = call(turn_kernel, fields, back_turn.reshape(1), closing, smem=1)
    swap = [(0, 1), (1, 0), (NK - 1, NK - 2), (NK - 2, NK - 1)]
    other = lax.ppermute(closing, "kstr", swap)
    p_1 = jnp.where(row == 0, closing, shifted(state, 1))
    p2 = jnp.where(row >= NK - 2, other, shifted(state, -2))
    p_2 = jnp.where(row <= 1, other, shifted(state, 2))

    y0 = inverse(whole_margin(part))
    y_1 = shifted(y0, 1)
    g0, total = call(slope_kernel, (grads, totals), y_1, y0, p_1, p1)
    y0_later, total = lax.optimization_barrier((y0, total))
    y1 = shifted(y0_later, -1)
    y_2 = shifted(y0_later, 2)
    total = whole_total(total)
    g_1, g1 = call(sides_kernel, (grads, grads), y_2, y_1, y0, y1, p_2, state, p2)
    q_1, q0, q1, part = call(
        advance_kernel,
        (fields, fields, fields, margins),
        *(total, p_1, state, p1, g_1, g0, g1),
    )

    y0 = inverse(whole_margin(part))
    y_1 = shifted(y0, 1)
    g0, total = call(slope_kernel, (grads, totals), y_1, y0, q_1, q1)
    total = whole_total(total)
    half = shape((NB, width), BF16)
    new_re, new_im = call(finish_kernel, (half, half), total, q0, g0)
    return new_re[None], new_im[None]


def solution(mesh):
    placed = (P("kstr", None, "pw"), P("kstr", None, "pw"), P("pw"))
    return jax.shard_map(
        body,
        mesh=mesh,
        in_specs=placed,
        out_specs=(P("kstr", None, "pw"), P("kstr", None, "pw")),
        check_vma=False,
    )
```

```python
import jax
import jax.numpy as jnp
from jax import lax
from jax.experimental import pallas as pl
from jax.experimental.pallas import tpu as pltpu
from jax.sharding import PartitionSpec as P

NEWTON = 4
NK = 16
NPW = 16384
NB = 256
PARTS = 32
EPS_SCALE = 1e-06
EPS_NORM = 1e-06
TAU_STEP = 0.25
F32 = jnp.float32
BF16 = jnp.bfloat16


def call(kernel, outs, *args, smem=0, flops=0):
    specs = [pl.BlockSpec(memory_space=pltpu.SMEM)] * smem
    specs += [pl.BlockSpec(memory_space=pltpu.VMEM)] * (len(args) - smem)
    single = not isinstance(outs, (tuple, list))
    outs = (outs,) if single else tuple(outs)
    moved = sum(a.size * a.dtype.itemsize for a in args) + sum(
        o.size * o.dtype.itemsize for o in outs
    )
    result = pl.pallas_call(
        kernel,
        out_shape=outs,
        in_specs=specs,
        out_specs=tuple(pl.BlockSpec(memory_space=pltpu.VMEM) for _ in outs),
        compiler_params=pltpu.CompilerParams(vmem_limit_bytes=14 * 1024 * 1024),
        cost_estimate=pl.CostEstimate(flops=flops, bytes_accessed=moved, transcendentals=0),
    )(*args)
    return result[0] if single else result


def shape(dims, dtype):
    return jax.ShapeDtypeStruct(dims, dtype)


def dot(left, right):
    return jnp.dot(left, right, preferred_element_type=F32)


def margin(left, right, out_ref):
    every = lax.dot_general(left, right, (((1,), (1,)), ((), ())), preferred_element_type=F32)
    out_ref[:NB, :] = (every[:NB, :NB] + every[NB:, NB:]).astype(out_ref.dtype)
    out_ref[NB:, :] = (every[:NB, NB:] - every[NB:, :NB]).astype(out_ref.dtype)


def margin_kernel(state_ref, next_ref, out_ref):
    margin(state_ref[...], next_ref[...], out_ref)


def rotate_kernel(amount_ref, block_ref, out_ref, rolled_ref):
    count, rows, width = block_ref.shape
    amount = amount_ref[0]
    first = amount // width
    rest = amount - first * width
    turn = lax.rem(width - rest, width)

    def roll(index, carry):
        rolled_ref[index] = pltpu.roll(block_ref[index].astype(F32), turn, 1)
        return carry

    lax.fori_loop(0, count, roll, 0, unroll=4)
    lane = lax.broadcasted_iota(jnp.int32, (rows, width), 1)

    def place(index, carry):
        here = lax.rem(index + first, count)
        after = lax.rem(index + first + 1, count)
        value = jnp.where(lane < width - rest, rolled_ref[here], rolled_ref[after])
        out_ref[index] = value.astype(BF16)
        return carry

    lax.fori_loop(0, count, place, 0, unroll=4)


def rotate(amount, block):
    return pl.pallas_call(
        rotate_kernel,
        out_shape=shape(block.shape, BF16),
        in_specs=[
            pl.BlockSpec(memory_space=pltpu.SMEM),
            pl.BlockSpec(memory_space=pltpu.VMEM),
        ],
        out_specs=pl.BlockSpec(memory_space=pltpu.VMEM),
        scratch_shapes=[pltpu.VMEM(block.shape, F32)],
        compiler_params=pltpu.CompilerParams(vmem_limit_bytes=14 * 1024 * 1024),
    )(amount, block)


def collect_kernel(parts_ref, out_ref):
    total = jnp.sum(parts_ref[...].astype(F32), axis=0) * (1.0 / NPW)
    out_ref[...] = jnp.broadcast_to(total.astype(out_ref.dtype)[None], out_ref.shape)


def spread_kernel(parts_ref, out_ref):
    total = jnp.sum(parts_ref[...], axis=0)
    out_ref[...] = jnp.broadcast_to(total[None], out_ref.shape)


def pieces(value, count):
    high = value.astype(BF16)
    if count == 1:
        return [high]
    return [high, (value - high.astype(F32)).astype(BF16)]


def newton_kernel(margin_ref, out_ref):
    stacked = margin_ref[...]
    whole = stacked.astype(F32)
    real, imag = whole[:NB], whole[NB:]
    magnitude = jnp.sqrt(real * real + imag * imag)
    colmax = jnp.max(jnp.sum(magnitude, axis=0, keepdims=True), axis=1, keepdims=True)
    rowmax = jnp.max(jnp.sum(magnitude, axis=1, keepdims=True), axis=0, keepdims=True)
    factor = 1.0 / (colmax * rowmax + EPS_SCALE)
    iterate = jnp.concatenate([real * factor, imag * factor], 1)

    for turn in range(NEWTON):
        parts = pieces(iterate, 2)
        product = None
        for part in parts:
            crossed = jnp.concatenate([part[:, NB:], -part[:, :NB]], 1)
            right = jnp.concatenate([part, crossed], 0)
            term = lax.dot_general(
                stacked, right, (((0,), (0,)), ((), ())), preferred_element_type=F32
            )
            product = term if product is None else product + term
        seconds = pieces(product, 2)
        change = None
        for j, second in enumerate(seconds):
            crossed = jnp.concatenate([-second[:, NB:], second[:, :NB]], 1)
            right = jnp.concatenate([second, crossed], 0)
            for i, part in enumerate(parts):
                if i + j < 2:
                    term = dot(part, right)
                    change = term if change is None else change + term
        iterate = 2.0 * iterate - change
    out_ref[...] = iterate.astype(BF16)


def slope(dual, following, dual_before, before):
    real, imag = dual[:, :NB], dual[:, NB:]
    forward = jnp.concatenate(
        [jnp.concatenate([-imag, real], 1), jnp.concatenate([-real, -imag], 1)], 0
    )
    real, imag = dual_before[:, :NB], dual_before[:, NB:]
    backward = jnp.concatenate(
        [jnp.concatenate([imag, real], 1), jnp.concatenate([-real, imag], 1)], 0
    )
    return dot(forward, following) - dot(backward, before).astype(BF16).astype(F32)


def squares(grad, count):
    part = grad[0:8]
    part = part * part
    for row in range(8, grad.shape[0], 8):
        more = grad[row : row + 8]
        part = part + more * more
    part = part[:, 0:128] + part[:, 128:256] + part[:, 256:384] + part[:, 384:512]
    return jnp.broadcast_to(part[None], (count, 8, 128))


def sides_kernel(y_2, y_1, y0, y1, p_2, p0, p2, g_1, g1):
    g_1[...] = slope(y_1[...], p0[...], y_2[...], p_2[...])
    g1[...] = slope(y1[...], p2[...], y0[...], p0[...])


def slope_kernel(y_1, y0, p_1, p1, g0, total_ref):
    grad = slope(y0[...], p1[...], y_1[...], p_1[...])
    g0[...] = grad
    total_ref[...] = squares(grad, PARTS)


def step_size(total_ref):
    part = jnp.sum(total_ref[...], axis=0)
    total = jnp.sum(jnp.sum(part, axis=1, keepdims=True), axis=0, keepdims=True)
    return TAU_STEP / jnp.sqrt(total / (2 * NK * NB * NPW) + EPS_NORM)


def advance_kernel(total_ref, p_1, p0, p1, g_1, g0, g1, q_1, q0, q1, out_ref):
    size = step_size(total_ref)
    q_1[...] = (p_1[...].astype(F32) + size * g_1[...]).astype(BF16)
    here = (p0[...].astype(F32) + size * g0[...]).astype(BF16)
    ahead = (p1[...].astype(F32) + size * g1[...]).astype(BF16)
    q0[...] = here
    q1[...] = ahead
    margin(here, ahead, out_ref)


def finish_kernel(total_ref, p0, g0, re_ref, im_ref):
    size = step_size(total_ref)
    value = (p0[...].astype(F32) + size * g0[...]).astype(BF16)
    re_ref[...] = value[:NB]
    im_ref[...] = value[NB:]


def shifted(value, by):
    return lax.ppermute(value, "kstr", [(i, (i + by) % NK) for i in range(NK)])


def exchange(value, axis):
    return lax.all_to_all(value, axis, 0, 0, tiled=True)


def whole_margin(part):
    rows = 2 * NB // PARTS
    parts = exchange(part, "pw").reshape(PARTS, rows, NB)
    own = call(collect_kernel, shape((PARTS, rows, NB), BF16), parts)
    return exchange(own.reshape(2 * NB, NB), "pw")


def whole_total(part):
    parts = exchange(part, "pw")
    own = call(spread_kernel, shape((NK, 8, 128), F32), parts)
    return exchange(own, "kstr")


def inverse(whole):
    return call(newton_kernel, shape((NB, 2 * NB), BF16), whole)


def body(states_re, states_im, gmap):
    width = states_re.shape[2]
    row = lax.axis_index("kstr")
    offset = jnp.mod(gmap[0] - lax.axis_index("pw") * width, NPW)
    amount = jnp.where(row < NK // 2, offset, NPW - offset).astype(jnp.int32)
    state = jnp.concatenate([states_re[0], states_im[0]], 0)
    full = 2 * NB
    duals = shape((NB, full), BF16)
    fields = shape((full, width), BF16)
    grads = shape((full, width), F32)
    margins = shape((full, NB), BF16)
    totals = shape((PARTS, 8, 128), F32)

    blocks = exchange(state, "pw").reshape(PARTS, full // PARTS, width)
    turned = exchange(rotate(amount.reshape(1), blocks).reshape(full, width), "pw")

    p1 = shifted(jnp.where(row == 0, turned, state), -1)
    part = call(margin_kernel, margins, state, p1)
    state, turned, part = lax.optimization_barrier((state, turned, part))
    p_1 = shifted(jnp.where(row == NK - 1, turned, state), 1)
    p2 = shifted(jnp.where(row <= 1, turned, state), -2)
    p_2 = shifted(jnp.where(row >= NK - 2, turned, state), 2)

    y0 = inverse(whole_margin(part))
    y_1 = shifted(y0, 1)
    g0, total = call(slope_kernel, (grads, totals), y_1, y0, p_1, p1)
    y0_later, total = lax.optimization_barrier((y0, total))
    y1 = shifted(y0_later, -1)
    y_2 = shifted(y0_later, 2)
    total = whole_total(total)
    g_1, g1 = call(sides_kernel, (grads, grads), y_2, y_1, y0, y1, p_2, state, p2)
    q_1, q0, q1, part = call(
        advance_kernel,
        (fields, fields, fields, margins),
        *(total, p_1, state, p1, g_1, g0, g1),
    )

    y0 = inverse(whole_margin(part))
    y_1 = shifted(y0, 1)
    g0, total = call(slope_kernel, (grads, totals), y_1, y0, q_1, q1)
    total = whole_total(total)
    half = shape((NB, width), BF16)
    new_re, new_im = call(finish_kernel, (half, half), total, q0, g0)
    return new_re[None], new_im[None]


def solution(mesh):
    placed = (P("kstr", None, "pw"), P("kstr", None, "pw"), P("pw"))
    return jax.shard_map(
        body,
        mesh=mesh,
        in_specs=placed,
        out_specs=(P("kstr", None, "pw"), P("kstr", None, "pw")),
        check_vma=False,
    )
```

```python
import jax
import jax.numpy as jnp
from jax import lax
from jax.experimental import pallas as pl
from jax.experimental.pallas import tpu as pltpu
from jax.sharding import PartitionSpec as P

NEWTON = 4
NK = 16
NPW = 16384
NB = 256
PARTS = 32
EPS_SCALE = 1e-06
EPS_NORM = 1e-06
TAU_STEP = 0.25
F32 = jnp.float32
BF16 = jnp.bfloat16


def call(kernel, outs, *args, smem=0, flops=0, scratch=()):
    specs = [pl.BlockSpec(memory_space=pltpu.SMEM)] * smem
    specs += [pl.BlockSpec(memory_space=pltpu.VMEM)] * (len(args) - smem)
    single = not isinstance(outs, (tuple, list))
    outs = (outs,) if single else tuple(outs)
    moved = sum(a.size * a.dtype.itemsize for a in args) + sum(
        o.size * o.dtype.itemsize for o in outs
    )
    result = pl.pallas_call(
        kernel,
        out_shape=outs,
        in_specs=specs,
        out_specs=tuple(pl.BlockSpec(memory_space=pltpu.VMEM) for _ in outs),
        scratch_shapes=list(scratch),
        compiler_params=pltpu.CompilerParams(vmem_limit_bytes=14 * 1024 * 1024),
        cost_estimate=pl.CostEstimate(flops=flops, bytes_accessed=moved, transcendentals=0),
    )(*args)
    return result[0] if single else result


def shape(dims, dtype):
    return jax.ShapeDtypeStruct(dims, dtype)


def dot(left, right):
    return jnp.dot(left, right, preferred_element_type=F32)


def margin(left, right, out_ref):
    every = lax.dot_general(left, right, (((1,), (1,)), ((), ())), preferred_element_type=F32)
    out_ref[:NB, :] = (every[:NB, :NB] + every[NB:, NB:]).astype(out_ref.dtype)
    out_ref[NB:, :] = (every[:NB, NB:] - every[NB:, :NB]).astype(out_ref.dtype)


def choose(flag, yes_ref, no_ref, out_ref):
    @pl.when(flag == 1)
    def _():
        out_ref[...] = yes_ref[...]

    @pl.when(flag != 1)
    def _():
        out_ref[...] = no_ref[...]


def margin_kernel(flags, state_ref, next_ref, closing_ref, out_ref, chosen_ref):
    choose(flags[3], closing_ref, next_ref, chosen_ref)
    margin(state_ref[...], chosen_ref[...], out_ref)


def rotate_kernel(amount_ref, block_ref, out_ref, rolled_ref):
    count, rows, width = block_ref.shape
    amount = amount_ref[0]
    first = amount // width
    rest = amount - first * width
    turn = lax.rem(width - rest, width)

    def roll(index, carry):
        rolled_ref[index] = pltpu.roll(block_ref[index].astype(F32), turn, 1)
        return carry

    lax.fori_loop(0, count, roll, 0, unroll=4)
    lane = lax.broadcasted_iota(jnp.int32, (rows, width), 1)

    def place(index, carry):
        here = lax.rem(index + first, count)
        after = lax.rem(index + first + 1, count)
        value = jnp.where(lane < width - rest, rolled_ref[here], rolled_ref[after])
        out_ref[index] = value.astype(BF16)
        return carry

    lax.fori_loop(0, count, place, 0, unroll=4)


def rotate(amount, block):
    return pl.pallas_call(
        rotate_kernel,
        out_shape=shape(block.shape, BF16),
        in_specs=[
            pl.BlockSpec(memory_space=pltpu.SMEM),
            pl.BlockSpec(memory_space=pltpu.VMEM),
        ],
        out_specs=pl.BlockSpec(memory_space=pltpu.VMEM),
        scratch_shapes=[pltpu.VMEM(block.shape, F32)],
        compiler_params=pltpu.CompilerParams(vmem_limit_bytes=14 * 1024 * 1024),
    )(amount, block)


def collect_kernel(parts_ref, out_ref):
    total = jnp.sum(parts_ref[...].astype(F32), axis=0) * (1.0 / NPW)
    out_ref[...] = jnp.broadcast_to(total.astype(out_ref.dtype)[None], out_ref.shape)


def spread_kernel(parts_ref, out_ref):
    total = jnp.sum(parts_ref[...], axis=0)
    out_ref[...] = jnp.broadcast_to(total[None], out_ref.shape)


def pieces(value, count):
    high = value.astype(BF16)
    if count == 1:
        return [high]
    return [high, (value - high.astype(F32)).astype(BF16)]


def newton_kernel(margin_ref, out_ref):
    stacked = margin_ref[...]
    whole = stacked.astype(F32)
    real, imag = whole[:NB], whole[NB:]
    magnitude = jnp.sqrt(real * real + imag * imag)
    colmax = jnp.max(jnp.sum(magnitude, axis=0, keepdims=True), axis=1, keepdims=True)
    rowmax = jnp.max(jnp.sum(magnitude, axis=1, keepdims=True), axis=0, keepdims=True)
    factor = 1.0 / (colmax * rowmax + EPS_SCALE)
    iterate = jnp.concatenate([real * factor, imag * factor], 1)

    for turn in range(NEWTON):
        parts = pieces(iterate, 2)
        product = None
        for part in parts:
            crossed = jnp.concatenate([part[:, NB:], -part[:, :NB]], 1)
            right = jnp.concatenate([part, crossed], 0)
            term = lax.dot_general(
                stacked, right, (((0,), (0,)), ((), ())), preferred_element_type=F32
            )
            product = term if product is None else product + term
        seconds = pieces(product, 2)
        change = None
        for j, second in enumerate(seconds):
            crossed = jnp.concatenate([-second[:, NB:], second[:, :NB]], 1)
            right = jnp.concatenate([second, crossed], 0)
            for i, part in enumerate(parts):
                if i + j < 2:
                    term = dot(part, right)
                    change = term if change is None else change + term
        iterate = 2.0 * iterate - change
    out_ref[...] = iterate.astype(BF16)


def slope(dual, following, dual_before, before):
    real, imag = dual[:, :NB], dual[:, NB:]
    forward = jnp.concatenate(
        [jnp.concatenate([-imag, real], 1), jnp.concatenate([-real, -imag], 1)], 0
    )
    real, imag = dual_before[:, :NB], dual_before[:, NB:]
    backward = jnp.concatenate(
        [jnp.concatenate([imag, real], 1), jnp.concatenate([-real, imag], 1)], 0
    )
    return dot(forward, following) - dot(backward, before).astype(BF16).astype(F32)


def squares(grad, count):
    part = grad[0:8]
    part = part * part
    for row in range(8, grad.shape[0], 8):
        more = grad[row : row + 8]
        part = part + more * more
    part = part[:, 0:128] + part[:, 128:256] + part[:, 256:384] + part[:, 384:512]
    return jnp.broadcast_to(part[None], (count, 8, 128))


def first_slope_kernel(flags, y_1, y0, p_1, closing, p1, g0, total_ref, chosen_ref):
    choose(flags[0], closing, p_1, chosen_ref)
    slope_kernel(y_1, y0, chosen_ref, p1, g0, total_ref)


def slope_kernel(y_1, y0, p_1, p1, g0, total_ref):
    grad = slope(y0[...], p1[...], y_1[...], p_1[...])
    g0[...] = grad
    total_ref[...] = squares(grad, PARTS)


def step_size(total_ref):
    part = jnp.sum(total_ref[...], axis=0)
    total = jnp.sum(jnp.sum(part, axis=1, keepdims=True), axis=0, keepdims=True)
    return TAU_STEP / jnp.sqrt(total / (2 * NK * NB * NPW) + EPS_NORM)


def advance_kernel(
    flags, total, y_2, y_1, y0, y1, p_2, p_1, p0, p1, p2, closing, g0, q_1, q0, q1, part, far
):
    size = step_size(total)
    here = (p0[...].astype(F32) + size * g0[...]).astype(BF16)
    q0[...] = here
    choose(flags[2], closing, p2, far)
    grad = slope(y1[...], far[...], y0[...], p0[...])
    ahead = (p1[...].astype(F32) + size * grad).astype(BF16)
    q1[...] = ahead
    margin(here, ahead, part)
    choose(flags[1], closing, p_2, far)
    grad = slope(y_1[...], p0[...], y_2[...], far[...])
    q_1[...] = (p_1[...].astype(F32) + size * grad).astype(BF16)


def finish_kernel(total_ref, p0, g0, re_ref, im_ref):
    size = step_size(total_ref)
    value = (p0[...].astype(F32) + size * g0[...]).astype(BF16)
    re_ref[...] = value[:NB]
    im_ref[...] = value[NB:]


def shifted(value, by):
    return lax.ppermute(value, "kstr", [(i, (i + by) % NK) for i in range(NK)])


def exchange(value, axis):
    return lax.all_to_all(value, axis, 0, 0, tiled=True)


def whole_margin(part):
    rows = 2 * NB // PARTS
    parts = exchange(part, "pw").reshape(PARTS, rows, NB)
    own = call(collect_kernel, shape((PARTS, rows, NB), BF16), parts)
    return exchange(own.reshape(2 * NB, NB), "pw")


def whole_total(part):
    parts = exchange(part, "pw")
    own = call(spread_kernel, shape((NK, 8, 128), F32), parts)
    return exchange(own, "kstr")


def inverse(whole):
    return call(newton_kernel, shape((NB, 2 * NB), BF16), whole)


def body(states_re, states_im, gmap):
    width = states_re.shape[2]
    row = lax.axis_index("kstr")
    offset = jnp.mod(gmap[0] - lax.axis_index("pw") * width, NPW)
    amount = jnp.where(row < NK // 2, offset, NPW - offset).astype(jnp.int32)
    state = jnp.concatenate([states_re[0], states_im[0]], 0)
    full = 2 * NB
    duals = shape((NB, full), BF16)
    fields = shape((full, width), BF16)
    grads = shape((full, width), F32)
    margins = shape((full, NB), BF16)
    totals = shape((PARTS, 8, 128), F32)

    flags = jnp.stack([row == 0, row <= 1, row >= NK - 2, row == NK - 1]).astype(jnp.int32)

    blocks = exchange(state, "pw").reshape(PARTS, full // PARTS, width)
    p2, p_2 = shifted(state, -2), shifted(state, 2)
    blocks, p2, p_2, state = lax.optimization_barrier((blocks, p2, p_2, state))
    turned = rotate(amount.reshape(1), blocks).reshape(full, width)
    turned, state = lax.optimization_barrier((turned, state))
    turned = exchange(turned, "pw")
    p1, p_1 = shifted(state, -1), shifted(state, 1)
    turned, p1, p_1 = lax.optimization_barrier((turned, p1, p_1))

    end = NK - 1
    near = lax.ppermute(turned, "kstr", [(0, end), (end, 0)])
    part, p1 = call(margin_kernel, (margins, fields), flags, state, p1, near, smem=1)
    turned, part = lax.optimization_barrier((turned, part))
    far = lax.ppermute(turned, "kstr", [(0, end - 1), (1, end), (end - 1, 0), (end, 1)])
    whole, far = lax.optimization_barrier((whole_margin(part), far))

    y0 = inverse(whole)
    y_1 = shifted(y0, 1)
    g0, total, p_1 = call(
        first_slope_kernel, (grads, totals, fields), flags, y_1, y0, p_1, near, p1, smem=1
    )
    y0_later, total = lax.optimization_barrier((y0, total))
    y1 = shifted(y0_later, -1)
    y_2 = shifted(y0_later, 2)
    total = whole_total(total)
    q_1, q0, q1, part = call(
        advance_kernel,
        (fields, fields, fields, margins),
        *(flags, total, y_2, y_1, y0, y1, p_2, p_1, state, p1, p2, far, g0),
        smem=1,
        scratch=(pltpu.VMEM((full, width), BF16),),
    )

    y0 = inverse(whole_margin(part))
    y_1 = shifted(y0, 1)
    g0, total = call(slope_kernel, (grads, totals), y_1, y0, q_1, q1)
    total = whole_total(total)
    half = shape((NB, width), BF16)
    new_re, new_im = call(finish_kernel, (half, half), total, q0, g0)
    return new_re[None], new_im[None]


def solution(mesh):
    placed = (P("kstr", None, "pw"), P("kstr", None, "pw"), P("pw"))
    return jax.shard_map(
        body,
        mesh=mesh,
        in_specs=placed,
        out_specs=(P("kstr", None, "pw"), P("kstr", None, "pw")),
        check_vma=False,
    )
```

```python
import jax
import jax.numpy as jnp
from jax import lax
from jax.experimental import pallas as pl
from jax.experimental.pallas import tpu as pltpu
from jax.sharding import PartitionSpec as P

NEWTON = 4
NK = 16
NPW = 16384
NB = 256
PARTS = 32
CHUNK = 2 * NB // PARTS
EPS_SCALE = 1e-06
EPS_NORM = 1e-06
TAU_STEP = 0.25
F32 = jnp.float32
BF16 = jnp.bfloat16


def call(kernel, outs, *args, smem=0, flops=0, scratch=()):
    specs = [pl.BlockSpec(memory_space=pltpu.SMEM)] * smem
    specs += [pl.BlockSpec(memory_space=pltpu.VMEM)] * (len(args) - smem)
    single = not isinstance(outs, (tuple, list))
    outs = (outs,) if single else tuple(outs)
    moved = sum(a.size * a.dtype.itemsize for a in args) + sum(
        o.size * o.dtype.itemsize for o in outs
    )
    result = pl.pallas_call(
        kernel,
        out_shape=outs,
        in_specs=specs,
        out_specs=tuple(pl.BlockSpec(memory_space=pltpu.VMEM) for _ in outs),
        scratch_shapes=list(scratch),
        compiler_params=pltpu.CompilerParams(vmem_limit_bytes=14 * 1024 * 1024),
        cost_estimate=pl.CostEstimate(flops=flops, bytes_accessed=moved, transcendentals=0),
    )(*args)
    return result[0] if single else result


def shape(dims, dtype):
    return jax.ShapeDtypeStruct(dims, dtype)


def dot(left, right):
    return jnp.dot(left, right, preferred_element_type=F32)


def margin(left, right):
    every = lax.dot_general(left, right, (((1,), (1,)), ((), ())), preferred_element_type=F32)
    real = every[:NB, :NB] + every[NB:, NB:]
    return jnp.concatenate([real, every[:NB, NB:] - every[NB:, :NB]], 0)


def choose(flag, yes_ref, no_ref, out_ref):
    @pl.when(flag == 1)
    def _():
        out_ref[...] = yes_ref[...]

    @pl.when(flag != 1)
    def _():
        out_ref[...] = no_ref[...]


def margin_kernel(state_ref, next_ref, out_ref):
    out_ref[...] = margin(state_ref[...], next_ref[...]).astype(BF16)


def rotate_kernel(amount_ref, block_ref, out_ref, rolled_ref):
    count, rows, width = block_ref.shape
    amount = amount_ref[0]
    first = amount // width
    rest = amount - first * width
    turn = lax.rem(width - rest, width)

    def roll(index, carry):
        rolled_ref[index] = pltpu.roll(block_ref[index].astype(F32), turn, 1)
        return carry

    lax.fori_loop(0, count, roll, 0, unroll=4)
    lane = lax.broadcasted_iota(jnp.int32, (rows, width), 1)

    def place(index, carry):
        here = lax.rem(index + first, count)
        after = lax.rem(index + first + 1, count)
        value = jnp.where(lane < width - rest, rolled_ref[here], rolled_ref[after])
        out_ref[index] = value.astype(BF16)
        return carry

    lax.fori_loop(0, count, place, 0, unroll=4)


def rotate(amount, block):
    return pl.pallas_call(
        rotate_kernel,
        out_shape=shape(block.shape, BF16),
        in_specs=[
            pl.BlockSpec(memory_space=pltpu.SMEM),
            pl.BlockSpec(memory_space=pltpu.VMEM),
        ],
        out_specs=pl.BlockSpec(memory_space=pltpu.VMEM),
        scratch_shapes=[pltpu.VMEM(block.shape, F32)],
        compiler_params=pltpu.CompilerParams(vmem_limit_bytes=14 * 1024 * 1024),
    )(amount, block)


def collect_kernel(parts_ref, out_ref, kept_ref):
    total = jnp.sum(parts_ref[...].astype(F32), axis=0) * (1.0 / NPW)
    kept_ref[...] = total
    out_ref[...] = jnp.broadcast_to(total.astype(BF16)[None], out_ref.shape)


def collect_orders_kernel(parts_ref, first_ref, second_ref, squares_ref):
    total = jnp.sum(parts_ref[...].astype(F32), axis=0)
    for half in range(2):
        lanes = pl.ds(128 * half, 128)
        first_ref[:, lanes] = total[CHUNK * half : CHUNK * (half + 1)] * (1.0 / NPW)
        second_ref[:, lanes] = total[CHUNK * (2 + half) : CHUNK * (3 + half)] * (1.0 / NPW)
    part = total[4 * CHUNK : 4 * CHUNK + 8] + total[4 * CHUNK + 8 :]
    squares_ref[...] = jnp.broadcast_to(part[None], squares_ref.shape)


def combine_kernel(total_ref, kept_ref, first_ref, second_ref, out_ref):
    size = step_size(total_ref)
    value = kept_ref[...] + size * (first_ref[...] + size * second_ref[...])
    out_ref[...] = jnp.broadcast_to(value.astype(BF16)[None], out_ref.shape)


def spread_kernel(parts_ref, out_ref):
    total = jnp.sum(parts_ref[...], axis=0)
    out_ref[...] = jnp.broadcast_to(total[None], out_ref.shape)


def pieces(value, count):
    high = value.astype(BF16)
    if count == 1:
        return [high]
    return [high, (value - high.astype(F32)).astype(BF16)]


def newton_kernel(margin_ref, out_ref):
    stacked = margin_ref[...]
    whole = stacked.astype(F32)
    real, imag = whole[:NB], whole[NB:]
    magnitude = jnp.sqrt(real * real + imag * imag)
    colmax = jnp.max(jnp.sum(magnitude, axis=0, keepdims=True), axis=1, keepdims=True)
    rowmax = jnp.max(jnp.sum(magnitude, axis=1, keepdims=True), axis=0, keepdims=True)
    factor = 1.0 / (colmax * rowmax + EPS_SCALE)
    iterate = jnp.concatenate([real * factor, imag * factor], 1)

    for turn in range(NEWTON):
        terms = 1 if turn < NEWTON // 2 else 2
        parts = pieces(iterate, terms)
        product = None
        for part in parts:
            crossed = jnp.concatenate([part[:, NB:], -part[:, :NB]], 1)
            right = jnp.concatenate([part, crossed], 0)
            term = lax.dot_general(
                stacked, right, (((0,), (0,)), ((), ())), preferred_element_type=F32
            )
            product = term if product is None else product + term
        seconds = pieces(product, terms)
        change = None
        for j, second in enumerate(seconds):
            crossed = jnp.concatenate([-second[:, NB:], second[:, :NB]], 1)
            right = jnp.concatenate([second, crossed], 0)
            for i, part in enumerate(parts):
                if i + j < terms:
                    term = dot(part, right)
                    change = term if change is None else change + term
        iterate = 2.0 * iterate - change
    out_ref[...] = iterate.astype(BF16)


def slope(dual, following, dual_before, before):
    real, imag = dual[:, :NB], dual[:, NB:]
    forward = jnp.concatenate(
        [jnp.concatenate([-imag, real], 1), jnp.concatenate([-real, -imag], 1)], 0
    )
    real, imag = dual_before[:, :NB], dual_before[:, NB:]
    backward = jnp.concatenate(
        [jnp.concatenate([imag, real], 1), jnp.concatenate([-real, imag], 1)], 0
    )
    return dot(forward, following) - dot(backward, before).astype(BF16).astype(F32)


def squares(grad):
    part = grad[0:8]
    part = part * part
    for row in range(8, grad.shape[0], 8):
        more = grad[row : row + 8]
        part = part + more * more
    return part[:, 0:128] + part[:, 128:256] + part[:, 256:384] + part[:, 384:512]


def orders_kernel(flags, y_1, y0, y1, p_1, p0, p1, p2, closing, g0, g1, out_ref, far):
    grad = slope(y0[...], p1[...], y_1[...], p_1[...])
    g0[...] = grad
    part = squares(grad)
    high = part.astype(BF16).astype(F32)
    pair = jnp.concatenate([high, part - high], 0).astype(BF16)
    here = grad.astype(BF16)
    choose(flags[2], closing, p2, far)
    ahead = slope(y1[...], far[...], y0[...], p0[...]).astype(BF16)
    g1[...] = ahead
    first = (margin(here, p1[...]) + margin(p0[...], ahead)).astype(BF16)
    second = margin(here, ahead).astype(BF16)
    for part in range(PARTS):
        rows = slice(CHUNK * part, CHUNK * (part + 1))
        for index, value in enumerate((first, second)):
            for half in range(2):
                at = pl.ds(CHUNK * (2 * index + half), CHUNK)
                out_ref[part, at, :] = value[rows, 128 * half : 128 * (half + 1)]
        out_ref[part, pl.ds(4 * CHUNK, CHUNK), :] = pair


def slope_kernel(y_1, y0, p_1, p1, g0, total_ref):
    grad = slope(y0[...], p1[...], y_1[...], p_1[...])
    g0[...] = grad
    total_ref[...] = jnp.broadcast_to(squares(grad)[None], total_ref.shape)


def step_size(total_ref):
    part = jnp.sum(total_ref[...], axis=0)
    total = jnp.sum(jnp.sum(part, axis=1, keepdims=True), axis=0, keepdims=True)
    return TAU_STEP / jnp.sqrt(total / (2 * NK * NB * NPW) + EPS_NORM)


def advance_kernel(flags, total, y_2, y_1, p_2, p_1, p0, p1, closing, g0, g1, q_1, q0, q1, far):
    size = step_size(total)
    q0[...] = (p0[...].astype(F32) + size * g0[...]).astype(BF16)
    q1[...] = (p1[...].astype(F32) + size * g1[...].astype(F32)).astype(BF16)
    choose(flags[1], closing, p_2, far)
    grad = slope(y_1[...], p0[...], y_2[...], far[...])
    q_1[...] = (p_1[...].astype(F32) + size * grad).astype(BF16)


def finish_kernel(total_ref, p0, g0, re_ref, im_ref):
    size = step_size(total_ref)
    value = (p0[...].astype(F32) + size * g0[...]).astype(BF16)
    re_ref[...] = value[:NB]
    im_ref[...] = value[NB:]


def shifted(value, by):
    return lax.ppermute(value, "kstr", [(i, (i + by) % NK) for i in range(NK)])


def exchange(value, axis):
    return lax.all_to_all(value, axis, 0, 0, tiled=True)


def whole_total(part):
    parts = exchange(part, "pw")
    own = call(spread_kernel, shape((NK, 8, 128), F32), parts)
    return exchange(own, "kstr")


def inverse(whole):
    return call(newton_kernel, shape((NB, 2 * NB), BF16), whole)


def body(states_re, states_im, gmap):
    width = states_re.shape[2]
    row = lax.axis_index("kstr")
    offset = jnp.mod(gmap[0] - lax.axis_index("pw") * width, NPW)
    amount = jnp.where(row < NK // 2, offset, NPW - offset).astype(jnp.int32)
    state = jnp.concatenate([states_re[0], states_im[0]], 0)
    full = 2 * NB
    end = NK - 1
    duals = shape((NB, full), BF16)
    fields = shape((full, width), BF16)
    grads = shape((full, width), F32)
    chunk = shape((CHUNK, NB), F32)
    chunks = shape((PARTS, CHUNK, NB), BF16)
    far_scratch = (pltpu.VMEM((full, width), BF16),)
    flags = jnp.stack([row == 0, row <= 1, row >= NK - 2, row == end]).astype(jnp.int32)

    blocks = exchange(state, "pw").reshape(PARTS, CHUNK, width)
    p2, p_2 = shifted(state, -2), shifted(state, 2)
    blocks, p2, p_2, state = lax.optimization_barrier((blocks, p2, p_2, state))
    turned = exchange(rotate(amount.reshape(1), blocks).reshape(full, width), "pw")
    p1 = shifted(jnp.where(row == 0, turned, state), -1)

    part = call(margin_kernel, shape((full, NB), BF16), state, p1)
    state, turned, part = lax.optimization_barrier((state, turned, part))
    parts = exchange(part, "pw").reshape(PARTS, CHUNK, NB)
    p_1 = shifted(jnp.where(row == end, turned, state), 1)
    parts, p_1, turned = lax.optimization_barrier((parts, p_1, turned))
    own, kept = call(collect_kernel, (chunks, chunk), parts)
    whole = exchange(own.reshape(full, NB), "pw")
    far = lax.ppermute(turned, "kstr", [(0, end - 1), (1, end), (end - 1, 0), (end, 1)])
    whole, far = lax.optimization_barrier((whole, far))

    y0 = inverse(whole)
    y_1 = shifted(y0, 1)
    y1 = shifted(y0, -1)
    g0, g1, part = call(
        orders_kernel,
        (grads, fields, shape((PARTS, 5 * CHUNK, 128), BF16)),
        *(flags, y_1, y0, y1, p_1, state, p1, p2, far),
        smem=1,
        scratch=far_scratch,
    )
    y0, part = lax.optimization_barrier((y0, part))
    y_2 = shifted(y0, 2)
    parts = exchange(part, "pw")
    first, second, total = call(
        collect_orders_kernel, (chunk, chunk, shape((NK, 8, 128), F32)), parts
    )
    total = exchange(total, "kstr")
    own = call(combine_kernel, chunks, total, kept, first, second)
    whole = exchange(own.reshape(full, NB), "pw")
    q_1, q0, q1 = call(
        advance_kernel,
        (fields, fields, fields),
        *(flags, total, y_2, y_1, p_2, p_1, state, p1, far, g0, g1),
        smem=1,
        scratch=far_scratch,
    )

    y0 = inverse(whole)
    y_1 = shifted(y0, 1)
    g0, total = call(slope_kernel, (grads, shape((PARTS, 8, 128), F32)), y_1, y0, q_1, q1)
    total = whole_total(total)
    half = shape((NB, width), BF16)
    new_re, new_im = call(finish_kernel, (half, half), total, q0, g0)
    return new_re[None], new_im[None]


def solution(mesh):
    placed = (P("kstr", None, "pw"), P("kstr", None, "pw"), P("pw"))
    return jax.shard_map(
        body,
        mesh=mesh,
        in_specs=placed,
        out_specs=(P("kstr", None, "pw"), P("kstr", None, "pw")),
        check_vma=False,
    )
```

```python
import jax
import jax.numpy as jnp
from jax import lax
from jax.experimental import pallas as pl
from jax.experimental.pallas import tpu as pltpu
from jax.sharding import PartitionSpec as P

NEWTON = 4
NK = 16
NPW = 16384
NB = 256
PARTS = 32
CHUNK = 2 * NB // PARTS
EPS_SCALE = 1e-06
EPS_NORM = 1e-06
TAU_STEP = 0.25
F32 = jnp.float32
BF16 = jnp.bfloat16


def call(kernel, outs, *args, smem=0, flops=0, scratch=()):
    specs = [pl.BlockSpec(memory_space=pltpu.SMEM)] * smem
    specs += [pl.BlockSpec(memory_space=pltpu.VMEM)] * (len(args) - smem)
    single = not isinstance(outs, (tuple, list))
    outs = (outs,) if single else tuple(outs)
    moved = sum(a.size * a.dtype.itemsize for a in args) + sum(
        o.size * o.dtype.itemsize for o in outs
    )
    result = pl.pallas_call(
        kernel,
        out_shape=outs,
        in_specs=specs,
        out_specs=tuple(pl.BlockSpec(memory_space=pltpu.VMEM) for _ in outs),
        scratch_shapes=list(scratch),
        compiler_params=pltpu.CompilerParams(vmem_limit_bytes=14 * 1024 * 1024),
        cost_estimate=pl.CostEstimate(flops=flops, bytes_accessed=moved, transcendentals=0),
    )(*args)
    return result[0] if single else result


def shape(dims, dtype):
    return jax.ShapeDtypeStruct(dims, dtype)


def dot(left, right):
    return jnp.dot(left, right, preferred_element_type=F32)


def margin(left, right):
    every = lax.dot_general(left, right, (((1,), (1,)), ((), ())), preferred_element_type=F32)
    real = every[:NB, :NB] + every[NB:, NB:]
    return jnp.concatenate([real, every[:NB, NB:] - every[NB:, :NB]], 0)


def choose(flag, yes_ref, no_ref, out_ref):
    @pl.when(flag == 1)
    def _():
        out_ref[...] = yes_ref[...]

    @pl.when(flag != 1)
    def _():
        out_ref[...] = no_ref[...]


def margin_kernel(state_ref, next_ref, out_ref):
    out_ref[...] = margin(state_ref[...], next_ref[...]).astype(BF16)


def first_margin_kernel(flags, state_ref, next_ref, closing_ref, out_ref, chosen_ref):
    choose(flags[3], closing_ref, next_ref, chosen_ref)
    margin_kernel(state_ref, chosen_ref, out_ref)


def merge_kernel(bounds, state_ref, beside_ref, out_ref):
    lane = lax.broadcasted_iota(jnp.int32, (CHUNK, state_ref.shape[1]), 1)
    own = (lane >= bounds[0]) & (lane < bounds[1])
    for row in range(0, state_ref.shape[0], CHUNK):
        rows = pl.ds(row, CHUNK)
        value = jnp.where(own, state_ref[rows, :].astype(F32), beside_ref[rows, :].astype(F32))
        out_ref[rows, :] = pltpu.roll(value, bounds[2], 1).astype(BF16)


def place(row, column):
    return row * PARTS + column % PARTS


def beside_pairs():
    pairs = []
    for j in range(PARTS):
        pairs += [(place(row, j), place(row, j - 1)) for row in (0, 1)]
        pairs += [(place(row, j), place(row, j + 1)) for row in (NK - 2, NK - 1)]
    return pairs


def closing_pairs(by):
    pairs = []
    for j in range(PARTS):
        for row in (0, 1):
            pairs.append((place(row, j), place(NK - 1 - row, j - by)))
            pairs.append((place(NK - 1 - row, j), place(row, j + by)))
    return pairs


def close_string(value, blocks):
    def branch(by):
        return lambda block: lax.ppermute(block, ("kstr", "pw"), closing_pairs(by))

    return lax.switch(blocks, [branch(by) for by in range(PARTS)], value)


def collect_kernel(parts_ref, out_ref, kept_ref):
    total = jnp.sum(parts_ref[...].astype(F32), axis=0) * (1.0 / NPW)
    kept_ref[...] = total
    out_ref[...] = jnp.broadcast_to(total.astype(BF16)[None], out_ref.shape)


def collect_orders_kernel(parts_ref, first_ref, second_ref, squares_ref):
    total = jnp.sum(parts_ref[...].astype(F32), axis=0)
    for half in range(2):
        lanes = pl.ds(128 * half, 128)
        first_ref[:, lanes] = total[CHUNK * half : CHUNK * (half + 1)] * (1.0 / NPW)
        second_ref[:, lanes] = total[CHUNK * (2 + half) : CHUNK * (3 + half)] * (1.0 / NPW)
    part = total[4 * CHUNK : 4 * CHUNK + 8] + total[4 * CHUNK + 8 :]
    squares_ref[...] = jnp.broadcast_to(part[None], squares_ref.shape)


def combine_kernel(total_ref, kept_ref, first_ref, second_ref, out_ref):
    size = step_size(total_ref)
    value = kept_ref[...] + size * (first_ref[...] + size * second_ref[...])
    out_ref[...] = jnp.broadcast_to(value.astype(BF16)[None], out_ref.shape)


def spread_kernel(parts_ref, out_ref):
    total = jnp.sum(parts_ref[...], axis=0)
    out_ref[...] = jnp.broadcast_to(total[None], out_ref.shape)


def pieces(value, count):
    high = value.astype(BF16)
    if count == 1:
        return [high]
    return [high, (value - high.astype(F32)).astype(BF16)]


def newton_kernel(margin_ref, out_ref):
    stacked = margin_ref[...]
    whole = stacked.astype(F32)
    real, imag = whole[:NB], whole[NB:]
    magnitude = jnp.sqrt(real * real + imag * imag)
    colmax = jnp.max(jnp.sum(magnitude, axis=0, keepdims=True), axis=1, keepdims=True)
    rowmax = jnp.max(jnp.sum(magnitude, axis=1, keepdims=True), axis=0, keepdims=True)
    factor = 1.0 / (colmax * rowmax + EPS_SCALE)
    iterate = jnp.concatenate([real * factor, imag * factor], 1)

    for turn in range(NEWTON):
        terms = 1 if turn < NEWTON // 2 else 2
        parts = pieces(iterate, terms)
        product = None
        for part in parts:
            crossed = jnp.concatenate([part[:, NB:], -part[:, :NB]], 1)
            right = jnp.concatenate([part, crossed], 0)
            term = lax.dot_general(
                stacked, right, (((0,), (0,)), ((), ())), preferred_element_type=F32
            )
            product = term if product is None else product + term
        seconds = pieces(product, terms)
        change = None
        for j, second in enumerate(seconds):
            crossed = jnp.concatenate([-second[:, NB:], second[:, :NB]], 1)
            right = jnp.concatenate([second, crossed], 0)
            for i, part in enumerate(parts):
                if i + j < terms:
                    term = dot(part, right)
                    change = term if change is None else change + term
        iterate = 2.0 * iterate - change
    out_ref[...] = iterate.astype(BF16)


def slope(dual, following, dual_before, before):
    real, imag = dual[:, :NB], dual[:, NB:]
    forward = jnp.concatenate(
        [jnp.concatenate([-imag, real], 1), jnp.concatenate([-real, -imag], 1)], 0
    )
    real, imag = dual_before[:, :NB], dual_before[:, NB:]
    backward = jnp.concatenate(
        [jnp.concatenate([imag, real], 1), jnp.concatenate([-real, imag], 1)], 0
    )
    return dot(forward, following) - dot(backward, before).astype(BF16).astype(F32)


def squares(grad):
    part = grad[0:8]
    part = part * part
    for row in range(8, grad.shape[0], 8):
        more = grad[row : row + 8]
        part = part + more * more
    return part[:, 0:128] + part[:, 128:256] + part[:, 256:384] + part[:, 384:512]


def orders_kernel(
    flags, y_1, y0, y1, before, p0, p1, p2, closing, beyond, g0, g1, p_1, out_ref, far
):
    choose(flags[0], closing, before, p_1)
    grad = slope(y0[...], p1[...], y_1[...], p_1[...])
    g0[...] = grad
    part = squares(grad)
    high = part.astype(BF16).astype(F32)
    pair = jnp.concatenate([high, part - high], 0).astype(BF16)
    here = grad.astype(BF16)
    choose(flags[2], beyond, p2, far)
    ahead = slope(y1[...], far[...], y0[...], p0[...]).astype(BF16)
    g1[...] = ahead
    first = (margin(here, p1[...]) + margin(p0[...], ahead)).astype(BF16)
    second = margin(here, ahead).astype(BF16)
    for part in range(PARTS):
        rows = slice(CHUNK * part, CHUNK * (part + 1))
        for index, value in enumerate((first, second)):
            for half in range(2):
                at = pl.ds(CHUNK * (2 * index + half), CHUNK)
                out_ref[part, at, :] = value[rows, 128 * half : 128 * (half + 1)]
        out_ref[part, pl.ds(4 * CHUNK, CHUNK), :] = pair


def slope_kernel(y_1, y0, p_1, p1, g0, total_ref):
    grad = slope(y0[...], p1[...], y_1[...], p_1[...])
    g0[...] = grad
    total_ref[...] = jnp.broadcast_to(squares(grad)[None], total_ref.shape)


def step_size(total_ref):
    part = jnp.sum(total_ref[...], axis=0)
    total = jnp.sum(jnp.sum(part, axis=1, keepdims=True), axis=0, keepdims=True)
    return TAU_STEP / jnp.sqrt(total / (2 * NK * NB * NPW) + EPS_NORM)


def advance_kernel(flags, total, y_2, y_1, p_2, p_1, p0, p1, closing, g0, g1, q_1, q0, q1, far):
    size = step_size(total)
    q0[...] = (p0[...].astype(F32) + size * g0[...]).astype(BF16)
    q1[...] = (p1[...].astype(F32) + size * g1[...].astype(F32)).astype(BF16)
    choose(flags[1], closing, p_2, far)
    grad = slope(y_1[...], p0[...], y_2[...], far[...])
    q_1[...] = (p_1[...].astype(F32) + size * grad).astype(BF16)


def finish_kernel(total_ref, p0, g0, re_ref, im_ref):
    size = step_size(total_ref)
    value = (p0[...].astype(F32) + size * g0[...]).astype(BF16)
    re_ref[...] = value[:NB]
    im_ref[...] = value[NB:]


def shifted(value, by):
    return lax.ppermute(value, "kstr", [(i, (i + by) % NK) for i in range(NK)])


def exchange(value, axis):
    return lax.all_to_all(value, axis, 0, 0, tiled=True)


def whole_total(part):
    parts = exchange(part, "pw")
    own = call(spread_kernel, shape((NK, 8, 128), F32), parts)
    return exchange(own, "kstr")


def inverse(whole):
    return call(newton_kernel, shape((NB, 2 * NB), BF16), whole)


def body(states_re, states_im, gmap):
    width = states_re.shape[2]
    row = lax.axis_index("kstr")
    offset = jnp.mod(gmap[0] - lax.axis_index("pw") * width, NPW)
    blocks = offset // width
    rest = offset - blocks * width
    first = row < NK // 2
    bounds = jnp.stack(
        [
            jnp.where(first, rest, 0),
            jnp.where(first, width, width - rest),
            jnp.where(first, jnp.mod(width - rest, width), rest),
        ]
    ).astype(jnp.int32)
    state = jnp.concatenate([states_re[0], states_im[0]], 0)
    full = 2 * NB
    end = NK - 1
    duals = shape((NB, full), BF16)
    fields = shape((full, width), BF16)
    grads = shape((full, width), F32)
    chunk = shape((CHUNK, NB), F32)
    chunks = shape((PARTS, CHUNK, NB), BF16)
    far_scratch = (pltpu.VMEM((full, width), BF16),)
    flags = jnp.stack([row == 0, row <= 1, row >= NK - 2, row == end]).astype(jnp.int32)

    beside = lax.ppermute(state, ("kstr", "pw"), beside_pairs())
    p1, p_2 = shifted(state, -1), shifted(state, 2)
    merged = call(merge_kernel, fields, bounds, state, beside, smem=1)
    near = close_string(merged, blocks)
    near, p1, p_2 = lax.optimization_barrier((near, p1, p_2))

    part, p1 = call(first_margin_kernel, (shape((full, NB), BF16), fields), flags, state, p1, near, smem=1)
    state, near, part = lax.optimization_barrier((state, near, part))
    parts = exchange(part, "pw").reshape(PARTS, CHUNK, NB)
    p_1 = shifted(state, 1)
    parts, p_1, near, p1 = lax.optimization_barrier((parts, p_1, near, p1))
    p2 = shifted(p1, -1)
    own, kept = call(collect_kernel, (chunks, chunk), parts)
    whole = exchange(own.reshape(full, NB), "pw")
    far = lax.ppermute(near, "kstr", [(0, 1), (1, 0), (end - 1, end), (end, end - 1)])
    whole, far, p2 = lax.optimization_barrier((whole, far, p2))

    y0 = inverse(whole)
    y_1 = shifted(y0, 1)
    y1 = shifted(y0, -1)
    g0, g1, p_1, part = call(
        orders_kernel,
        (grads, fields, fields, shape((PARTS, 5 * CHUNK, 128), BF16)),
        *(flags, y_1, y0, y1, p_1, state, p1, p2, near, far),
        smem=1,
        scratch=far_scratch,
    )
    y0, part = lax.optimization_barrier((y0, part))
    y_2 = shifted(y0, 2)
    parts = exchange(part, "pw")
    first, second, total = call(
        collect_orders_kernel, (chunk, chunk, shape((NK, 8, 128), F32)), parts
    )
    total = exchange(total, "kstr")
    own = call(combine_kernel, chunks, total, kept, first, second)
    whole = exchange(own.reshape(full, NB), "pw")
    q_1, q0, q1 = call(
        advance_kernel,
        (fields, fields, fields),
        *(flags, total, y_2, y_1, p_2, p_1, state, p1, far, g0, g1),
        smem=1,
        scratch=far_scratch,
    )

    y0 = inverse(whole)
    y_1 = shifted(y0, 1)
    g0, total = call(slope_kernel, (grads, shape((PARTS, 8, 128), F32)), y_1, y0, q_1, q1)
    total = whole_total(total)
    half = shape((NB, width), BF16)
    new_re, new_im = call(finish_kernel, (half, half), total, q0, g0)
    return new_re[None], new_im[None]


def solution(mesh):
    placed = (P("kstr", None, "pw"), P("kstr", None, "pw"), P("pw"))
    return jax.shard_map(
        body,
        mesh=mesh,
        in_specs=placed,
        out_specs=(P("kstr", None, "pw"), P("kstr", None, "pw")),
        check_vma=False,
    )
```

```python
import jax
import jax.numpy as jnp
from jax import lax
from jax.experimental import pallas as pl
from jax.experimental.pallas import tpu as pltpu
from jax.sharding import PartitionSpec as P

NEWTON = 4
NK = 16
NPW = 16384
NB = 256
PARTS = 32
CHUNK = 2 * NB // PARTS
EPS_SCALE = 1e-06
EPS_NORM = 1e-06
TAU_STEP = 0.25
F32 = jnp.float32
BF16 = jnp.bfloat16


def call(kernel, outs, *args, smem=0, flops=0, scratch=()):
    specs = [pl.BlockSpec(memory_space=pltpu.SMEM)] * smem
    specs += [pl.BlockSpec(memory_space=pltpu.VMEM)] * (len(args) - smem)
    single = not isinstance(outs, (tuple, list))
    outs = (outs,) if single else tuple(outs)
    moved = sum(a.size * a.dtype.itemsize for a in args) + sum(
        o.size * o.dtype.itemsize for o in outs
    )
    result = pl.pallas_call(
        kernel,
        out_shape=outs,
        in_specs=specs,
        out_specs=tuple(pl.BlockSpec(memory_space=pltpu.VMEM) for _ in outs),
        scratch_shapes=list(scratch),
        compiler_params=pltpu.CompilerParams(vmem_limit_bytes=14 * 1024 * 1024),
        cost_estimate=pl.CostEstimate(flops=flops, bytes_accessed=moved, transcendentals=0),
    )(*args)
    return result[0] if single else result


def shape(dims, dtype):
    return jax.ShapeDtypeStruct(dims, dtype)


def dot(left, right):
    return jnp.dot(left, right, preferred_element_type=F32)


def margin(left, right):
    every = lax.dot_general(left, right, (((1,), (1,)), ((), ())), preferred_element_type=F32)
    real = every[:NB, :NB] + every[NB:, NB:]
    return jnp.concatenate([real, every[:NB, NB:] - every[NB:, :NB]], 0)


def choose(flag, yes_ref, no_ref, out_ref):
    @pl.when(flag == 1)
    def _():
        out_ref[...] = yes_ref[...]

    @pl.when(flag != 1)
    def _():
        out_ref[...] = no_ref[...]


def margin_kernel(state_ref, next_ref, out_ref):
    out_ref[...] = margin(state_ref[...], next_ref[...]).astype(BF16)


def first_margin_kernel(flags, state_ref, next_ref, closing_ref, out_ref, chosen_ref):
    choose(flags[3], closing_ref, next_ref, chosen_ref)
    margin_kernel(state_ref, chosen_ref, out_ref)


def merge_kernel(bounds, state_ref, beside_ref, out_ref):
    lane = lax.broadcasted_iota(jnp.int32, (CHUNK, state_ref.shape[1]), 1)
    own = (lane >= bounds[0]) & (lane < bounds[1])
    for row in range(0, state_ref.shape[0], CHUNK):
        rows = pl.ds(row, CHUNK)
        value = jnp.where(own, state_ref[rows, :].astype(F32), beside_ref[rows, :].astype(F32))
        out_ref[rows, :] = pltpu.roll(value, bounds[2], 1).astype(BF16)


def place(row, column):
    return row * PARTS + column % PARTS


def beside_pairs():
    pairs = []
    for j in range(PARTS):
        pairs += [(place(row, j), place(row, j - 1)) for row in (0, 1)]
        pairs += [(place(row, j), place(row, j + 1)) for row in (NK - 2, NK - 1)]
    return pairs


def closing_pairs(by):
    pairs = []
    for j in range(PARTS):
        for row in (0, 1):
            pairs.append((place(row, j), place(NK - 1 - row, j - by)))
            pairs.append((place(NK - 1 - row, j), place(row, j + by)))
    return pairs


def close_string(value, blocks):
    def branch(by):
        return lambda block: lax.ppermute(block, ("kstr", "pw"), closing_pairs(by))

    return lax.switch(blocks, [branch(by) for by in range(PARTS)], value)


def collect_kernel(parts_ref, out_ref, kept_ref):
    total = jnp.sum(parts_ref[...].astype(F32), axis=0) * (1.0 / NPW)
    kept_ref[...] = total
    out_ref[...] = jnp.broadcast_to(total.astype(BF16)[None], out_ref.shape)


def collect_orders_kernel(parts_ref, first_ref, second_ref, squares_ref):
    total = jnp.sum(parts_ref[...].astype(F32), axis=0)
    for half in range(2):
        lanes = pl.ds(128 * half, 128)
        first_ref[:, lanes] = total[CHUNK * half : CHUNK * (half + 1)] * (1.0 / NPW)
        second_ref[:, lanes] = total[CHUNK * (2 + half) : CHUNK * (3 + half)] * (1.0 / NPW)
    part = total[4 * CHUNK : 4 * CHUNK + 8] + total[4 * CHUNK + 8 :]
    squares_ref[...] = jnp.broadcast_to(part[None], squares_ref.shape)


def combine_kernel(total_ref, kept_ref, first_ref, second_ref, out_ref):
    size = step_size(total_ref)
    value = kept_ref[...] + size * (first_ref[...] + size * second_ref[...])
    out_ref[...] = jnp.broadcast_to(value.astype(BF16)[None], out_ref.shape)


def spread_kernel(parts_ref, out_ref):
    total = jnp.sum(parts_ref[...], axis=0)
    out_ref[...] = jnp.broadcast_to(total[None], out_ref.shape)


def pieces(value, count):
    high = value.astype(BF16)
    if count == 1:
        return [high]
    return [high, (value - high.astype(F32)).astype(BF16)]


def newton_kernel(margin_ref, out_ref):
    stacked = margin_ref[...]
    whole = stacked.astype(F32)
    real, imag = whole[:NB], whole[NB:]
    magnitude = jnp.sqrt(real * real + imag * imag)
    colmax = jnp.max(jnp.sum(magnitude, axis=0, keepdims=True), axis=1, keepdims=True)
    rowmax = jnp.max(jnp.sum(magnitude, axis=1, keepdims=True), axis=0, keepdims=True)
    factor = 1.0 / (colmax * rowmax + EPS_SCALE)
    iterate = jnp.concatenate([real * factor, imag * factor], 1)

    for turn in range(NEWTON):
        terms = 1 if turn < NEWTON // 2 else 2
        parts = pieces(iterate, terms)
        product = None
        for part in parts:
            crossed = jnp.concatenate([part[:, NB:], -part[:, :NB]], 1)
            right = jnp.concatenate([part, crossed], 0)
            term = lax.dot_general(
                stacked, right, (((0,), (0,)), ((), ())), preferred_element_type=F32
            )
            product = term if product is None else product + term
        seconds = pieces(product, terms)
        change = None
        for j, second in enumerate(seconds):
            crossed = jnp.concatenate([-second[:, NB:], second[:, :NB]], 1)
            right = jnp.concatenate([second, crossed], 0)
            for i, part in enumerate(parts):
                if i + j < terms:
                    term = dot(part, right)
                    change = term if change is None else change + term
        iterate = 2.0 * iterate - change
    out_ref[...] = iterate.astype(BF16)


def slope(dual, following, dual_before, before):
    real, imag = dual[:, :NB], dual[:, NB:]
    forward = jnp.concatenate(
        [jnp.concatenate([-imag, real], 1), jnp.concatenate([-real, -imag], 1)], 0
    )
    real, imag = dual_before[:, :NB], dual_before[:, NB:]
    backward = jnp.concatenate(
        [jnp.concatenate([imag, real], 1), jnp.concatenate([-real, imag], 1)], 0
    )
    return dot(forward, following) - dot(backward, before).astype(BF16).astype(F32)


def squares(grad):
    part = grad[0:8]
    part = part * part
    for row in range(8, grad.shape[0], 8):
        more = grad[row : row + 8]
        part = part + more * more
    return part[:, 0:128] + part[:, 128:256] + part[:, 256:384] + part[:, 384:512]


def orders_kernel(
    flags, y_1, y0, y1, before, p0, p1, p2, closing, beyond, g0, g1, p_1, out_ref, far
):
    choose(flags[0], closing, before, p_1)
    grad = slope(y0[...], p1[...], y_1[...], p_1[...])
    g0[...] = grad
    part = squares(grad)
    high = part.astype(BF16).astype(F32)
    pair = jnp.concatenate([high, part - high], 0).astype(BF16)
    here = grad.astype(BF16)
    choose(flags[2], beyond, p2, far)
    ahead = slope(y1[...], far[...], y0[...], p0[...]).astype(BF16)
    g1[...] = ahead
    first = (margin(here, p1[...]) + margin(p0[...], ahead)).astype(BF16)
    second = margin(here, ahead).astype(BF16)
    for part in range(PARTS):
        rows = slice(CHUNK * part, CHUNK * (part + 1))
        for index, value in enumerate((first, second)):
            for half in range(2):
                at = pl.ds(CHUNK * (2 * index + half), CHUNK)
                out_ref[part, at, :] = value[rows, 128 * half : 128 * (half + 1)]
        out_ref[part, pl.ds(4 * CHUNK, CHUNK), :] = pair


def slope_kernel(y_1, y0, p_1, p1, g0, total_ref):
    grad = slope(y0[...], p1[...], y_1[...], p_1[...])
    g0[...] = grad
    total_ref[...] = jnp.broadcast_to(squares(grad)[None], total_ref.shape)


def step_size(total_ref):
    part = jnp.sum(total_ref[...], axis=0)
    total = jnp.sum(jnp.sum(part, axis=1, keepdims=True), axis=0, keepdims=True)
    return TAU_STEP / jnp.sqrt(total / (2 * NK * NB * NPW) + EPS_NORM)


def advance_kernel(flags, total, y_2, y_1, p_2, p_1, p0, p1, closing, g0, g1, q_1, q0, q1, far):
    size = step_size(total)
    q0[...] = (p0[...].astype(F32) + size * g0[...]).astype(BF16)
    q1[...] = (p1[...].astype(F32) + size * g1[...].astype(F32)).astype(BF16)
    choose(flags[1], closing, p_2, far)
    grad = slope(y_1[...], p0[...], y_2[...], far[...])
    q_1[...] = (p_1[...].astype(F32) + size * grad).astype(BF16)


def finish_kernel(total_ref, p0, g0, re_ref, im_ref):
    size = step_size(total_ref)
    value = (p0[...].astype(F32) + size * g0[...]).astype(BF16)
    re_ref[...] = value[:NB]
    im_ref[...] = value[NB:]


def shifted(value, by):
    return lax.ppermute(value, "kstr", [(i, (i + by) % NK) for i in range(NK)])


def exchange(value, axis):
    return lax.all_to_all(value, axis, 0, 0, tiled=True)


def whole_total(part):
    parts = exchange(part, "pw")
    own = call(spread_kernel, shape((NK, 8, 128), F32), parts)
    return exchange(own, "kstr")


def inverse(whole):
    return call(newton_kernel, shape((NB, 2 * NB), BF16), whole)


def body(states_re, states_im, gmap):
    width = states_re.shape[2]
    row = lax.axis_index("kstr")
    offset = jnp.mod(gmap[0] - lax.axis_index("pw") * width, NPW)
    blocks = offset // width
    rest = offset - blocks * width
    first = row < NK // 2
    bounds = jnp.stack(
        [
            jnp.where(first, rest, 0),
            jnp.where(first, width, width - rest),
            jnp.where(first, jnp.mod(width - rest, width), rest),
        ]
    ).astype(jnp.int32)
    state = jnp.concatenate([states_re[0], states_im[0]], 0)
    full = 2 * NB
    end = NK - 1
    duals = shape((NB, full), BF16)
    fields = shape((full, width), BF16)
    grads = shape((full, width), F32)
    chunk = shape((CHUNK, NB), F32)
    chunks = shape((PARTS, CHUNK, NB), BF16)
    far_scratch = (pltpu.VMEM((full, width), BF16),)
    flags = jnp.stack([row == 0, row <= 1, row >= NK - 2, row == end]).astype(jnp.int32)

    beside = lax.ppermute(state, ("kstr", "pw"), beside_pairs())
    p1, p_2 = shifted(state, -1), shifted(state, 2)
    p2 = shifted(state, -2)
    merged = call(merge_kernel, fields, bounds, state, beside, smem=1)
    near = close_string(merged, blocks)
    near, p1, p2, p_2 = lax.optimization_barrier((near, p1, p2, p_2))

    part, p1 = call(first_margin_kernel, (shape((full, NB), BF16), fields), flags, state, p1, near, smem=1)
    state, near, part = lax.optimization_barrier((state, near, part))
    parts = exchange(part, "pw").reshape(PARTS, CHUNK, NB)
    p_1 = shifted(state, 1)
    parts, p_1, near = lax.optimization_barrier((parts, p_1, near))
    own, kept = call(collect_kernel, (chunks, chunk), parts)
    whole = exchange(own.reshape(full, NB), "pw")
    far = lax.ppermute(near, "kstr", [(0, 1), (1, 0), (end - 1, end), (end, end - 1)])
    whole, far = lax.optimization_barrier((whole, far))

    y0 = inverse(whole)
    y_1 = shifted(y0, 1)
    y1 = shifted(y0, -1)
    g0, g1, p_1, part = call(
        orders_kernel,
        (grads, fields, fields, shape((PARTS, 5 * CHUNK, 128), BF16)),
        *(flags, y_1, y0, y1, p_1, state, p1, p2, near, far),
        smem=1,
        scratch=far_scratch,
    )
    y0, part = lax.optimization_barrier((y0, part))
    y_2 = shifted(y0, 2)
    parts = exchange(part, "pw")
    first, second, total = call(
        collect_orders_kernel, (chunk, chunk, shape((NK, 8, 128), F32)), parts
    )
    total = exchange(total, "kstr")
    own = call(combine_kernel, chunks, total, kept, first, second)
    whole = exchange(own.reshape(full, NB), "pw")
    q_1, q0, q1 = call(
        advance_kernel,
        (fields, fields, fields),
        *(flags, total, y_2, y_1, p_2, p_1, state, p1, far, g0, g1),
        smem=1,
        scratch=far_scratch,
    )

    y0 = inverse(whole)
    y_1 = shifted(y0, 1)
    g0, total = call(slope_kernel, (grads, shape((PARTS, 8, 128), F32)), y_1, y0, q_1, q1)
    total = whole_total(total)
    half = shape((NB, width), BF16)
    new_re, new_im = call(finish_kernel, (half, half), total, q0, g0)
    return new_re[None], new_im[None]


def solution(mesh):
    placed = (P("kstr", None, "pw"), P("kstr", None, "pw"), P("pw"))
    return jax.shard_map(
        body,
        mesh=mesh,
        in_specs=placed,
        out_specs=(P("kstr", None, "pw"), P("kstr", None, "pw")),
        check_vma=False,
    )
```

```python
import jax
import jax.numpy as jnp
from jax import lax
from jax.experimental import pallas as pl
from jax.experimental.pallas import tpu as pltpu
from jax.sharding import PartitionSpec as P

NEWTON = 4
NK = 16
NPW = 16384
NB = 256
PARTS = 32
CHUNK = 2 * NB // PARTS
EPS_SCALE = 1e-06
EPS_NORM = 1e-06
TAU_STEP = 0.25
F32 = jnp.float32
BF16 = jnp.bfloat16


def call(kernel, outs, *args, smem=0, flops=0, scratch=()):
    specs = [pl.BlockSpec(memory_space=pltpu.SMEM)] * smem
    specs += [pl.BlockSpec(memory_space=pltpu.VMEM)] * (len(args) - smem)
    single = not isinstance(outs, (tuple, list))
    outs = (outs,) if single else tuple(outs)
    moved = sum(a.size * a.dtype.itemsize for a in args) + sum(
        o.size * o.dtype.itemsize for o in outs
    )
    result = pl.pallas_call(
        kernel,
        out_shape=outs,
        in_specs=specs,
        out_specs=tuple(pl.BlockSpec(memory_space=pltpu.VMEM) for _ in outs),
        scratch_shapes=list(scratch),
        compiler_params=pltpu.CompilerParams(vmem_limit_bytes=14 * 1024 * 1024),
        cost_estimate=pl.CostEstimate(flops=flops, bytes_accessed=moved, transcendentals=0),
    )(*args)
    return result[0] if single else result


def shape(dims, dtype):
    return jax.ShapeDtypeStruct(dims, dtype)


def dot(left, right):
    return jnp.dot(left, right, preferred_element_type=F32)


def margin(left, right):
    every = lax.dot_general(left, right, (((1,), (1,)), ((), ())), preferred_element_type=F32)
    real = every[:NB, :NB] + every[NB:, NB:]
    return jnp.concatenate([real, every[:NB, NB:] - every[NB:, :NB]], 0)


def choose(flag, yes_ref, no_ref, out_ref):
    @pl.when(flag == 1)
    def _():
        out_ref[...] = yes_ref[...]

    @pl.when(flag != 1)
    def _():
        out_ref[...] = no_ref[...]


def margin_kernel(state_ref, next_ref, out_ref):
    out_ref[...] = margin(state_ref[...], next_ref[...]).astype(BF16)


def first_margin_kernel(flags, state_ref, next_ref, closing_ref, out_ref, chosen_ref):
    choose(flags[3], closing_ref, next_ref, chosen_ref)
    margin_kernel(state_ref, chosen_ref, out_ref)


def merge_kernel(bounds, state_ref, beside_ref, out_ref):
    lane = lax.broadcasted_iota(jnp.int32, (CHUNK, state_ref.shape[1]), 1)
    own = (lane >= bounds[0]) & (lane < bounds[1])
    for row in range(0, state_ref.shape[0], CHUNK):
        rows = pl.ds(row, CHUNK)
        value = jnp.where(own, state_ref[rows, :].astype(F32), beside_ref[rows, :].astype(F32))
        out_ref[rows, :] = pltpu.roll(value, bounds[2], 1).astype(BF16)


def place(row, column):
    return row * PARTS + column % PARTS


def beside_pairs():
    pairs = []
    for j in range(PARTS):
        pairs += [(place(row, j), place(row, j - 1)) for row in (0, 1)]
        pairs += [(place(row, j), place(row, j + 1)) for row in (NK - 2, NK - 1)]
    return pairs


def closing_pairs(by):
    pairs = []
    for j in range(PARTS):
        for row in (0, 1):
            pairs.append((place(row, j), place(NK - 1 - row, j - by)))
            pairs.append((place(NK - 1 - row, j), place(row, j + by)))
    return pairs


def close_string(value, blocks):
    def branch(by):
        return lambda block: lax.ppermute(block, ("kstr", "pw"), closing_pairs(by))

    return lax.switch(blocks, [branch(by) for by in range(PARTS)], value)


def collect_kernel(parts_ref, out_ref, kept_ref):
    total = jnp.sum(parts_ref[...].astype(F32), axis=0) * (1.0 / NPW)
    kept_ref[...] = total
    out_ref[...] = jnp.broadcast_to(total.astype(BF16)[None], out_ref.shape)


def collect_orders_kernel(parts_ref, first_ref, second_ref, squares_ref):
    total = jnp.sum(parts_ref[...].astype(F32), axis=0)
    for half in range(2):
        lanes = pl.ds(128 * half, 128)
        first_ref[:, lanes] = total[CHUNK * half : CHUNK * (half + 1)] * (1.0 / NPW)
        second_ref[:, lanes] = total[CHUNK * (2 + half) : CHUNK * (3 + half)] * (1.0 / NPW)
    part = total[4 * CHUNK : 4 * CHUNK + 8] + total[4 * CHUNK + 8 :]
    squares_ref[...] = jnp.broadcast_to(part[None], squares_ref.shape)


def combine_kernel(total_ref, kept_ref, first_ref, second_ref, out_ref):
    size = step_size(total_ref)
    value = kept_ref[...] + size * (first_ref[...] + size * second_ref[...])
    out_ref[...] = jnp.broadcast_to(value.astype(BF16)[None], out_ref.shape)


def spread_kernel(parts_ref, out_ref):
    total = jnp.sum(parts_ref[...], axis=0)
    out_ref[...] = jnp.broadcast_to(total[None], out_ref.shape)


def pieces(value, count):
    high = value.astype(BF16)
    if count == 1:
        return [high]
    return [high, (value - high.astype(F32)).astype(BF16)]


def newton_kernel(margin_ref, out_ref):
    stacked = margin_ref[...]
    whole = stacked.astype(F32)
    real, imag = whole[:NB], whole[NB:]
    magnitude = jnp.sqrt(real * real + imag * imag)
    colmax = jnp.max(jnp.sum(magnitude, axis=0, keepdims=True), axis=1, keepdims=True)
    rowmax = jnp.max(jnp.sum(magnitude, axis=1, keepdims=True), axis=0, keepdims=True)
    factor = 1.0 / (colmax * rowmax + EPS_SCALE)
    iterate = jnp.concatenate([real * factor, imag * factor], 1)

    for turn in range(NEWTON):
        terms = 1 if turn < NEWTON // 2 else 2
        parts = pieces(iterate, terms)
        product = None
        for part in parts:
            crossed = jnp.concatenate([part[:, NB:], -part[:, :NB]], 1)
            right = jnp.concatenate([part, crossed], 0)
            term = lax.dot_general(
                stacked, right, (((0,), (0,)), ((), ())), preferred_element_type=F32
            )
            product = term if product is None else product + term
        seconds = pieces(product, terms)
        change = None
        for j, second in enumerate(seconds):
            crossed = jnp.concatenate([-second[:, NB:], second[:, :NB]], 1)
            right = jnp.concatenate([second, crossed], 0)
            for i, part in enumerate(parts):
                if i + j < terms:
                    term = dot(part, right)
                    change = term if change is None else change + term
        iterate = 2.0 * iterate - change
    out_ref[...] = iterate.astype(BF16)


def slope(dual, following, dual_before, before):
    real, imag = dual[:, :NB], dual[:, NB:]
    forward = jnp.concatenate(
        [jnp.concatenate([-imag, real], 1), jnp.concatenate([-real, -imag], 1)], 0
    )
    real, imag = dual_before[:, :NB], dual_before[:, NB:]
    backward = jnp.concatenate(
        [jnp.concatenate([imag, real], 1), jnp.concatenate([-real, imag], 1)], 0
    )
    return dot(forward, following) - dot(backward, before).astype(BF16).astype(F32)


def squares(grad):
    part = grad[0:8]
    part = part * part
    for row in range(8, grad.shape[0], 8):
        more = grad[row : row + 8]
        part = part + more * more
    return part[:, 0:128] + part[:, 128:256] + part[:, 256:384] + part[:, 384:512]


def orders_kernel(
    flags, y_1, y0, y1, before, p0, p1, p2, closing, beyond, g0, g1, p_1, out_ref, far
):
    choose(flags[0], closing, before, p_1)
    grad = slope(y0[...], p1[...], y_1[...], p_1[...])
    g0[...] = grad
    part = squares(grad)
    high = part.astype(BF16).astype(F32)
    pair = jnp.concatenate([high, part - high], 0).astype(BF16)
    here = grad.astype(BF16)
    choose(flags[2], beyond, p2, far)
    ahead = slope(y1[...], far[...], y0[...], p0[...]).astype(BF16)
    g1[...] = ahead
    first = (margin(here, p1[...]) + margin(p0[...], ahead)).astype(BF16)
    second = margin(here, ahead).astype(BF16)
    for part in range(PARTS):
        rows = slice(CHUNK * part, CHUNK * (part + 1))
        for index, value in enumerate((first, second)):
            for half in range(2):
                at = pl.ds(CHUNK * (2 * index + half), CHUNK)
                out_ref[part, at, :] = value[rows, 128 * half : 128 * (half + 1)]
        out_ref[part, pl.ds(4 * CHUNK, CHUNK), :] = pair


def slope_kernel(y_1, y0, p_1, p1, g0, total_ref):
    grad = slope(y0[...], p1[...], y_1[...], p_1[...])
    g0[...] = grad
    total_ref[...] = jnp.broadcast_to(squares(grad)[None], total_ref.shape)


def step_size(total_ref):
    part = jnp.sum(total_ref[...], axis=0)
    total = jnp.sum(jnp.sum(part, axis=1, keepdims=True), axis=0, keepdims=True)
    return TAU_STEP / jnp.sqrt(total / (2 * NK * NB * NPW) + EPS_NORM)


def advance_kernel(flags, total, y_2, y_1, p_2, p_1, p0, p1, closing, g0, g1, q_1, q0, q1, far):
    size = step_size(total)
    q0[...] = (p0[...].astype(F32) + size * g0[...]).astype(BF16)
    q1[...] = (p1[...].astype(F32) + size * g1[...].astype(F32)).astype(BF16)
    choose(flags[1], closing, p_2, far)
    grad = slope(y_1[...], p0[...], y_2[...], far[...])
    q_1[...] = (p_1[...].astype(F32) + size * grad).astype(BF16)


def finish_kernel(total_ref, p0, g0, re_ref, im_ref):
    size = step_size(total_ref)
    value = (p0[...].astype(F32) + size * g0[...]).astype(BF16)
    re_ref[...] = value[:NB]
    im_ref[...] = value[NB:]


def shifted(value, by):
    return lax.ppermute(value, "kstr", [(i, (i + by) % NK) for i in range(NK)])


def exchange(value, axis):
    return lax.all_to_all(value, axis, 0, 0, tiled=True)


def whole_total(part):
    parts = exchange(part, "pw")
    own = call(spread_kernel, shape((NK, 8, 128), F32), parts)
    return exchange(own, "kstr")


def inverse(whole):
    return call(newton_kernel, shape((NB, 2 * NB), BF16), whole)


def body(states_re, states_im, gmap):
    width = states_re.shape[2]
    row = lax.axis_index("kstr")
    offset = jnp.mod(gmap[0] - lax.axis_index("pw") * width, NPW)
    blocks = offset // width
    rest = offset - blocks * width
    first = row < NK // 2
    bounds = jnp.stack(
        [
            jnp.where(first, rest, 0),
            jnp.where(first, width, width - rest),
            jnp.where(first, jnp.mod(width - rest, width), rest),
        ]
    ).astype(jnp.int32)
    state = jnp.concatenate([states_re[0], states_im[0]], 0)
    full = 2 * NB
    end = NK - 1
    duals = shape((NB, full), BF16)
    fields = shape((full, width), BF16)
    grads = shape((full, width), F32)
    chunk = shape((CHUNK, NB), F32)
    chunks = shape((PARTS, CHUNK, NB), BF16)
    far_scratch = (pltpu.VMEM((full, width), BF16),)
    flags = jnp.stack([row == 0, row <= 1, row >= NK - 2, row == end]).astype(jnp.int32)

    beside = lax.ppermute(state, ("kstr", "pw"), beside_pairs())
    p1, p_1, p_2 = shifted(state, -1), shifted(state, 1), shifted(state, 2)
    p2 = shifted(state, -2)
    merged = call(merge_kernel, fields, bounds, state, beside, smem=1)
    near = close_string(merged, blocks)
    near, p1, p_1, p2, p_2 = lax.optimization_barrier((near, p1, p_1, p2, p_2))

    part, p1 = call(first_margin_kernel, (shape((full, NB), BF16), fields), flags, state, p1, near, smem=1)
    near, part = lax.optimization_barrier((near, part))
    parts = exchange(part, "pw").reshape(PARTS, CHUNK, NB)
    parts, near = lax.optimization_barrier((parts, near))
    own, kept = call(collect_kernel, (chunks, chunk), parts)
    whole = exchange(own.reshape(full, NB), "pw")
    far = lax.ppermute(near, "kstr", [(0, 1), (1, 0), (end - 1, end), (end, end - 1)])
    whole, far = lax.optimization_barrier((whole, far))

    y0 = inverse(whole)
    y_1 = shifted(y0, 1)
    y1 = shifted(y0, -1)
    g0, g1, p_1, part = call(
        orders_kernel,
        (grads, fields, fields, shape((PARTS, 5 * CHUNK, 128), BF16)),
        *(flags, y_1, y0, y1, p_1, state, p1, p2, near, far),
        smem=1,
        scratch=far_scratch,
    )
    y0, part = lax.optimization_barrier((y0, part))
    y_2 = shifted(y0, 2)
    parts = exchange(part, "pw")
    first, second, total = call(
        collect_orders_kernel, (chunk, chunk, shape((NK, 8, 128), F32)), parts
    )
    total = exchange(total, "kstr")
    own = call(combine_kernel, chunks, total, kept, first, second)
    whole = exchange(own.reshape(full, NB), "pw")
    q_1, q0, q1 = call(
        advance_kernel,
        (fields, fields, fields),
        *(flags, total, y_2, y_1, p_2, p_1, state, p1, far, g0, g1),
        smem=1,
        scratch=far_scratch,
    )

    y0 = inverse(whole)
    y_1 = shifted(y0, 1)
    g0, total = call(slope_kernel, (grads, shape((PARTS, 8, 128), F32)), y_1, y0, q_1, q1)
    total = whole_total(total)
    half = shape((NB, width), BF16)
    new_re, new_im = call(finish_kernel, (half, half), total, q0, g0)
    return new_re[None], new_im[None]


def solution(mesh):
    placed = (P("kstr", None, "pw"), P("kstr", None, "pw"), P("pw"))
    return jax.shard_map(
        body,
        mesh=mesh,
        in_specs=placed,
        out_specs=(P("kstr", None, "pw"), P("kstr", None, "pw")),
        check_vma=False,
    )
```

```python
import jax
import jax.numpy as jnp
from jax import lax
from jax.experimental import pallas as pl
from jax.experimental.pallas import tpu as pltpu
from jax.sharding import PartitionSpec as P

NEWTON = 4
NK = 16
NPW = 16384
NB = 256
PARTS = 32
CHUNK = 2 * NB // PARTS
EPS_SCALE = 1e-06
EPS_NORM = 1e-06
TAU_STEP = 0.25
F32 = jnp.float32
BF16 = jnp.bfloat16


def call(kernel, outs, *args, smem=0, flops=0, scratch=()):
    specs = [pl.BlockSpec(memory_space=pltpu.SMEM)] * smem
    specs += [pl.BlockSpec(memory_space=pltpu.VMEM)] * (len(args) - smem)
    single = not isinstance(outs, (tuple, list))
    outs = (outs,) if single else tuple(outs)
    moved = sum(a.size * a.dtype.itemsize for a in args) + sum(
        o.size * o.dtype.itemsize for o in outs
    )
    result = pl.pallas_call(
        kernel,
        out_shape=outs,
        in_specs=specs,
        out_specs=tuple(pl.BlockSpec(memory_space=pltpu.VMEM) for _ in outs),
        scratch_shapes=list(scratch),
        compiler_params=pltpu.CompilerParams(vmem_limit_bytes=14 * 1024 * 1024),
        cost_estimate=pl.CostEstimate(flops=flops, bytes_accessed=moved, transcendentals=0),
    )(*args)
    return result[0] if single else result


def shape(dims, dtype):
    return jax.ShapeDtypeStruct(dims, dtype)


def dot(left, right):
    return jnp.dot(left, right, preferred_element_type=F32)


def margin(left, right):
    every = lax.dot_general(left, right, (((1,), (1,)), ((), ())), preferred_element_type=F32)
    real = every[:NB, :NB] + every[NB:, NB:]
    return jnp.concatenate([real, every[:NB, NB:] - every[NB:, :NB]], 0)


def choose(flag, yes_ref, no_ref, out_ref):
    @pl.when(flag == 1)
    def _():
        out_ref[...] = yes_ref[...]

    @pl.when(flag != 1)
    def _():
        out_ref[...] = no_ref[...]


def margin_kernel(state_ref, next_ref, out_ref):
    out_ref[...] = margin(state_ref[...], next_ref[...]).astype(BF16)


def first_margin_kernel(flags, state_ref, next_ref, closing_ref, out_ref, chosen_ref):
    choose(flags[3], closing_ref, next_ref, chosen_ref)
    margin_kernel(state_ref, chosen_ref, out_ref)


def merge_kernel(bounds, state_ref, beside_ref, out_ref):
    lane = lax.broadcasted_iota(jnp.int32, (CHUNK, state_ref.shape[1]), 1)
    own = (lane >= bounds[0]) & (lane < bounds[1])
    for row in range(0, state_ref.shape[0], CHUNK):
        rows = pl.ds(row, CHUNK)
        value = jnp.where(own, state_ref[rows, :].astype(F32), beside_ref[rows, :].astype(F32))
        out_ref[rows, :] = pltpu.roll(value, bounds[2], 1).astype(BF16)


def place(row, column):
    return row * PARTS + column % PARTS


def beside_pairs():
    pairs = []
    for j in range(PARTS):
        pairs += [(place(row, j), place(row, j - 1)) for row in (0, 1)]
        pairs += [(place(row, j), place(row, j + 1)) for row in (NK - 2, NK - 1)]
    return pairs


def closing_pairs(by):
    pairs = []
    for j in range(PARTS):
        for row in (0, 1):
            pairs.append((place(row, j), place(NK - 1 - row, j - by)))
            pairs.append((place(NK - 1 - row, j), place(row, j + by)))
    for row in range(2, NK - 2):
        pairs += [(place(row, j), place(row, j)) for j in range(PARTS)]
    return pairs


def close_string(value, blocks):
    def branch(by):
        return lambda block: lax.ppermute(block, ("kstr", "pw"), closing_pairs(by))

    return lax.switch(blocks, [branch(by) for by in range(PARTS)], value)


def collect_kernel(parts_ref, out_ref, kept_ref):
    total = jnp.sum(parts_ref[...].astype(F32), axis=0) * (1.0 / NPW)
    kept_ref[...] = total
    out_ref[...] = jnp.broadcast_to(total.astype(BF16)[None], out_ref.shape)


def collect_orders_kernel(parts_ref, first_ref, second_ref, squares_ref):
    total = jnp.sum(parts_ref[...].astype(F32), axis=0)
    for half in range(2):
        lanes = pl.ds(128 * half, 128)
        first_ref[:, lanes] = total[CHUNK * half : CHUNK * (half + 1)] * (1.0 / NPW)
        second_ref[:, lanes] = total[CHUNK * (2 + half) : CHUNK * (3 + half)] * (1.0 / NPW)
    part = total[4 * CHUNK : 4 * CHUNK + 8] + total[4 * CHUNK + 8 :]
    squares_ref[...] = jnp.broadcast_to(part[None], squares_ref.shape)


def combine_kernel(total_ref, kept_ref, first_ref, second_ref, out_ref):
    size = step_size(total_ref)
    value = kept_ref[...] + size * (first_ref[...] + size * second_ref[...])
    out_ref[...] = jnp.broadcast_to(value.astype(BF16)[None], out_ref.shape)


def spread_kernel(parts_ref, out_ref):
    total = jnp.sum(parts_ref[...], axis=0)
    out_ref[...] = jnp.broadcast_to(total[None], out_ref.shape)


def pieces(value, count):
    high = value.astype(BF16)
    if count == 1:
        return [high]
    return [high, (value - high.astype(F32)).astype(BF16)]


def newton_kernel(margin_ref, out_ref):
    stacked = margin_ref[...]
    whole = stacked.astype(F32)
    real, imag = whole[:NB], whole[NB:]
    magnitude = jnp.sqrt(real * real + imag * imag)
    colmax = jnp.max(jnp.sum(magnitude, axis=0, keepdims=True), axis=1, keepdims=True)
    rowmax = jnp.max(jnp.sum(magnitude, axis=1, keepdims=True), axis=0, keepdims=True)
    factor = 1.0 / (colmax * rowmax + EPS_SCALE)
    iterate = jnp.concatenate([real * factor, imag * factor], 1)

    for turn in range(NEWTON):
        terms = 1 if turn < NEWTON // 2 else 2
        parts = pieces(iterate, terms)
        product = None
        for part in parts:
            crossed = jnp.concatenate([part[:, NB:], -part[:, :NB]], 1)
            right = jnp.concatenate([part, crossed], 0)
            term = lax.dot_general(
                stacked, right, (((0,), (0,)), ((), ())), preferred_element_type=F32
            )
            product = term if product is None else product + term
        seconds = pieces(product, terms)
        change = None
        for j, second in enumerate(seconds):
            crossed = jnp.concatenate([-second[:, NB:], second[:, :NB]], 1)
            right = jnp.concatenate([second, crossed], 0)
            for i, part in enumerate(parts):
                if i + j < terms:
                    term = dot(part, right)
                    change = term if change is None else change + term
        iterate = 2.0 * iterate - change
    out_ref[...] = iterate.astype(BF16)


def slope(dual, following, dual_before, before):
    real, imag = dual[:, :NB], dual[:, NB:]
    forward = jnp.concatenate(
        [jnp.concatenate([-imag, real], 1), jnp.concatenate([-real, -imag], 1)], 0
    )
    real, imag = dual_before[:, :NB], dual_before[:, NB:]
    backward = jnp.concatenate(
        [jnp.concatenate([imag, real], 1), jnp.concatenate([-real, imag], 1)], 0
    )
    return dot(forward, following) - dot(backward, before).astype(BF16).astype(F32)


def squares(grad):
    part = grad[0:8]
    part = part * part
    for row in range(8, grad.shape[0], 8):
        more = grad[row : row + 8]
        part = part + more * more
    return part[:, 0:128] + part[:, 128:256] + part[:, 256:384] + part[:, 384:512]


def orders_kernel(
    flags, y_1, y0, y1, before, p0, p1, p2, closing, beyond, g0, g1, p_1, out_ref, far
):
    choose(flags[0], closing, before, p_1)
    grad = slope(y0[...], p1[...], y_1[...], p_1[...])
    g0[...] = grad
    part = squares(grad)
    high = part.astype(BF16).astype(F32)
    pair = jnp.concatenate([high, part - high], 0).astype(BF16)
    here = grad.astype(BF16)
    choose(flags[2], beyond, p2, far)
    ahead = slope(y1[...], far[...], y0[...], p0[...]).astype(BF16)
    g1[...] = ahead
    first = (margin(here, p1[...]) + margin(p0[...], ahead)).astype(BF16)
    second = margin(here, ahead).astype(BF16)
    for part in range(PARTS):
        rows = slice(CHUNK * part, CHUNK * (part + 1))
        for index, value in enumerate((first, second)):
            for half in range(2):
                at = pl.ds(CHUNK * (2 * index + half), CHUNK)
                out_ref[part, at, :] = value[rows, 128 * half : 128 * (half + 1)]
        out_ref[part, pl.ds(4 * CHUNK, CHUNK), :] = pair


def slope_kernel(y_1, y0, p_1, p1, g0, total_ref):
    grad = slope(y0[...], p1[...], y_1[...], p_1[...])
    g0[...] = grad
    total_ref[...] = jnp.broadcast_to(squares(grad)[None], total_ref.shape)


def step_size(total_ref):
    part = jnp.sum(total_ref[...], axis=0)
    total = jnp.sum(jnp.sum(part, axis=1, keepdims=True), axis=0, keepdims=True)
    return TAU_STEP / jnp.sqrt(total / (2 * NK * NB * NPW) + EPS_NORM)


def advance_kernel(flags, total, y_2, y_1, p_2, p_1, p0, p1, closing, g0, g1, q_1, q0, q1, far):
    size = step_size(total)
    q0[...] = (p0[...].astype(F32) + size * g0[...]).astype(BF16)
    q1[...] = (p1[...].astype(F32) + size * g1[...].astype(F32)).astype(BF16)
    choose(flags[1], closing, p_2, far)
    grad = slope(y_1[...], p0[...], y_2[...], far[...])
    q_1[...] = (p_1[...].astype(F32) + size * grad).astype(BF16)


def finish_kernel(total_ref, p0, g0, re_ref, im_ref):
    size = step_size(total_ref)
    value = (p0[...].astype(F32) + size * g0[...]).astype(BF16)
    re_ref[...] = value[:NB]
    im_ref[...] = value[NB:]


def shifted(value, by):
    return lax.ppermute(value, "kstr", [(i, (i + by) % NK) for i in range(NK)])


def exchange(value, axis):
    return lax.all_to_all(value, axis, 0, 0, tiled=True)


def whole_total(part):
    parts = exchange(part, "pw")
    own = call(spread_kernel, shape((NK, 8, 128), F32), parts)
    return exchange(own, "kstr")


def inverse(whole):
    return call(newton_kernel, shape((NB, 2 * NB), BF16), whole)


def body(states_re, states_im, gmap):
    width = states_re.shape[2]
    row = lax.axis_index("kstr")
    offset = jnp.mod(gmap[0] - lax.axis_index("pw") * width, NPW)
    blocks = offset // width
    rest = offset - blocks * width
    first = row < NK // 2
    bounds = jnp.stack(
        [
            jnp.where(first, rest, 0),
            jnp.where(first, width, width - rest),
            jnp.where(first, jnp.mod(width - rest, width), rest),
        ]
    ).astype(jnp.int32)
    state = jnp.concatenate([states_re[0], states_im[0]], 0)
    full = 2 * NB
    end = NK - 1
    duals = shape((NB, full), BF16)
    fields = shape((full, width), BF16)
    grads = shape((full, width), F32)
    chunk = shape((CHUNK, NB), F32)
    chunks = shape((PARTS, CHUNK, NB), BF16)
    far_scratch = (pltpu.VMEM((full, width), BF16),)
    flags = jnp.stack([row == 0, row <= 1, row >= NK - 2, row == end]).astype(jnp.int32)

    beside = lax.ppermute(state, ("kstr", "pw"), beside_pairs())
    p1, p_2 = shifted(state, -1), shifted(state, 2)
    p2 = shifted(state, -2)
    merged = call(merge_kernel, fields, bounds, state, beside, smem=1)
    near = close_string(merged, blocks)
    near, p1, p2, p_2 = lax.optimization_barrier((near, p1, p2, p_2))

    part, p1 = call(first_margin_kernel, (shape((full, NB), BF16), fields), flags, state, p1, near, smem=1)
    state, near, part = lax.optimization_barrier((state, near, part))
    parts = exchange(part, "pw").reshape(PARTS, CHUNK, NB)
    p_1 = shifted(state, 1)
    parts, p_1, near = lax.optimization_barrier((parts, p_1, near))
    own, kept = call(collect_kernel, (chunks, chunk), parts)
    whole = exchange(own.reshape(full, NB), "pw")
    far = lax.ppermute(near, "kstr", [(0, 1), (1, 0), (end - 1, end), (end, end - 1)])
    whole, far = lax.optimization_barrier((whole, far))

    y0 = inverse(whole)
    y_1 = shifted(y0, 1)
    y1 = shifted(y0, -1)
    g0, g1, p_1, part = call(
        orders_kernel,
        (grads, fields, fields, shape((PARTS, 5 * CHUNK, 128), BF16)),
        *(flags, y_1, y0, y1, p_1, state, p1, p2, near, far),
        smem=1,
        scratch=far_scratch,
    )
    y0, part = lax.optimization_barrier((y0, part))
    y_2 = shifted(y0, 2)
    parts = exchange(part, "pw")
    first, second, total = call(
        collect_orders_kernel, (chunk, chunk, shape((NK, 8, 128), F32)), parts
    )
    total = exchange(total, "kstr")
    own = call(combine_kernel, chunks, total, kept, first, second)
    whole = exchange(own.reshape(full, NB), "pw")
    q_1, q0, q1 = call(
        advance_kernel,
        (fields, fields, fields),
        *(flags, total, y_2, y_1, p_2, p_1, state, p1, far, g0, g1),
        smem=1,
        scratch=far_scratch,
    )

    y0 = inverse(whole)
    y_1 = shifted(y0, 1)
    g0, total = call(slope_kernel, (grads, shape((PARTS, 8, 128), F32)), y_1, y0, q_1, q1)
    total = whole_total(total)
    half = shape((NB, width), BF16)
    new_re, new_im = call(finish_kernel, (half, half), total, q0, g0)
    return new_re[None], new_im[None]


def solution(mesh):
    placed = (P("kstr", None, "pw"), P("kstr", None, "pw"), P("pw"))
    return jax.shard_map(
        body,
        mesh=mesh,
        in_specs=placed,
        out_specs=(P("kstr", None, "pw"), P("kstr", None, "pw")),
        check_vma=False,
    )
```

```python
import jax
import jax.numpy as jnp
from jax import lax
from jax.experimental import pallas as pl
from jax.experimental.pallas import tpu as pltpu
from jax.sharding import PartitionSpec as P

NEWTON = 4
NK = 16
NPW = 16384
NB = 256
PARTS = 32
CHUNK = 2 * NB // PARTS
EPS_SCALE = 1e-06
EPS_NORM = 1e-06
TAU_STEP = 0.25
F32 = jnp.float32
BF16 = jnp.bfloat16


def call(kernel, outs, *args, smem=0, flops=0, scratch=()):
    specs = [pl.BlockSpec(memory_space=pltpu.SMEM)] * smem
    specs += [pl.BlockSpec(memory_space=pltpu.VMEM)] * (len(args) - smem)
    single = not isinstance(outs, (tuple, list))
    outs = (outs,) if single else tuple(outs)
    moved = sum(a.size * a.dtype.itemsize for a in args) + sum(
        o.size * o.dtype.itemsize for o in outs
    )
    result = pl.pallas_call(
        kernel,
        out_shape=outs,
        in_specs=specs,
        out_specs=tuple(pl.BlockSpec(memory_space=pltpu.VMEM) for _ in outs),
        scratch_shapes=list(scratch),
        compiler_params=pltpu.CompilerParams(vmem_limit_bytes=14 * 1024 * 1024),
        cost_estimate=pl.CostEstimate(flops=flops, bytes_accessed=moved, transcendentals=0),
    )(*args)
    return result[0] if single else result


def shape(dims, dtype):
    return jax.ShapeDtypeStruct(dims, dtype)


def dot(left, right):
    return jnp.dot(left, right, preferred_element_type=F32)


def margin(left, right):
    every = lax.dot_general(left, right, (((1,), (1,)), ((), ())), preferred_element_type=F32)
    real = every[:NB, :NB] + every[NB:, NB:]
    return jnp.concatenate([real, every[:NB, NB:] - every[NB:, :NB]], 0)


def choose(flag, yes_ref, no_ref, out_ref):
    @pl.when(flag == 1)
    def _():
        out_ref[...] = yes_ref[...]

    @pl.when(flag != 1)
    def _():
        out_ref[...] = no_ref[...]


def margin_kernel(state_ref, next_ref, out_ref):
    out_ref[...] = margin(state_ref[...], next_ref[...]).astype(BF16)


def first_margin_kernel(flags, state_ref, next_ref, closing_ref, out_ref, chosen_ref):
    choose(flags[3], closing_ref, next_ref, chosen_ref)
    margin_kernel(state_ref, chosen_ref, out_ref)


def merge_kernel(bounds, state_ref, beside_ref, out_ref):
    lane = lax.broadcasted_iota(jnp.int32, (CHUNK, state_ref.shape[1]), 1)
    own = (lane >= bounds[0]) & (lane < bounds[1])
    for row in range(0, state_ref.shape[0], CHUNK):
        rows = pl.ds(row, CHUNK)
        value = jnp.where(own, state_ref[rows, :].astype(F32), beside_ref[rows, :].astype(F32))
        out_ref[rows, :] = pltpu.roll(value, bounds[2], 1).astype(BF16)


def place(row, column):
    return row * PARTS + column % PARTS


def beside_pairs():
    pairs = []
    for j in range(PARTS):
        pairs += [(place(row, j), place(row, j - 1)) for row in (0, 1)]
        pairs += [(place(row, j), place(row, j + 1)) for row in (NK - 2, NK - 1)]
    return pairs


def closing_pairs(by):
    pairs = []
    for j in range(PARTS):
        for row in (0, 1):
            pairs.append((place(row, j), place(NK - 1 - row, j - by)))
            pairs.append((place(NK - 1 - row, j), place(row, j + by)))
    for row in range(2, NK - 2):
        pairs += [(place(row, j), place(row, j)) for j in range(PARTS)]
    return pairs


def close_string(value, blocks):
    def branch(by):
        return lambda block: lax.ppermute(block, ("kstr", "pw"), closing_pairs(by))

    return lax.switch(blocks, [branch(by) for by in range(PARTS)], value)


def collect_kernel(parts_ref, out_ref, kept_ref):
    total = jnp.sum(parts_ref[...].astype(F32), axis=0) * (1.0 / NPW)
    kept_ref[...] = total
    out_ref[...] = jnp.broadcast_to(total.astype(BF16)[None], out_ref.shape)


def collect_orders_kernel(parts_ref, first_ref, second_ref, squares_ref):
    total = jnp.sum(parts_ref[...].astype(F32), axis=0)
    for half in range(2):
        lanes = pl.ds(128 * half, 128)
        first_ref[:, lanes] = total[CHUNK * half : CHUNK * (half + 1)] * (1.0 / NPW)
        second_ref[:, lanes] = total[CHUNK * (2 + half) : CHUNK * (3 + half)] * (1.0 / NPW)
    part = total[4 * CHUNK : 4 * CHUNK + 8] + total[4 * CHUNK + 8 :]
    squares_ref[...] = jnp.broadcast_to(part[None], squares_ref.shape)


def combine_kernel(total_ref, kept_ref, first_ref, second_ref, out_ref):
    size = step_size(total_ref)
    value = kept_ref[...] + size * (first_ref[...] + size * second_ref[...])
    out_ref[...] = jnp.broadcast_to(value.astype(BF16)[None], out_ref.shape)


def spread_kernel(parts_ref, out_ref):
    total = jnp.sum(parts_ref[...], axis=0)
    out_ref[...] = jnp.broadcast_to(total[None], out_ref.shape)


def pieces(value, count):
    high = value.astype(BF16)
    if count == 1:
        return [high]
    return [high, (value - high.astype(F32)).astype(BF16)]


def newton_kernel(margin_ref, out_ref):
    stacked = margin_ref[...]
    whole = stacked.astype(F32)
    real, imag = whole[:NB], whole[NB:]
    magnitude = jnp.sqrt(real * real + imag * imag)
    colmax = jnp.max(jnp.sum(magnitude, axis=0, keepdims=True), axis=1, keepdims=True)
    rowmax = jnp.max(jnp.sum(magnitude, axis=1, keepdims=True), axis=0, keepdims=True)
    factor = 1.0 / (colmax * rowmax + EPS_SCALE)
    iterate = jnp.concatenate([real * factor, imag * factor], 1)

    for turn in range(NEWTON):
        terms = 1 if turn < NEWTON // 2 else 2
        parts = pieces(iterate, terms)
        product = None
        for part in parts:
            crossed = jnp.concatenate([part[:, NB:], -part[:, :NB]], 1)
            right = jnp.concatenate([part, crossed], 0)
            term = lax.dot_general(
                stacked, right, (((0,), (0,)), ((), ())), preferred_element_type=F32
            )
            product = term if product is None else product + term
        seconds = pieces(product, terms)
        change = None
        for j, second in enumerate(seconds):
            crossed = jnp.concatenate([-second[:, NB:], second[:, :NB]], 1)
            right = jnp.concatenate([second, crossed], 0)
            for i, part in enumerate(parts):
                if i + j < terms:
                    term = dot(part, right)
                    change = term if change is None else change + term
        iterate = 2.0 * iterate - change
    out_ref[...] = iterate.astype(BF16)


def slope(dual, following, dual_before, before):
    real, imag = dual[:, :NB], dual[:, NB:]
    forward = jnp.concatenate(
        [jnp.concatenate([-imag, real], 1), jnp.concatenate([-real, -imag], 1)], 0
    )
    real, imag = dual_before[:, :NB], dual_before[:, NB:]
    backward = jnp.concatenate(
        [jnp.concatenate([imag, real], 1), jnp.concatenate([-real, imag], 1)], 0
    )
    return dot(forward, following) - dot(backward, before).astype(BF16).astype(F32)


def squares(grad):
    part = grad[0:8]
    part = part * part
    for row in range(8, grad.shape[0], 8):
        more = grad[row : row + 8]
        part = part + more * more
    return part[:, 0:128] + part[:, 128:256] + part[:, 256:384] + part[:, 384:512]


def orders_kernel(
    flags, y_1, y0, y1, before, p0, p1, p2, closing, beyond, g0, g1, p_1, out_ref, far
):
    choose(flags[0], closing, before, p_1)
    grad = slope(y0[...], p1[...], y_1[...], p_1[...])
    g0[...] = grad
    part = squares(grad)
    high = part.astype(BF16).astype(F32)
    pair = jnp.concatenate([high, part - high], 0).astype(BF16)
    here = grad.astype(BF16)
    choose(flags[2], beyond, p2, far)
    ahead = slope(y1[...], far[...], y0[...], p0[...]).astype(BF16)
    g1[...] = ahead
    first = (margin(here, p1[...]) + margin(p0[...], ahead)).astype(BF16)
    second = margin(here, ahead).astype(BF16)
    for part in range(PARTS):
        rows = slice(CHUNK * part, CHUNK * (part + 1))
        for index, value in enumerate((first, second)):
            for half in range(2):
                at = pl.ds(CHUNK * (2 * index + half), CHUNK)
                out_ref[part, at, :] = value[rows, 128 * half : 128 * (half + 1)]
        out_ref[part, pl.ds(4 * CHUNK, CHUNK), :] = pair


def slope_kernel(y_1, y0, p_1, p1, g0, total_ref):
    grad = slope(y0[...], p1[...], y_1[...], p_1[...])
    g0[...] = grad
    total_ref[...] = jnp.broadcast_to(squares(grad)[None], total_ref.shape)


def step_size(total_ref):
    part = jnp.sum(total_ref[...], axis=0)
    total = jnp.sum(jnp.sum(part, axis=1, keepdims=True), axis=0, keepdims=True)
    return TAU_STEP / jnp.sqrt(total / (2 * NK * NB * NPW) + EPS_NORM)


def advance_kernel(flags, total, y_2, y_1, p_2, p_1, p0, p1, closing, g0, g1, q_1, q0, q1, far):
    size = step_size(total)
    q0[...] = (p0[...].astype(F32) + size * g0[...]).astype(BF16)
    q1[...] = (p1[...].astype(F32) + size * g1[...].astype(F32)).astype(BF16)
    choose(flags[1], closing, p_2, far)
    grad = slope(y_1[...], p0[...], y_2[...], far[...])
    q_1[...] = (p_1[...].astype(F32) + size * grad).astype(BF16)


def finish_kernel(total_ref, p0, g0, re_ref, im_ref):
    size = step_size(total_ref)
    value = (p0[...].astype(F32) + size * g0[...]).astype(BF16)
    re_ref[...] = value[:NB]
    im_ref[...] = value[NB:]


def shifted(value, by):
    return lax.ppermute(value, "kstr", [(i, (i + by) % NK) for i in range(NK)])


def exchange(value, axis):
    return lax.all_to_all(value, axis, 0, 0, tiled=True)


def whole_total(part):
    parts = exchange(part, "pw")
    own = call(spread_kernel, shape((NK, 8, 128), F32), parts)
    return exchange(own, "kstr")


def inverse(whole):
    return call(newton_kernel, shape((NB, 2 * NB), BF16), whole)


def body(states_re, states_im, gmap):
    width = states_re.shape[2]
    row = lax.axis_index("kstr")
    offset = jnp.mod(gmap[0] - lax.axis_index("pw") * width, NPW)
    blocks = offset // width
    rest = offset - blocks * width
    first = row < NK // 2
    bounds = jnp.stack(
        [
            jnp.where(first, rest, 0),
            jnp.where(first, width, width - rest),
            jnp.where(first, jnp.mod(width - rest, width), rest),
        ]
    ).astype(jnp.int32)
    state = jnp.concatenate([states_re[0], states_im[0]], 0)
    full = 2 * NB
    end = NK - 1
    duals = shape((NB, full), BF16)
    fields = shape((full, width), BF16)
    grads = shape((full, width), F32)
    chunk = shape((CHUNK, NB), F32)
    chunks = shape((PARTS, CHUNK, NB), BF16)
    far_scratch = (pltpu.VMEM((full, width), BF16),)
    flags = jnp.stack([row == 0, row <= 1, row >= NK - 2, row == end]).astype(jnp.int32)

    beside = lax.ppermute(state, ("kstr", "pw"), beside_pairs())
    p1, p_2 = shifted(state, -1), shifted(state, 2)
    p2 = shifted(state, -2)
    merged = call(merge_kernel, fields, bounds, state, beside, smem=1)
    near = close_string(merged, blocks)
    near, p1, p2, p_2 = lax.optimization_barrier((near, p1, p2, p_2))

    part, p1 = call(first_margin_kernel, (shape((full, NB), BF16), fields), flags, state, p1, near, smem=1)
    state, near, part = lax.optimization_barrier((state, near, part))
    p_1 = shifted(state, 1)
    far = lax.ppermute(near, "kstr", [(0, 1), (1, 0), (end - 1, end), (end, end - 1)])
    parts = exchange(part, "pw").reshape(PARTS, CHUNK, NB)
    own, kept = call(collect_kernel, (chunks, chunk), parts)
    whole = exchange(own.reshape(full, NB), "pw")
    whole, far, p_1 = lax.optimization_barrier((whole, far, p_1))

    y0 = inverse(whole)
    y_1 = shifted(y0, 1)
    y1 = shifted(y0, -1)
    g0, g1, p_1, part = call(
        orders_kernel,
        (grads, fields, fields, shape((PARTS, 5 * CHUNK, 128), BF16)),
        *(flags, y_1, y0, y1, p_1, state, p1, p2, near, far),
        smem=1,
        scratch=far_scratch,
    )
    y0, part = lax.optimization_barrier((y0, part))
    y_2 = shifted(y0, 2)
    parts = exchange(part, "pw")
    first, second, total = call(
        collect_orders_kernel, (chunk, chunk, shape((NK, 8, 128), F32)), parts
    )
    total = exchange(total, "kstr")
    own = call(combine_kernel, chunks, total, kept, first, second)
    whole = exchange(own.reshape(full, NB), "pw")
    q_1, q0, q1 = call(
        advance_kernel,
        (fields, fields, fields),
        *(flags, total, y_2, y_1, p_2, p_1, state, p1, far, g0, g1),
        smem=1,
        scratch=far_scratch,
    )

    y0 = inverse(whole)
    y_1 = shifted(y0, 1)
    g0, total = call(slope_kernel, (grads, shape((PARTS, 8, 128), F32)), y_1, y0, q_1, q1)
    total = whole_total(total)
    half = shape((NB, width), BF16)
    new_re, new_im = call(finish_kernel, (half, half), total, q0, g0)
    return new_re[None], new_im[None]


def solution(mesh):
    placed = (P("kstr", None, "pw"), P("kstr", None, "pw"), P("pw"))
    return jax.shard_map(
        body,
        mesh=mesh,
        in_specs=placed,
        out_specs=(P("kstr", None, "pw"), P("kstr", None, "pw")),
        check_vma=False,
    )
```

```python
import jax
import jax.numpy as jnp
from jax import lax
from jax.experimental import pallas as pl
from jax.experimental.pallas import tpu as pltpu
from jax.sharding import PartitionSpec as P

NEWTON = 4
NK = 16
NPW = 16384
NB = 256
PARTS = 32
CHUNK = 2 * NB // PARTS
EPS_SCALE = 1e-06
EPS_NORM = 1e-06
TAU_STEP = 0.25
F32 = jnp.float32
BF16 = jnp.bfloat16


def call(kernel, outs, *args, smem=0, flops=0, scratch=()):
    specs = [pl.BlockSpec(memory_space=pltpu.SMEM)] * smem
    specs += [pl.BlockSpec(memory_space=pltpu.VMEM)] * (len(args) - smem)
    single = not isinstance(outs, (tuple, list))
    outs = (outs,) if single else tuple(outs)
    moved = sum(a.size * a.dtype.itemsize for a in args) + sum(
        o.size * o.dtype.itemsize for o in outs
    )
    result = pl.pallas_call(
        kernel,
        out_shape=outs,
        in_specs=specs,
        out_specs=tuple(pl.BlockSpec(memory_space=pltpu.VMEM) for _ in outs),
        scratch_shapes=list(scratch),
        compiler_params=pltpu.CompilerParams(vmem_limit_bytes=14 * 1024 * 1024),
        cost_estimate=pl.CostEstimate(flops=flops, bytes_accessed=moved, transcendentals=0),
    )(*args)
    return result[0] if single else result


def shape(dims, dtype):
    return jax.ShapeDtypeStruct(dims, dtype)


def dot(left, right):
    return jnp.dot(left, right, preferred_element_type=F32)


def margin(left, right):
    every = lax.dot_general(left, right, (((1,), (1,)), ((), ())), preferred_element_type=F32)
    real = every[:NB, :NB] + every[NB:, NB:]
    return jnp.concatenate([real, every[:NB, NB:] - every[NB:, :NB]], 0)


def choose(flag, yes_ref, no_ref, out_ref):
    @pl.when(flag == 1)
    def _():
        out_ref[...] = yes_ref[...]

    @pl.when(flag != 1)
    def _():
        out_ref[...] = no_ref[...]


def margin_kernel(state_ref, next_ref, out_ref):
    out_ref[...] = margin(state_ref[...], next_ref[...]).astype(BF16)


def first_margin_kernel(flags, state_ref, next_ref, closing_ref, out_ref, chosen_ref):
    choose(flags[3], closing_ref, next_ref, chosen_ref)
    margin_kernel(state_ref, chosen_ref, out_ref)


def merge_kernel(bounds, state_ref, beside_ref, out_ref):
    lane = lax.broadcasted_iota(jnp.int32, (CHUNK, state_ref.shape[1]), 1)
    own = (lane >= bounds[0]) & (lane < bounds[1])
    for row in range(0, state_ref.shape[0], CHUNK):
        rows = pl.ds(row, CHUNK)
        value = jnp.where(own, state_ref[rows, :].astype(F32), beside_ref[rows, :].astype(F32))
        out_ref[rows, :] = pltpu.roll(value, bounds[2], 1).astype(BF16)


def place(row, column):
    return row * PARTS + column % PARTS


def beside_pairs():
    pairs = []
    for j in range(PARTS):
        pairs += [(place(row, j), place(row, j - 1)) for row in (0, 1)]
        pairs += [(place(row, j), place(row, j + 1)) for row in (NK - 2, NK - 1)]
    return pairs


def closing_pairs(by):
    pairs = []
    for j in range(PARTS):
        for row in (0, 1):
            pairs.append((place(row, j), place(NK - 1 - row, j - by)))
            pairs.append((place(NK - 1 - row, j), place(row, j + by)))
    for row in range(2, NK - 2):
        pairs += [(place(row, j), place(row, j)) for j in range(PARTS)]
    return pairs


def close_string(value, blocks):
    def branch(by):
        return lambda block: lax.ppermute(block, ("kstr", "pw"), closing_pairs(by))

    return lax.switch(blocks, [branch(by) for by in range(PARTS)], value)


def collect_kernel(parts_ref, out_ref, kept_ref):
    total = jnp.sum(parts_ref[...].astype(F32), axis=0) * (1.0 / NPW)
    kept_ref[...] = total
    out_ref[...] = jnp.broadcast_to(total.astype(BF16)[None], out_ref.shape)


def collect_orders_kernel(parts_ref, first_ref, second_ref, squares_ref):
    total = jnp.sum(parts_ref[...].astype(F32), axis=0)
    for half in range(2):
        lanes = pl.ds(128 * half, 128)
        first_ref[:, lanes] = total[CHUNK * half : CHUNK * (half + 1)] * (1.0 / NPW)
        second_ref[:, lanes] = total[CHUNK * (2 + half) : CHUNK * (3 + half)] * (1.0 / NPW)
    part = total[4 * CHUNK : 4 * CHUNK + 8] + total[4 * CHUNK + 8 :]
    squares_ref[...] = jnp.broadcast_to(part[None], squares_ref.shape)


def combine_kernel(total_ref, kept_ref, first_ref, second_ref, out_ref):
    size = step_size(total_ref)
    value = kept_ref[...] + size * (first_ref[...] + size * second_ref[...])
    out_ref[...] = jnp.broadcast_to(value.astype(BF16)[None], out_ref.shape)


def spread_kernel(parts_ref, out_ref):
    total = jnp.sum(parts_ref[...], axis=0)
    out_ref[...] = jnp.broadcast_to(total[None], out_ref.shape)


def pieces(value, count):
    high = value.astype(BF16)
    if count == 1:
        return [high]
    return [high, (value - high.astype(F32)).astype(BF16)]


def newton_kernel(margin_ref, out_ref):
    stacked = margin_ref[...]
    whole = stacked.astype(F32)
    real, imag = whole[:NB], whole[NB:]
    magnitude = jnp.sqrt(real * real + imag * imag)
    colmax = jnp.max(jnp.sum(magnitude, axis=0, keepdims=True), axis=1, keepdims=True)
    rowmax = jnp.max(jnp.sum(magnitude, axis=1, keepdims=True), axis=0, keepdims=True)
    factor = 1.0 / (colmax * rowmax + EPS_SCALE)
    iterate = jnp.concatenate([real * factor, imag * factor], 1)

    for turn in range(NEWTON):
        terms = 1 if turn < NEWTON // 2 else 2
        parts = pieces(iterate, terms)
        product = None
        for part in parts:
            crossed = jnp.concatenate([part[:, NB:], -part[:, :NB]], 1)
            right = jnp.concatenate([part, crossed], 0)
            term = lax.dot_general(
                stacked, right, (((0,), (0,)), ((), ())), preferred_element_type=F32
            )
            product = term if product is None else product + term
        seconds = pieces(product, terms)
        change = None
        for j, second in enumerate(seconds):
            crossed = jnp.concatenate([-second[:, NB:], second[:, :NB]], 1)
            right = jnp.concatenate([second, crossed], 0)
            for i, part in enumerate(parts):
                if i + j < terms:
                    term = dot(part, right)
                    change = term if change is None else change + term
        iterate = 2.0 * iterate - change
    out_ref[...] = iterate.astype(BF16)


def slope(dual, following, dual_before, before):
    real, imag = dual[:, :NB], dual[:, NB:]
    forward = jnp.concatenate(
        [jnp.concatenate([-imag, real], 1), jnp.concatenate([-real, -imag], 1)], 0
    )
    real, imag = dual_before[:, :NB], dual_before[:, NB:]
    backward = jnp.concatenate(
        [jnp.concatenate([imag, real], 1), jnp.concatenate([-real, imag], 1)], 0
    )
    return dot(forward, following) - dot(backward, before).astype(BF16).astype(F32)


def squares(grad):
    part = grad[0:8]
    part = part * part
    for row in range(8, grad.shape[0], 8):
        more = grad[row : row + 8]
        part = part + more * more
    return part[:, 0:128] + part[:, 128:256] + part[:, 256:384] + part[:, 384:512]


def orders_kernel(
    flags, y_1, y0, y1, before, p0, p1, p2, closing, beyond, g0, g1, p_1, out_ref, far
):
    choose(flags[0], closing, before, p_1)
    grad = slope(y0[...], p1[...], y_1[...], p_1[...])
    g0[...] = grad
    part = squares(grad)
    high = part.astype(BF16).astype(F32)
    pair = jnp.concatenate([high, part - high], 0).astype(BF16)
    here = grad.astype(BF16)
    choose(flags[2], beyond, p2, far)
    ahead = slope(y1[...], far[...], y0[...], p0[...]).astype(BF16)
    g1[...] = ahead
    first = (margin(here, p1[...]) + margin(p0[...], ahead)).astype(BF16)
    second = margin(here, ahead).astype(BF16)
    for part in range(PARTS):
        rows = slice(CHUNK * part, CHUNK * (part + 1))
        for index, value in enumerate((first, second)):
            for half in range(2):
                at = pl.ds(CHUNK * (2 * index + half), CHUNK)
                out_ref[part, at, :] = value[rows, 128 * half : 128 * (half + 1)]
        out_ref[part, pl.ds(4 * CHUNK, CHUNK), :] = pair


def slope_kernel(y_1, y0, p_1, p1, g0, total_ref):
    grad = slope(y0[...], p1[...], y_1[...], p_1[...])
    g0[...] = grad
    total_ref[...] = jnp.broadcast_to(squares(grad)[None], total_ref.shape)


def step_size(total_ref):
    part = jnp.sum(total_ref[...], axis=0)
    total = jnp.sum(jnp.sum(part, axis=1, keepdims=True), axis=0, keepdims=True)
    return TAU_STEP / jnp.sqrt(total / (2 * NK * NB * NPW) + EPS_NORM)


def advance_kernel(flags, total, y_2, y_1, p_2, p_1, p0, p1, closing, g0, g1, q_1, q0, q1, far):
    size = step_size(total)
    q0[...] = (p0[...].astype(F32) + size * g0[...]).astype(BF16)
    q1[...] = (p1[...].astype(F32) + size * g1[...].astype(F32)).astype(BF16)
    choose(flags[1], closing, p_2, far)
    grad = slope(y_1[...], p0[...], y_2[...], far[...])
    q_1[...] = (p_1[...].astype(F32) + size * grad).astype(BF16)


def finish_kernel(total_ref, p0, g0, re_ref, im_ref):
    size = step_size(total_ref)
    value = (p0[...].astype(F32) + size * g0[...]).astype(BF16)
    re_ref[...] = value[:NB]
    im_ref[...] = value[NB:]


def shifted(value, by):
    return lax.ppermute(value, "kstr", [(i, (i + by) % NK) for i in range(NK)])


def exchange(value, axis):
    return lax.all_to_all(value, axis, 0, 0, tiled=True)


def whole_total(part):
    parts = exchange(part, "pw")
    own = call(spread_kernel, shape((NK, 8, 128), F32), parts)
    return exchange(own, "kstr")


def inverse(whole):
    return call(newton_kernel, shape((NB, 2 * NB), BF16), whole)


def body(states_re, states_im, gmap):
    width = states_re.shape[2]
    row = lax.axis_index("kstr")
    offset = jnp.mod(gmap[0] - lax.axis_index("pw") * width, NPW)
    blocks = offset // width
    rest = offset - blocks * width
    first = row < NK // 2
    bounds = jnp.stack(
        [
            jnp.where(first, rest, 0),
            jnp.where(first, width, width - rest),
            jnp.where(first, jnp.mod(width - rest, width), rest),
        ]
    ).astype(jnp.int32)
    state = jnp.concatenate([states_re[0], states_im[0]], 0)
    full = 2 * NB
    end = NK - 1
    duals = shape((NB, full), BF16)
    fields = shape((full, width), BF16)
    grads = shape((full, width), F32)
    chunk = shape((CHUNK, NB), F32)
    chunks = shape((PARTS, CHUNK, NB), BF16)
    far_scratch = (pltpu.VMEM((full, width), BF16),)
    flags = jnp.stack([row == 0, row <= 1, row >= NK - 2, row == end]).astype(jnp.int32)

    beside = lax.ppermute(state, ("kstr", "pw"), beside_pairs())
    p1, p_2 = shifted(state, -1), shifted(state, 2)
    p2 = shifted(state, -2)
    merged = call(merge_kernel, fields, bounds, state, beside, smem=1)
    near = close_string(merged, blocks)
    near, p1, p2, p_2 = lax.optimization_barrier((near, p1, p2, p_2))

    part, p1 = call(first_margin_kernel, (shape((full, NB), BF16), fields), flags, state, p1, near, smem=1)
    state, near, part = lax.optimization_barrier((state, near, part))
    p_1 = shifted(state, 1)
    parts = exchange(part, "pw").reshape(PARTS, CHUNK, NB)
    own, kept = call(collect_kernel, (chunks, chunk), parts)
    own, near = lax.optimization_barrier((own, near))
    far = lax.ppermute(near, "kstr", [(0, 1), (1, 0), (end - 1, end), (end, end - 1)])
    whole = exchange(own.reshape(full, NB), "pw")
    whole, p_1 = lax.optimization_barrier((whole, p_1))

    y0, far = lax.optimization_barrier((inverse(whole), far))
    y_1 = shifted(y0, 1)
    y1 = shifted(y0, -1)
    g0, g1, p_1, part = call(
        orders_kernel,
        (grads, fields, fields, shape((PARTS, 5 * CHUNK, 128), BF16)),
        *(flags, y_1, y0, y1, p_1, state, p1, p2, near, far),
        smem=1,
        scratch=far_scratch,
    )
    y0, part = lax.optimization_barrier((y0, part))
    y_2 = shifted(y0, 2)
    parts = exchange(part, "pw")
    first, second, total = call(
        collect_orders_kernel, (chunk, chunk, shape((NK, 8, 128), F32)), parts
    )
    total = exchange(total, "kstr")
    own = call(combine_kernel, chunks, total, kept, first, second)
    whole = exchange(own.reshape(full, NB), "pw")
    q_1, q0, q1 = call(
        advance_kernel,
        (fields, fields, fields),
        *(flags, total, y_2, y_1, p_2, p_1, state, p1, far, g0, g1),
        smem=1,
        scratch=far_scratch,
    )

    y0 = inverse(whole)
    y_1 = shifted(y0, 1)
    g0, total = call(slope_kernel, (grads, shape((PARTS, 8, 128), F32)), y_1, y0, q_1, q1)
    total = whole_total(total)
    half = shape((NB, width), BF16)
    new_re, new_im = call(finish_kernel, (half, half), total, q0, g0)
    return new_re[None], new_im[None]


def solution(mesh):
    placed = (P("kstr", None, "pw"), P("kstr", None, "pw"), P("pw"))
    return jax.shard_map(
        body,
        mesh=mesh,
        in_specs=placed,
        out_specs=(P("kstr", None, "pw"), P("kstr", None, "pw")),
        check_vma=False,
    )
```

```python
import jax
import jax.numpy as jnp
from jax import lax
from jax.experimental import pallas as pl
from jax.experimental.pallas import tpu as pltpu
from jax.sharding import PartitionSpec as P

NEWTON = 4
NK = 16
NPW = 16384
NB = 256
PARTS = 32
CHUNK = 2 * NB // PARTS
EPS_SCALE = 1e-06
EPS_NORM = 1e-06
TAU_STEP = 0.25
F32 = jnp.float32
BF16 = jnp.bfloat16


def call(kernel, outs, *args, smem=0, flops=0, scratch=()):
    specs = [pl.BlockSpec(memory_space=pltpu.SMEM)] * smem
    specs += [pl.BlockSpec(memory_space=pltpu.VMEM)] * (len(args) - smem)
    single = not isinstance(outs, (tuple, list))
    outs = (outs,) if single else tuple(outs)
    moved = sum(a.size * a.dtype.itemsize for a in args) + sum(
        o.size * o.dtype.itemsize for o in outs
    )
    result = pl.pallas_call(
        kernel,
        out_shape=outs,
        in_specs=specs,
        out_specs=tuple(pl.BlockSpec(memory_space=pltpu.VMEM) for _ in outs),
        scratch_shapes=list(scratch),
        compiler_params=pltpu.CompilerParams(vmem_limit_bytes=14 * 1024 * 1024),
        cost_estimate=pl.CostEstimate(flops=flops, bytes_accessed=moved, transcendentals=0),
    )(*args)
    return result[0] if single else result


def shape(dims, dtype):
    return jax.ShapeDtypeStruct(dims, dtype)


def dot(left, right):
    return jnp.dot(left, right, preferred_element_type=F32)


def margin(left, right):
    every = lax.dot_general(left, right, (((1,), (1,)), ((), ())), preferred_element_type=F32)
    real = every[:NB, :NB] + every[NB:, NB:]
    return jnp.concatenate([real, every[:NB, NB:] - every[NB:, :NB]], 0)


def choose(flag, yes_ref, no_ref, out_ref):
    @pl.when(flag == 1)
    def _():
        out_ref[...] = yes_ref[...]

    @pl.when(flag != 1)
    def _():
        out_ref[...] = no_ref[...]


def margin_kernel(state_ref, next_ref, out_ref):
    out_ref[...] = margin(state_ref[...], next_ref[...]).astype(BF16)


def first_margin_kernel(flags, state_ref, next_ref, closing_ref, out_ref, chosen_ref):
    choose(flags[3], closing_ref, next_ref, chosen_ref)
    margin_kernel(state_ref, chosen_ref, out_ref)


def merge_kernel(bounds, state_ref, beside_ref, out_ref):
    lane = lax.broadcasted_iota(jnp.int32, (CHUNK, state_ref.shape[1]), 1)
    own = (lane >= bounds[0]) & (lane < bounds[1])
    for row in range(0, state_ref.shape[0], CHUNK):
        rows = pl.ds(row, CHUNK)
        value = jnp.where(own, state_ref[rows, :].astype(F32), beside_ref[rows, :].astype(F32))
        out_ref[rows, :] = pltpu.roll(value, bounds[2], 1).astype(BF16)


def place(row, column):
    return row * PARTS + column % PARTS


def beside_pairs():
    pairs = []
    for j in range(PARTS):
        pairs += [(place(row, j), place(row, j - 1)) for row in (0, 1)]
        pairs += [(place(row, j), place(row, j + 1)) for row in (NK - 2, NK - 1)]
    return pairs


def closing_pairs(by):
    pairs = []
    for j in range(PARTS):
        for row in (0, 1):
            pairs.append((place(row, j), place(NK - 1 - row, j - by)))
            pairs.append((place(NK - 1 - row, j), place(row, j + by)))
    if by % 8 == 0:
        for row in range(2, NK - 2):
            pairs += [(place(row, j), place(row, j)) for j in range(PARTS)]
    return pairs


def close_string(value, blocks):
    def branch(by):
        return lambda block: lax.ppermute(block, ("kstr", "pw"), closing_pairs(by))

    return lax.switch(blocks, [branch(by) for by in range(PARTS)], value)


def collect_kernel(parts_ref, out_ref, kept_ref):
    total = jnp.sum(parts_ref[...].astype(F32), axis=0) * (1.0 / NPW)
    kept_ref[...] = total
    out_ref[...] = jnp.broadcast_to(total.astype(BF16)[None], out_ref.shape)


def collect_orders_kernel(parts_ref, first_ref, second_ref, squares_ref):
    total = jnp.sum(parts_ref[...].astype(F32), axis=0)
    for half in range(2):
        lanes = pl.ds(128 * half, 128)
        first_ref[:, lanes] = total[CHUNK * half : CHUNK * (half + 1)] * (1.0 / NPW)
        second_ref[:, lanes] = total[CHUNK * (2 + half) : CHUNK * (3 + half)] * (1.0 / NPW)
    part = total[4 * CHUNK : 4 * CHUNK + 8] + total[4 * CHUNK + 8 :]
    squares_ref[...] = jnp.broadcast_to(part[None], squares_ref.shape)


def combine_kernel(total_ref, kept_ref, first_ref, second_ref, out_ref):
    size = step_size(total_ref)
    value = kept_ref[...] + size * (first_ref[...] + size * second_ref[...])
    out_ref[...] = jnp.broadcast_to(value.astype(BF16)[None], out_ref.shape)


def spread_kernel(parts_ref, out_ref):
    total = jnp.sum(parts_ref[...], axis=0)
    out_ref[...] = jnp.broadcast_to(total[None], out_ref.shape)


def pieces(value, count):
    high = value.astype(BF16)
    if count == 1:
        return [high]
    return [high, (value - high.astype(F32)).astype(BF16)]


def newton_kernel(margin_ref, out_ref):
    stacked = margin_ref[...]
    whole = stacked.astype(F32)
    real, imag = whole[:NB], whole[NB:]
    magnitude = jnp.sqrt(real * real + imag * imag)
    colmax = jnp.max(jnp.sum(magnitude, axis=0, keepdims=True), axis=1, keepdims=True)
    rowmax = jnp.max(jnp.sum(magnitude, axis=1, keepdims=True), axis=0, keepdims=True)
    factor = 1.0 / (colmax * rowmax + EPS_SCALE)
    iterate = jnp.concatenate([real * factor, imag * factor], 1)

    for turn in range(NEWTON):
        terms = 1 if turn < NEWTON // 2 else 2
        parts = pieces(iterate, terms)
        product = None
        for part in parts:
            crossed = jnp.concatenate([part[:, NB:], -part[:, :NB]], 1)
            right = jnp.concatenate([part, crossed], 0)
            term = lax.dot_general(
                stacked, right, (((0,), (0,)), ((), ())), preferred_element_type=F32
            )
            product = term if product is None else product + term
        seconds = pieces(product, terms)
        change = None
        for j, second in enumerate(seconds):
            crossed = jnp.concatenate([-second[:, NB:], second[:, :NB]], 1)
            right = jnp.concatenate([second, crossed], 0)
            for i, part in enumerate(parts):
                if i + j < terms:
                    term = dot(part, right)
                    change = term if change is None else change + term
        iterate = 2.0 * iterate - change
    out_ref[...] = iterate.astype(BF16)


def slope(dual, following, dual_before, before):
    real, imag = dual[:, :NB], dual[:, NB:]
    forward = jnp.concatenate(
        [jnp.concatenate([-imag, real], 1), jnp.concatenate([-real, -imag], 1)], 0
    )
    real, imag = dual_before[:, :NB], dual_before[:, NB:]
    backward = jnp.concatenate(
        [jnp.concatenate([imag, real], 1), jnp.concatenate([-real, imag], 1)], 0
    )
    return dot(forward, following) - dot(backward, before).astype(BF16).astype(F32)


def squares(grad):
    part = grad[0:8]
    part = part * part
    for row in range(8, grad.shape[0], 8):
        more = grad[row : row + 8]
        part = part + more * more
    return part[:, 0:128] + part[:, 128:256] + part[:, 256:384] + part[:, 384:512]


def orders_kernel(
    flags, y_1, y0, y1, before, p0, p1, p2, closing, beyond, g0, g1, p_1, out_ref, far
):
    choose(flags[0], closing, before, p_1)
    grad = slope(y0[...], p1[...], y_1[...], p_1[...])
    g0[...] = grad
    part = squares(grad)
    high = part.astype(BF16).astype(F32)
    pair = jnp.concatenate([high, part - high], 0).astype(BF16)
    here = grad.astype(BF16)
    choose(flags[2], beyond, p2, far)
    ahead = slope(y1[...], far[...], y0[...], p0[...]).astype(BF16)
    g1[...] = ahead
    first = (margin(here, p1[...]) + margin(p0[...], ahead)).astype(BF16)
    second = margin(here, ahead).astype(BF16)
    for part in range(PARTS):
        rows = slice(CHUNK * part, CHUNK * (part + 1))
        for index, value in enumerate((first, second)):
            for half in range(2):
                at = pl.ds(CHUNK * (2 * index + half), CHUNK)
                out_ref[part, at, :] = value[rows, 128 * half : 128 * (half + 1)]
        out_ref[part, pl.ds(4 * CHUNK, CHUNK), :] = pair


def slope_kernel(y_1, y0, p_1, p1, g0, total_ref):
    grad = slope(y0[...], p1[...], y_1[...], p_1[...])
    g0[...] = grad
    total_ref[...] = jnp.broadcast_to(squares(grad)[None], total_ref.shape)


def step_size(total_ref):
    part = jnp.sum(total_ref[...], axis=0)
    total = jnp.sum(jnp.sum(part, axis=1, keepdims=True), axis=0, keepdims=True)
    return TAU_STEP / jnp.sqrt(total / (2 * NK * NB * NPW) + EPS_NORM)


def advance_kernel(flags, total, y_2, y_1, p_2, p_1, p0, p1, closing, g0, g1, q_1, q0, q1, far):
    size = step_size(total)
    q0[...] = (p0[...].astype(F32) + size * g0[...]).astype(BF16)
    q1[...] = (p1[...].astype(F32) + size * g1[...].astype(F32)).astype(BF16)
    choose(flags[1], closing, p_2, far)
    grad = slope(y_1[...], p0[...], y_2[...], far[...])
    q_1[...] = (p_1[...].astype(F32) + size * grad).astype(BF16)


def finish_kernel(total_ref, p0, g0, re_ref, im_ref):
    size = step_size(total_ref)
    value = (p0[...].astype(F32) + size * g0[...]).astype(BF16)
    re_ref[...] = value[:NB]
    im_ref[...] = value[NB:]


def shifted(value, by):
    return lax.ppermute(value, "kstr", [(i, (i + by) % NK) for i in range(NK)])


def exchange(value, axis):
    return lax.all_to_all(value, axis, 0, 0, tiled=True)


def whole_total(part):
    parts = exchange(part, "pw")
    own = call(spread_kernel, shape((NK, 8, 128), F32), parts)
    return exchange(own, "kstr")


def inverse(whole):
    return call(newton_kernel, shape((NB, 2 * NB), BF16), whole)


def body(states_re, states_im, gmap):
    width = states_re.shape[2]
    row = lax.axis_index("kstr")
    offset = jnp.mod(gmap[0] - lax.axis_index("pw") * width, NPW)
    blocks = offset // width
    rest = offset - blocks * width
    first = row < NK // 2
    bounds = jnp.stack(
        [
            jnp.where(first, rest, 0),
            jnp.where(first, width, width - rest),
            jnp.where(first, jnp.mod(width - rest, width), rest),
        ]
    ).astype(jnp.int32)
    state = jnp.concatenate([states_re[0], states_im[0]], 0)
    full = 2 * NB
    end = NK - 1
    duals = shape((NB, full), BF16)
    fields = shape((full, width), BF16)
    grads = shape((full, width), F32)
    chunk = shape((CHUNK, NB), F32)
    chunks = shape((PARTS, CHUNK, NB), BF16)
    far_scratch = (pltpu.VMEM((full, width), BF16),)
    flags = jnp.stack([row == 0, row <= 1, row >= NK - 2, row == end]).astype(jnp.int32)

    beside = lax.ppermute(state, ("kstr", "pw"), beside_pairs())
    p1, p_2 = shifted(state, -1), shifted(state, 2)
    p2 = lax.ppermute(state, "kstr", [(i + 2, i) for i in range(NK - 2)])
    merged = call(merge_kernel, fields, bounds, state, beside, smem=1)
    near = close_string(merged, blocks)
    near, p1, p2, p_2 = lax.optimization_barrier((near, p1, p2, p_2))

    part, p1 = call(first_margin_kernel, (shape((full, NB), BF16), fields), flags, state, p1, near, smem=1)
    state, near, part = lax.optimization_barrier((state, near, part))
    p_1 = shifted(state, 1)
    parts = exchange(part, "pw").reshape(PARTS, CHUNK, NB)
    own, kept = call(collect_kernel, (chunks, chunk), parts)
    own, near = lax.optimization_barrier((own, near))
    far = lax.ppermute(near, "kstr", [(0, 1), (1, 0), (end - 1, end), (end, end - 1)])
    whole = exchange(own.reshape(full, NB), "pw")
    whole, p_1 = lax.optimization_barrier((whole, p_1))

    y0, far = lax.optimization_barrier((inverse(whole), far))
    y_1 = shifted(y0, 1)
    y1 = shifted(y0, -1)
    g0, g1, p_1, part = call(
        orders_kernel,
        (grads, fields, fields, shape((PARTS, 5 * CHUNK, 128), BF16)),
        *(flags, y_1, y0, y1, p_1, state, p1, p2, near, far),
        smem=1,
        scratch=far_scratch,
    )
    y0, part = lax.optimization_barrier((y0, part))
    y_2 = shifted(y0, 2)
    parts = exchange(part, "pw")
    first, second, total = call(
        collect_orders_kernel, (chunk, chunk, shape((NK, 8, 128), F32)), parts
    )
    total = exchange(total, "kstr")
    own = call(combine_kernel, chunks, total, kept, first, second)
    whole = exchange(own.reshape(full, NB), "pw")
    q_1, q0, q1 = call(
        advance_kernel,
        (fields, fields, fields),
        *(flags, total, y_2, y_1, p_2, p_1, state, p1, far, g0, g1),
        smem=1,
        scratch=far_scratch,
    )

    y0 = inverse(whole)
    y_1 = shifted(y0, 1)
    g0, total = call(slope_kernel, (grads, shape((PARTS, 8, 128), F32)), y_1, y0, q_1, q1)
    total = whole_total(total)
    half = shape((NB, width), BF16)
    new_re, new_im = call(finish_kernel, (half, half), total, q0, g0)
    return new_re[None], new_im[None]


def solution(mesh):
    placed = (P("kstr", None, "pw"), P("kstr", None, "pw"), P("pw"))
    return jax.shard_map(
        body,
        mesh=mesh,
        in_specs=placed,
        out_specs=(P("kstr", None, "pw"), P("kstr", None, "pw")),
        check_vma=False,
    )
```

```python
import jax
import jax.numpy as jnp
from jax import lax
from jax.experimental import pallas as pl
from jax.experimental.pallas import tpu as pltpu
from jax.sharding import PartitionSpec as P

NEWTON = 4
NK = 16
NPW = 16384
NB = 256
PARTS = 32
CHUNK = 2 * NB // PARTS
EPS_SCALE = 1e-06
EPS_NORM = 1e-06
TAU_STEP = 0.25
F32 = jnp.float32
BF16 = jnp.bfloat16


def call(kernel, outs, *args, smem=0, flops=0, scratch=()):
    specs = [pl.BlockSpec(memory_space=pltpu.SMEM)] * smem
    specs += [pl.BlockSpec(memory_space=pltpu.VMEM)] * (len(args) - smem)
    single = not isinstance(outs, (tuple, list))
    outs = (outs,) if single else tuple(outs)
    moved = sum(a.size * a.dtype.itemsize for a in args) + sum(
        o.size * o.dtype.itemsize for o in outs
    )
    result = pl.pallas_call(
        kernel,
        out_shape=outs,
        in_specs=specs,
        out_specs=tuple(pl.BlockSpec(memory_space=pltpu.VMEM) for _ in outs),
        scratch_shapes=list(scratch),
        compiler_params=pltpu.CompilerParams(vmem_limit_bytes=14 * 1024 * 1024),
        cost_estimate=pl.CostEstimate(flops=flops, bytes_accessed=moved, transcendentals=0),
    )(*args)
    return result[0] if single else result


def shape(dims, dtype):
    return jax.ShapeDtypeStruct(dims, dtype)


def dot(left, right):
    return jnp.dot(left, right, preferred_element_type=F32)


def margin(left, right):
    every = lax.dot_general(left, right, (((1,), (1,)), ((), ())), preferred_element_type=F32)
    real = every[:NB, :NB] + every[NB:, NB:]
    return jnp.concatenate([real, every[:NB, NB:] - every[NB:, :NB]], 0)


def choose(flag, yes_ref, no_ref, out_ref):
    @pl.when(flag == 1)
    def _():
        out_ref[...] = yes_ref[...]

    @pl.when(flag != 1)
    def _():
        out_ref[...] = no_ref[...]


def margin_kernel(state_ref, next_ref, out_ref):
    out_ref[...] = margin(state_ref[...], next_ref[...]).astype(BF16)


def first_margin_kernel(flags, state_ref, next_ref, closing_ref, out_ref, chosen_ref):
    choose(flags[3], closing_ref, next_ref, chosen_ref)
    margin_kernel(state_ref, chosen_ref, out_ref)


def merge_kernel(bounds, state_ref, beside_ref, out_ref):
    lane = lax.broadcasted_iota(jnp.int32, (CHUNK, state_ref.shape[1]), 1)
    own = (lane >= bounds[0]) & (lane < bounds[1])
    for row in range(0, state_ref.shape[0], CHUNK):
        rows = pl.ds(row, CHUNK)
        value = jnp.where(own, state_ref[rows, :].astype(F32), beside_ref[rows, :].astype(F32))
        out_ref[rows, :] = pltpu.roll(value, bounds[2], 1).astype(BF16)


def place(row, column):
    return row * PARTS + column % PARTS


def beside_pairs():
    pairs = []
    for j in range(PARTS):
        pairs += [(place(row, j), place(row, j - 1)) for row in (0, 1)]
        pairs += [(place(row, j), place(row, j + 1)) for row in (NK - 2, NK - 1)]
    return pairs


def closing_pairs(by):
    pairs = []
    for j in range(PARTS):
        for row in (0, 1):
            pairs.append((place(row, j), place(NK - 1 - row, j - by)))
            pairs.append((place(NK - 1 - row, j), place(row, j + by)))
    if by % 8 == 0:
        for row in range(2, NK - 2):
            pairs += [(place(row, j), place(row, j)) for j in range(PARTS)]
    return pairs


def close_string(value, blocks):
    def branch(by):
        return lambda block: lax.ppermute(block, ("kstr", "pw"), closing_pairs(by))

    return lax.switch(blocks, [branch(by) for by in range(PARTS)], value)


def collect_kernel(parts_ref, out_ref, kept_ref):
    total = jnp.sum(parts_ref[...].astype(F32), axis=0) * (1.0 / NPW)
    kept_ref[...] = total
    out_ref[...] = jnp.broadcast_to(total.astype(BF16)[None], out_ref.shape)


def collect_orders_kernel(parts_ref, first_ref, second_ref, squares_ref):
    total = jnp.sum(parts_ref[...].astype(F32), axis=0)
    for half in range(2):
        lanes = pl.ds(128 * half, 128)
        first_ref[:, lanes] = total[CHUNK * half : CHUNK * (half + 1)] * (1.0 / NPW)
        second_ref[:, lanes] = total[CHUNK * (2 + half) : CHUNK * (3 + half)] * (1.0 / NPW)
    part = total[4 * CHUNK : 4 * CHUNK + 8] + total[4 * CHUNK + 8 :]
    squares_ref[...] = jnp.broadcast_to(part[None], squares_ref.shape)


def combine_kernel(total_ref, kept_ref, first_ref, second_ref, out_ref):
    size = step_size(total_ref)
    value = kept_ref[...] + size * (first_ref[...] + size * second_ref[...])
    out_ref[...] = jnp.broadcast_to(value.astype(BF16)[None], out_ref.shape)


def spread_kernel(parts_ref, out_ref):
    total = jnp.sum(parts_ref[...], axis=0)
    out_ref[...] = jnp.broadcast_to(total[None], out_ref.shape)


def pieces(value, count):
    high = value.astype(BF16)
    if count == 1:
        return [high]
    return [high, (value - high.astype(F32)).astype(BF16)]


def newton_kernel(margin_ref, out_ref):
    stacked = margin_ref[...]
    whole = stacked.astype(F32)
    real, imag = whole[:NB], whole[NB:]
    magnitude = jnp.sqrt(real * real + imag * imag)
    colmax = jnp.max(jnp.sum(magnitude, axis=0, keepdims=True), axis=1, keepdims=True)
    rowmax = jnp.max(jnp.sum(magnitude, axis=1, keepdims=True), axis=0, keepdims=True)
    factor = 1.0 / (colmax * rowmax + EPS_SCALE)
    iterate = jnp.concatenate([real * factor, imag * factor], 1)

    for turn in range(NEWTON):
        terms = 1 if turn < NEWTON // 2 else 2
        parts = pieces(iterate, terms)
        product = None
        for part in parts:
            crossed = jnp.concatenate([part[:, NB:], -part[:, :NB]], 1)
            right = jnp.concatenate([part, crossed], 0)
            term = lax.dot_general(
                stacked, right, (((0,), (0,)), ((), ())), preferred_element_type=F32
            )
            product = term if product is None else product + term
        seconds = pieces(product, terms)
        change = None
        for j, second in enumerate(seconds):
            crossed = jnp.concatenate([-second[:, NB:], second[:, :NB]], 1)
            right = jnp.concatenate([second, crossed], 0)
            for i, part in enumerate(parts):
                if i + j < terms:
                    term = dot(part, right)
                    change = term if change is None else change + term
        iterate = 2.0 * iterate - change
    out_ref[...] = iterate.astype(BF16)


def slope(dual, following, dual_before, before):
    real, imag = dual[:, :NB], dual[:, NB:]
    forward = jnp.concatenate(
        [jnp.concatenate([-imag, real], 1), jnp.concatenate([-real, -imag], 1)], 0
    )
    real, imag = dual_before[:, :NB], dual_before[:, NB:]
    backward = jnp.concatenate(
        [jnp.concatenate([imag, real], 1), jnp.concatenate([-real, imag], 1)], 0
    )
    return dot(forward, following) - dot(backward, before).astype(BF16).astype(F32)


def squares(grad):
    part = grad[0:8]
    part = part * part
    for row in range(8, grad.shape[0], 8):
        more = grad[row : row + 8]
        part = part + more * more
    return part[:, 0:128] + part[:, 128:256] + part[:, 256:384] + part[:, 384:512]


def orders_kernel(
    flags, y_1, y0, y1, before, p0, p1, p2, closing, beyond, g0, g1, p_1, out_ref, far
):
    choose(flags[0], closing, before, p_1)
    grad = slope(y0[...], p1[...], y_1[...], p_1[...])
    g0[...] = grad
    part = squares(grad)
    high = part.astype(BF16).astype(F32)
    pair = jnp.concatenate([high, part - high], 0).astype(BF16)
    here = grad.astype(BF16)
    choose(flags[2], beyond, p2, far)
    ahead = slope(y1[...], far[...], y0[...], p0[...]).astype(BF16)
    g1[...] = ahead
    first = (margin(here, p1[...]) + margin(p0[...], ahead)).astype(BF16)
    second = margin(here, ahead).astype(BF16)
    for part in range(PARTS):
        rows = slice(CHUNK * part, CHUNK * (part + 1))
        for index, value in enumerate((first, second)):
            for half in range(2):
                at = pl.ds(CHUNK * (2 * index + half), CHUNK)
                out_ref[part, at, :] = value[rows, 128 * half : 128 * (half + 1)]
        out_ref[part, pl.ds(4 * CHUNK, CHUNK), :] = pair


def slope_kernel(y_1, y0, p_1, p1, g0, total_ref):
    grad = slope(y0[...], p1[...], y_1[...], p_1[...])
    g0[...] = grad
    total_ref[...] = jnp.broadcast_to(squares(grad)[None], total_ref.shape)


def step_size(total_ref):
    part = jnp.sum(total_ref[...], axis=0)
    total = jnp.sum(jnp.sum(part, axis=1, keepdims=True), axis=0, keepdims=True)
    return TAU_STEP / jnp.sqrt(total / (2 * NK * NB * NPW) + EPS_NORM)


def advance_kernel(flags, total, y_2, y_1, p_2, p_1, p0, p1, closing, g0, g1, q_1, q0, q1, far):
    size = step_size(total)
    q0[...] = (p0[...].astype(F32) + size * g0[...]).astype(BF16)
    q1[...] = (p1[...].astype(F32) + size * g1[...].astype(F32)).astype(BF16)
    choose(flags[1], closing, p_2, far)
    grad = slope(y_1[...], p0[...], y_2[...], far[...])
    q_1[...] = (p_1[...].astype(F32) + size * grad).astype(BF16)


def finish_kernel(total_ref, p0, g0, re_ref, im_ref):
    size = step_size(total_ref)
    value = (p0[...].astype(F32) + size * g0[...]).astype(BF16)
    re_ref[...] = value[:NB]
    im_ref[...] = value[NB:]


def shifted(value, by):
    return lax.ppermute(value, "kstr", [(i, (i + by) % NK) for i in range(NK)])


def exchange(value, axis):
    return lax.all_to_all(value, axis, 0, 0, tiled=True)


def whole_total(part):
    parts = exchange(part, "pw")
    own = call(spread_kernel, shape((NK, 8, 128), F32), parts)
    return exchange(own, "kstr")


def inverse(whole):
    return call(newton_kernel, shape((NB, 2 * NB), BF16), whole)


def body(states_re, states_im, gmap):
    width = states_re.shape[2]
    row = lax.axis_index("kstr")
    offset = jnp.mod(gmap[0] - lax.axis_index("pw") * width, NPW)
    blocks = offset // width
    rest = offset - blocks * width
    first = row < NK // 2
    bounds = jnp.stack(
        [
            jnp.where(first, rest, 0),
            jnp.where(first, width, width - rest),
            jnp.where(first, jnp.mod(width - rest, width), rest),
        ]
    ).astype(jnp.int32)
    state = jnp.concatenate([states_re[0], states_im[0]], 0)
    full = 2 * NB
    end = NK - 1
    duals = shape((NB, full), BF16)
    fields = shape((full, width), BF16)
    grads = shape((full, width), F32)
    chunk = shape((CHUNK, NB), F32)
    chunks = shape((PARTS, CHUNK, NB), BF16)
    far_scratch = (pltpu.VMEM((full, width), BF16),)
    flags = jnp.stack([row == 0, row <= 1, row >= NK - 2, row == end]).astype(jnp.int32)

    beside = lax.ppermute(state, ("kstr", "pw"), beside_pairs())
    p1, p_2 = shifted(state, -1), shifted(state, 2)
    p2 = lax.ppermute(state, "kstr", [(i + 2, i) for i in range(NK - 2)])
    merged = call(merge_kernel, fields, bounds, state, beside, smem=1)
    near = close_string(merged, blocks)
    near, p1, p2, p_2 = lax.optimization_barrier((near, p1, p2, p_2))

    part, p1 = call(first_margin_kernel, (shape((full, NB), BF16), fields), flags, state, p1, near, smem=1)
    state, near, part = lax.optimization_barrier((state, near, part))
    p_1 = shifted(state, 1)
    far = lax.ppermute(near, "kstr", [(0, 1), (1, 0), (end - 1, end), (end, end - 1)])
    parts = exchange(part, "pw").reshape(PARTS, CHUNK, NB)
    own, kept = call(collect_kernel, (chunks, chunk), parts)
    whole = exchange(own.reshape(full, NB), "pw")
    whole, far, p_1 = lax.optimization_barrier((whole, far, p_1))

    y0 = inverse(whole)
    y_1 = shifted(y0, 1)
    y1 = shifted(y0, -1)
    g0, g1, p_1, part = call(
        orders_kernel,
        (grads, fields, fields, shape((PARTS, 5 * CHUNK, 128), BF16)),
        *(flags, y_1, y0, y1, p_1, state, p1, p2, near, far),
        smem=1,
        scratch=far_scratch,
    )
    y0, part = lax.optimization_barrier((y0, part))
    y_2 = shifted(y0, 2)
    parts = exchange(part, "pw")
    first, second, total = call(
        collect_orders_kernel, (chunk, chunk, shape((NK, 8, 128), F32)), parts
    )
    total = exchange(total, "kstr")
    own = call(combine_kernel, chunks, total, kept, first, second)
    whole = exchange(own.reshape(full, NB), "pw")
    q_1, q0, q1 = call(
        advance_kernel,
        (fields, fields, fields),
        *(flags, total, y_2, y_1, p_2, p_1, state, p1, far, g0, g1),
        smem=1,
        scratch=far_scratch,
    )

    y0 = inverse(whole)
    y_1 = shifted(y0, 1)
    g0, total = call(slope_kernel, (grads, shape((PARTS, 8, 128), F32)), y_1, y0, q_1, q1)
    total = whole_total(total)
    half = shape((NB, width), BF16)
    new_re, new_im = call(finish_kernel, (half, half), total, q0, g0)
    return new_re[None], new_im[None]


def solution(mesh):
    placed = (P("kstr", None, "pw"), P("kstr", None, "pw"), P("pw"))
    return jax.shard_map(
        body,
        mesh=mesh,
        in_specs=placed,
        out_specs=(P("kstr", None, "pw"), P("kstr", None, "pw")),
        check_vma=False,
    )
```

```python
import jax
import jax.numpy as jnp
from jax import lax
from jax.experimental import pallas as pl
from jax.experimental.pallas import tpu as pltpu
from jax.sharding import PartitionSpec as P

NEWTON = 4
NK = 16
NPW = 16384
NB = 256
PARTS = 32
CHUNK = 2 * NB // PARTS
EPS_SCALE = 1e-06
EPS_NORM = 1e-06
TAU_STEP = 0.25
F32 = jnp.float32
BF16 = jnp.bfloat16


def call(kernel, outs, *args, smem=0, flops=0, scratch=()):
    specs = [pl.BlockSpec(memory_space=pltpu.SMEM)] * smem
    specs += [pl.BlockSpec(memory_space=pltpu.VMEM)] * (len(args) - smem)
    single = not isinstance(outs, (tuple, list))
    outs = (outs,) if single else tuple(outs)
    moved = sum(a.size * a.dtype.itemsize for a in args) + sum(
        o.size * o.dtype.itemsize for o in outs
    )
    result = pl.pallas_call(
        kernel,
        out_shape=outs,
        in_specs=specs,
        out_specs=tuple(pl.BlockSpec(memory_space=pltpu.VMEM) for _ in outs),
        scratch_shapes=list(scratch),
        compiler_params=pltpu.CompilerParams(vmem_limit_bytes=14 * 1024 * 1024),
        cost_estimate=pl.CostEstimate(flops=flops, bytes_accessed=moved, transcendentals=0),
    )(*args)
    return result[0] if single else result


def shape(dims, dtype):
    return jax.ShapeDtypeStruct(dims, dtype)


def dot(left, right):
    return jnp.dot(left, right, preferred_element_type=F32)


def margin(left, right):
    every = lax.dot_general(left, right, (((1,), (1,)), ((), ())), preferred_element_type=F32)
    real = every[:NB, :NB] + every[NB:, NB:]
    return jnp.concatenate([real, every[:NB, NB:] - every[NB:, :NB]], 0)


def choose(flag, yes_ref, no_ref, out_ref):
    @pl.when(flag == 1)
    def _():
        out_ref[...] = yes_ref[...]

    @pl.when(flag != 1)
    def _():
        out_ref[...] = no_ref[...]


def margin_kernel(state_ref, next_ref, out_ref):
    out_ref[...] = margin(state_ref[...], next_ref[...]).astype(BF16)


def first_margin_kernel(flags, state_ref, next_ref, closing_ref, out_ref, chosen_ref):
    choose(flags[3], closing_ref, next_ref, chosen_ref)
    margin_kernel(state_ref, chosen_ref, out_ref)


def merge_kernel(bounds, state_ref, beside_ref, out_ref):
    lane = lax.broadcasted_iota(jnp.int32, (CHUNK, state_ref.shape[1]), 1)
    own = (lane >= bounds[0]) & (lane < bounds[1])
    for row in range(0, state_ref.shape[0], CHUNK):
        rows = pl.ds(row, CHUNK)
        value = jnp.where(own, state_ref[rows, :].astype(F32), beside_ref[rows, :].astype(F32))
        out_ref[rows, :] = pltpu.roll(value, bounds[2], 1).astype(BF16)


def place(row, column):
    return row * PARTS + column % PARTS


def beside_pairs():
    pairs = []
    for j in range(PARTS):
        pairs += [(place(row, j), place(row, j - 1)) for row in (0, 1)]
        pairs += [(place(row, j), place(row, j + 1)) for row in (NK - 2, NK - 1)]
    return pairs


def closing_pairs(by):
    pairs = []
    for j in range(PARTS):
        for row in (0, 1):
            pairs.append((place(row, j), place(NK - 1 - row, j - by)))
            pairs.append((place(NK - 1 - row, j), place(row, j + by)))
    if by % 8 == 0:
        for row in range(2, NK - 2):
            pairs += [(place(row, j), place(row, j)) for j in range(PARTS)]
    return pairs


def close_string(value, blocks):
    def branch(by):
        return lambda block: lax.ppermute(block, ("kstr", "pw"), closing_pairs(by))

    return lax.switch(blocks, [branch(by) for by in range(PARTS)], value)


def collect_kernel(parts_ref, out_ref, kept_ref):
    total = jnp.sum(parts_ref[...].astype(F32), axis=0) * (1.0 / NPW)
    kept_ref[...] = total
    out_ref[...] = jnp.broadcast_to(total.astype(BF16)[None], out_ref.shape)


def collect_orders_kernel(parts_ref, first_ref, second_ref, squares_ref):
    total = jnp.sum(parts_ref[...].astype(F32), axis=0)
    for half in range(2):
        lanes = pl.ds(128 * half, 128)
        first_ref[:, lanes] = total[CHUNK * half : CHUNK * (half + 1)] * (1.0 / NPW)
        second_ref[:, lanes] = total[CHUNK * (2 + half) : CHUNK * (3 + half)] * (1.0 / NPW)
    part = jnp.sum(total[4 * CHUNK :], axis=0, keepdims=True)
    squares_ref[...] = jnp.broadcast_to(part[None], squares_ref.shape)


def combine_kernel(total_ref, kept_ref, first_ref, second_ref, out_ref):
    size = step_size(total_ref)
    value = kept_ref[...] + size * (first_ref[...] + size * second_ref[...])
    out_ref[...] = jnp.broadcast_to(value.astype(BF16)[None], out_ref.shape)


def spread_kernel(parts_ref, out_ref):
    total = jnp.sum(parts_ref[...], axis=0)
    out_ref[...] = jnp.broadcast_to(total[None], out_ref.shape)


def pieces(value, count):
    high = value.astype(BF16)
    if count == 1:
        return [high]
    return [high, (value - high.astype(F32)).astype(BF16)]


def newton_kernel(margin_ref, out_ref):
    stacked = margin_ref[...]
    whole = stacked.astype(F32)
    real, imag = whole[:NB], whole[NB:]
    magnitude = jnp.sqrt(real * real + imag * imag)
    colmax = jnp.max(jnp.sum(magnitude, axis=0, keepdims=True), axis=1, keepdims=True)
    rowmax = jnp.max(jnp.sum(magnitude, axis=1, keepdims=True), axis=0, keepdims=True)
    factor = 1.0 / (colmax * rowmax + EPS_SCALE)
    iterate = jnp.concatenate([real * factor, imag * factor], 1)

    for turn in range(NEWTON):
        terms = 1 if turn < NEWTON // 2 else 2
        parts = pieces(iterate, terms)
        product = None
        for part in parts:
            crossed = jnp.concatenate([part[:, NB:], -part[:, :NB]], 1)
            right = jnp.concatenate([part, crossed], 0)
            term = lax.dot_general(
                stacked, right, (((0,), (0,)), ((), ())), preferred_element_type=F32
            )
            product = term if product is None else product + term
        seconds = pieces(product, terms)
        change = None
        for j, second in enumerate(seconds):
            crossed = jnp.concatenate([-second[:, NB:], second[:, :NB]], 1)
            right = jnp.concatenate([second, crossed], 0)
            for i, part in enumerate(parts):
                if i + j < terms:
                    term = dot(part, right)
                    change = term if change is None else change + term
        iterate = 2.0 * iterate - change
    out_ref[...] = iterate.astype(BF16)


def slope(dual, following, dual_before, before):
    real, imag = dual[:, :NB], dual[:, NB:]
    forward = jnp.concatenate(
        [jnp.concatenate([-imag, real], 1), jnp.concatenate([-real, -imag], 1)], 0
    )
    real, imag = dual_before[:, :NB], dual_before[:, NB:]
    backward = jnp.concatenate(
        [jnp.concatenate([imag, real], 1), jnp.concatenate([-real, imag], 1)], 0
    )
    return dot(forward, following) - dot(backward, before).astype(BF16).astype(F32)


def squares(grad):
    part = grad[0:8]
    part = part * part
    for row in range(8, grad.shape[0], 8):
        more = grad[row : row + 8]
        part = part + more * more
    return part[:, 0:128] + part[:, 128:256] + part[:, 256:384] + part[:, 384:512]


def orders_kernel(
    flags, y_1, y0, y1, before, p0, p1, p2, closing, beyond, g0, g1, p_1, out_ref, far
):
    choose(flags[0], closing, before, p_1)
    grad = slope(y0[...], p1[...], y_1[...], p_1[...])
    g0[...] = grad
    part = squares(grad)
    high = part.astype(BF16).astype(F32)
    pair = jnp.concatenate([high, part - high], 0).astype(BF16)
    here = grad.astype(BF16)
    choose(flags[2], beyond, p2, far)
    ahead = slope(y1[...], far[...], y0[...], p0[...]).astype(BF16)
    g1[...] = ahead
    first = (margin(here, p1[...]) + margin(p0[...], ahead)).astype(BF16)
    second = margin(here, ahead).astype(BF16)
    for part in range(PARTS):
        rows = slice(CHUNK * part, CHUNK * (part + 1))
        for index, value in enumerate((first, second)):
            for half in range(2):
                at = pl.ds(CHUNK * (2 * index + half), CHUNK)
                out_ref[part, at, :] = value[rows, 128 * half : 128 * (half + 1)]
        out_ref[part, pl.ds(4 * CHUNK, CHUNK), :] = pair


def slope_kernel(y_1, y0, p_1, p1, g0, total_ref):
    grad = slope(y0[...], p1[...], y_1[...], p_1[...])
    g0[...] = grad
    part = jnp.sum(squares(grad), axis=0, keepdims=True)
    total_ref[...] = jnp.broadcast_to(part[None], total_ref.shape)


def step_size(total_ref):
    part = jnp.sum(total_ref[...], axis=0)
    total = jnp.sum(jnp.sum(part, axis=1, keepdims=True), axis=0, keepdims=True)
    return TAU_STEP / jnp.sqrt(total / (2 * NK * NB * NPW) + EPS_NORM)


def advance_kernel(flags, total, y_2, y_1, p_2, p_1, p0, p1, closing, g0, g1, q_1, q0, q1, far):
    size = step_size(total)
    q0[...] = (p0[...].astype(F32) + size * g0[...]).astype(BF16)
    q1[...] = (p1[...].astype(F32) + size * g1[...].astype(F32)).astype(BF16)
    choose(flags[1], closing, p_2, far)
    grad = slope(y_1[...], p0[...], y_2[...], far[...])
    q_1[...] = (p_1[...].astype(F32) + size * grad).astype(BF16)


def finish_kernel(total_ref, p0, g0, re_ref, im_ref):
    size = step_size(total_ref)
    value = (p0[...].astype(F32) + size * g0[...]).astype(BF16)
    re_ref[...] = value[:NB]
    im_ref[...] = value[NB:]


def shifted(value, by):
    return lax.ppermute(value, "kstr", [(i, (i + by) % NK) for i in range(NK)])


def exchange(value, axis):
    return lax.all_to_all(value, axis, 0, 0, tiled=True)


def whole_total(part):
    parts = exchange(part, "pw")
    own = call(spread_kernel, shape((NK, 1, 128), F32), parts)
    return exchange(own, "kstr")


def inverse(whole):
    return call(newton_kernel, shape((NB, 2 * NB), BF16), whole)


def body(states_re, states_im, gmap):
    width = states_re.shape[2]
    row = lax.axis_index("kstr")
    offset = jnp.mod(gmap[0] - lax.axis_index("pw") * width, NPW)
    blocks = offset // width
    rest = offset - blocks * width
    first = row < NK // 2
    bounds = jnp.stack(
        [
            jnp.where(first, rest, 0),
            jnp.where(first, width, width - rest),
            jnp.where(first, jnp.mod(width - rest, width), rest),
        ]
    ).astype(jnp.int32)
    state = jnp.concatenate([states_re[0], states_im[0]], 0)
    full = 2 * NB
    end = NK - 1
    duals = shape((NB, full), BF16)
    fields = shape((full, width), BF16)
    grads = shape((full, width), F32)
    chunk = shape((CHUNK, NB), F32)
    chunks = shape((PARTS, CHUNK, NB), BF16)
    far_scratch = (pltpu.VMEM((full, width), BF16),)
    flags = jnp.stack([row == 0, row <= 1, row >= NK - 2, row == end]).astype(jnp.int32)

    beside = lax.ppermute(state, ("kstr", "pw"), beside_pairs())
    p1, p_2 = shifted(state, -1), shifted(state, 2)
    p2 = lax.ppermute(state, "kstr", [(i + 2, i) for i in range(NK - 2)])
    merged = call(merge_kernel, fields, bounds, state, beside, smem=1)
    near = close_string(merged, blocks)
    near, p1, p2, p_2 = lax.optimization_barrier((near, p1, p2, p_2))

    part, p1 = call(first_margin_kernel, (shape((full, NB), BF16), fields), flags, state, p1, near, smem=1)
    state, near, part = lax.optimization_barrier((state, near, part))
    p_1 = shifted(state, 1)
    far = lax.ppermute(near, "kstr", [(0, 1), (1, 0), (end - 1, end), (end, end - 1)])
    parts = exchange(part, "pw").reshape(PARTS, CHUNK, NB)
    own, kept = call(collect_kernel, (chunks, chunk), parts)
    whole = exchange(own.reshape(full, NB), "pw")
    whole, far, p_1 = lax.optimization_barrier((whole, far, p_1))

    y0 = inverse(whole)
    y_1 = shifted(y0, 1)
    y1 = shifted(y0, -1)
    g0, g1, p_1, part = call(
        orders_kernel,
        (grads, fields, fields, shape((PARTS, 5 * CHUNK, 128), BF16)),
        *(flags, y_1, y0, y1, p_1, state, p1, p2, near, far),
        smem=1,
        scratch=far_scratch,
    )
    y0, part = lax.optimization_barrier((y0, part))
    y_2 = shifted(y0, 2)
    parts = exchange(part, "pw")
    first, second, total = call(
        collect_orders_kernel, (chunk, chunk, shape((NK, 1, 128), F32)), parts
    )
    total = exchange(total, "kstr")
    own = call(combine_kernel, chunks, total, kept, first, second)
    whole = exchange(own.reshape(full, NB), "pw")
    q_1, q0, q1 = call(
        advance_kernel,
        (fields, fields, fields),
        *(flags, total, y_2, y_1, p_2, p_1, state, p1, far, g0, g1),
        smem=1,
        scratch=far_scratch,
    )

    y0 = inverse(whole)
    y_1 = shifted(y0, 1)
    g0, total = call(slope_kernel, (grads, shape((PARTS, 1, 128), F32)), y_1, y0, q_1, q1)
    total = whole_total(total)
    half = shape((NB, width), BF16)
    new_re, new_im = call(finish_kernel, (half, half), total, q0, g0)
    return new_re[None], new_im[None]


def solution(mesh):
    placed = (P("kstr", None, "pw"), P("kstr", None, "pw"), P("pw"))
    return jax.shard_map(
        body,
        mesh=mesh,
        in_specs=placed,
        out_specs=(P("kstr", None, "pw"), P("kstr", None, "pw")),
        check_vma=False,
    )
```

```python
import jax
import jax.numpy as jnp
from jax import lax
from jax.experimental import pallas as pl
from jax.experimental.pallas import tpu as pltpu
from jax.sharding import PartitionSpec as P

NEWTON = 4
NK = 16
NPW = 16384
NB = 256
PARTS = 32
CHUNK = 2 * NB // PARTS
EPS_SCALE = 1e-06
EPS_NORM = 1e-06
TAU_STEP = 0.25
F32 = jnp.float32
BF16 = jnp.bfloat16


def call(kernel, outs, *args, smem=0, flops=0, scratch=()):
    specs = [pl.BlockSpec(memory_space=pltpu.SMEM)] * smem
    specs += [pl.BlockSpec(memory_space=pltpu.VMEM)] * (len(args) - smem)
    single = not isinstance(outs, (tuple, list))
    outs = (outs,) if single else tuple(outs)
    moved = sum(a.size * a.dtype.itemsize for a in args) + sum(
        o.size * o.dtype.itemsize for o in outs
    )
    result = pl.pallas_call(
        kernel,
        out_shape=outs,
        in_specs=specs,
        out_specs=tuple(pl.BlockSpec(memory_space=pltpu.VMEM) for _ in outs),
        scratch_shapes=list(scratch),
        compiler_params=pltpu.CompilerParams(vmem_limit_bytes=14 * 1024 * 1024),
        cost_estimate=pl.CostEstimate(flops=flops, bytes_accessed=moved, transcendentals=0),
    )(*args)
    return result[0] if single else result


def shape(dims, dtype):
    return jax.ShapeDtypeStruct(dims, dtype)


def dot(left, right):
    return jnp.dot(left, right, preferred_element_type=F32)


def margin(left, right):
    every = lax.dot_general(left, right, (((1,), (1,)), ((), ())), preferred_element_type=F32)
    real = every[:NB, :NB] + every[NB:, NB:]
    return jnp.concatenate([real, every[:NB, NB:] - every[NB:, :NB]], 0)


def choose(flag, yes_ref, no_ref, out_ref):
    @pl.when(flag == 1)
    def _():
        out_ref[...] = yes_ref[...]

    @pl.when(flag != 1)
    def _():
        out_ref[...] = no_ref[...]


def margin_kernel(state_ref, next_ref, out_ref):
    out_ref[...] = margin(state_ref[...], next_ref[...]).astype(BF16)


def first_margin_kernel(flags, state_ref, next_ref, closing_ref, out_ref, chosen_ref):
    choose(flags[3], closing_ref, next_ref, chosen_ref)
    margin_kernel(state_ref, chosen_ref, out_ref)


def merge_kernel(bounds, state_ref, beside_ref, out_ref):
    lane = lax.broadcasted_iota(jnp.int32, (CHUNK, state_ref.shape[1]), 1)
    own = (lane >= bounds[0]) & (lane < bounds[1])
    for row in range(0, state_ref.shape[0], CHUNK):
        rows = pl.ds(row, CHUNK)
        value = jnp.where(own, state_ref[rows, :].astype(F32), beside_ref[rows, :].astype(F32))
        out_ref[rows, :] = pltpu.roll(value, bounds[2], 1).astype(BF16)


def place(row, column):
    return row * PARTS + column % PARTS


def beside_pairs():
    pairs = []
    for j in range(PARTS):
        pairs += [(place(row, j), place(row, j - 1)) for row in (0, 1)]
        pairs += [(place(row, j), place(row, j + 1)) for row in (NK - 2, NK - 1)]
    return pairs


def closing_pairs(by):
    pairs = []
    for j in range(PARTS):
        for row in (0, 1):
            pairs.append((place(row, j), place(NK - 1 - row, j - by)))
            pairs.append((place(NK - 1 - row, j), place(row, j + by)))
    for row in range(2, NK - 2):
        pairs += [(place(row, j), place(row, j)) for j in range(PARTS)]
    return pairs


def close_string(value, blocks):
    def branch(by):
        return lambda block: lax.ppermute(block, ("kstr", "pw"), closing_pairs(by))

    return lax.switch(blocks, [branch(by) for by in range(PARTS)], value)


def collect_kernel(parts_ref, out_ref, kept_ref):
    total = jnp.sum(parts_ref[...].astype(F32), axis=0) * (1.0 / NPW)
    kept_ref[...] = total
    out_ref[...] = jnp.broadcast_to(total.astype(BF16)[None], out_ref.shape)


def collect_orders_kernel(parts_ref, first_ref, second_ref, squares_ref):
    total = jnp.sum(parts_ref[...].astype(F32), axis=0)
    for half in range(2):
        lanes = pl.ds(128 * half, 128)
        first_ref[:, lanes] = total[CHUNK * half : CHUNK * (half + 1)] * (1.0 / NPW)
        second_ref[:, lanes] = total[CHUNK * (2 + half) : CHUNK * (3 + half)] * (1.0 / NPW)
    part = jnp.sum(total[4 * CHUNK :], axis=0, keepdims=True)
    squares_ref[...] = jnp.broadcast_to(part[None], squares_ref.shape)


def combine_kernel(total_ref, kept_ref, first_ref, second_ref, out_ref):
    size = step_size(total_ref)
    value = kept_ref[...] + size * (first_ref[...] + size * second_ref[...])
    out_ref[...] = jnp.broadcast_to(value.astype(BF16)[None], out_ref.shape)


def spread_kernel(parts_ref, out_ref):
    total = jnp.sum(parts_ref[...], axis=0)
    out_ref[...] = jnp.broadcast_to(total[None], out_ref.shape)


def pieces(value, count):
    high = value.astype(BF16)
    if count == 1:
        return [high]
    return [high, (value - high.astype(F32)).astype(BF16)]


def newton_kernel(margin_ref, out_ref):
    stacked = margin_ref[...]
    whole = stacked.astype(F32)
    real, imag = whole[:NB], whole[NB:]
    magnitude = jnp.sqrt(real * real + imag * imag)
    colmax = jnp.max(jnp.sum(magnitude, axis=0, keepdims=True), axis=1, keepdims=True)
    rowmax = jnp.max(jnp.sum(magnitude, axis=1, keepdims=True), axis=0, keepdims=True)
    factor = 1.0 / (colmax * rowmax + EPS_SCALE)
    iterate = jnp.concatenate([real * factor, imag * factor], 1)

    for turn in range(NEWTON):
        terms = 1 if turn < NEWTON // 2 else 2
        parts = pieces(iterate, terms)
        product = None
        for part in parts:
            crossed = jnp.concatenate([part[:, NB:], -part[:, :NB]], 1)
            right = jnp.concatenate([part, crossed], 0)
            term = lax.dot_general(
                stacked, right, (((0,), (0,)), ((), ())), preferred_element_type=F32
            )
            product = term if product is None else product + term
        seconds = pieces(product, terms)
        change = None
        for j, second in enumerate(seconds):
            crossed = jnp.concatenate([-second[:, NB:], second[:, :NB]], 1)
            right = jnp.concatenate([second, crossed], 0)
            for i, part in enumerate(parts):
                if i + j < terms:
                    term = dot(part, right)
                    change = term if change is None else change + term
        iterate = 2.0 * iterate - change
    out_ref[...] = iterate.astype(BF16)


def slope(dual, following, dual_before, before):
    real, imag = dual[:, :NB], dual[:, NB:]
    forward = jnp.concatenate(
        [jnp.concatenate([-imag, real], 1), jnp.concatenate([-real, -imag], 1)], 0
    )
    real, imag = dual_before[:, :NB], dual_before[:, NB:]
    backward = jnp.concatenate(
        [jnp.concatenate([imag, real], 1), jnp.concatenate([-real, imag], 1)], 0
    )
    return dot(forward, following) - dot(backward, before).astype(BF16).astype(F32)


def squares(grad):
    part = grad[0:8]
    part = part * part
    for row in range(8, grad.shape[0], 8):
        more = grad[row : row + 8]
        part = part + more * more
    return part[:, 0:128] + part[:, 128:256] + part[:, 256:384] + part[:, 384:512]


def orders_kernel(
    flags, y_1, y0, y1, before, p0, p1, p2, closing, beyond, g0, g1, p_1, out_ref, far
):
    choose(flags[0], closing, before, p_1)
    grad = slope(y0[...], p1[...], y_1[...], p_1[...])
    g0[...] = grad
    part = squares(grad)
    high = part.astype(BF16).astype(F32)
    pair = jnp.concatenate([high, part - high], 0).astype(BF16)
    here = grad.astype(BF16)
    choose(flags[2], beyond, p2, far)
    ahead = slope(y1[...], far[...], y0[...], p0[...]).astype(BF16)
    g1[...] = ahead
    first = (margin(here, p1[...]) + margin(p0[...], ahead)).astype(BF16)
    second = margin(here, ahead).astype(BF16)
    for part in range(PARTS):
        rows = slice(CHUNK * part, CHUNK * (part + 1))
        for index, value in enumerate((first, second)):
            for half in range(2):
                at = pl.ds(CHUNK * (2 * index + half), CHUNK)
                out_ref[part, at, :] = value[rows, 128 * half : 128 * (half + 1)]
        out_ref[part, pl.ds(4 * CHUNK, CHUNK), :] = pair


def slope_kernel(y_1, y0, p_1, p1, g0, total_ref):
    grad = slope(y0[...], p1[...], y_1[...], p_1[...])
    g0[...] = grad
    part = jnp.sum(squares(grad), axis=0, keepdims=True)
    total_ref[...] = jnp.broadcast_to(part[None], total_ref.shape)


def step_size(total_ref):
    part = jnp.sum(total_ref[...], axis=0)
    total = jnp.sum(jnp.sum(part, axis=1, keepdims=True), axis=0, keepdims=True)
    return TAU_STEP / jnp.sqrt(total / (2 * NK * NB * NPW) + EPS_NORM)


def advance_kernel(flags, total, y_2, y_1, p_2, p_1, p0, p1, closing, g0, g1, q_1, q0, q1, far):
    size = step_size(total)
    q0[...] = (p0[...].astype(F32) + size * g0[...]).astype(BF16)
    q1[...] = (p1[...].astype(F32) + size * g1[...].astype(F32)).astype(BF16)
    choose(flags[1], closing, p_2, far)
    grad = slope(y_1[...], p0[...], y_2[...], far[...])
    q_1[...] = (p_1[...].astype(F32) + size * grad).astype(BF16)


def finish_kernel(total_ref, p0, g0, re_ref, im_ref):
    size = step_size(total_ref)
    value = (p0[...].astype(F32) + size * g0[...]).astype(BF16)
    re_ref[...] = value[:NB]
    im_ref[...] = value[NB:]


def shifted(value, by):
    return lax.ppermute(value, "kstr", [(i, (i + by) % NK) for i in range(NK)])


def exchange(value, axis):
    return lax.all_to_all(value, axis, 0, 0, tiled=True)


def whole_total(part):
    parts = exchange(part, "pw")
    own = call(spread_kernel, shape((NK, 1, 128), F32), parts)
    return exchange(own, "kstr")


def inverse(whole):
    return call(newton_kernel, shape((NB, 2 * NB), BF16), whole)


def body(states_re, states_im, gmap):
    width = states_re.shape[2]
    row = lax.axis_index("kstr")
    offset = jnp.mod(gmap[0] - lax.axis_index("pw") * width, NPW)
    blocks = offset // width
    rest = offset - blocks * width
    first = row < NK // 2
    bounds = jnp.stack(
        [
            jnp.where(first, rest, 0),
            jnp.where(first, width, width - rest),
            jnp.where(first, jnp.mod(width - rest, width), rest),
        ]
    ).astype(jnp.int32)
    state = jnp.concatenate([states_re[0], states_im[0]], 0)
    full = 2 * NB
    end = NK - 1
    duals = shape((NB, full), BF16)
    fields = shape((full, width), BF16)
    grads = shape((full, width), F32)
    chunk = shape((CHUNK, NB), F32)
    chunks = shape((PARTS, CHUNK, NB), BF16)
    far_scratch = (pltpu.VMEM((full, width), BF16),)
    flags = jnp.stack([row == 0, row <= 1, row >= NK - 2, row == end]).astype(jnp.int32)

    beside = lax.ppermute(state, ("kstr", "pw"), beside_pairs())
    p1, p_2 = shifted(state, -1), shifted(state, 2)
    p2 = shifted(state, -2)
    merged = call(merge_kernel, fields, bounds, state, beside, smem=1)
    near = close_string(merged, blocks)
    near, p1, p2, p_2 = lax.optimization_barrier((near, p1, p2, p_2))

    part, p1 = call(first_margin_kernel, (shape((full, NB), BF16), fields), flags, state, p1, near, smem=1)
    state, near, part = lax.optimization_barrier((state, near, part))
    p_1 = shifted(state, 1)
    far = lax.ppermute(near, "kstr", [(0, 1), (1, 0), (end - 1, end), (end, end - 1)])
    parts = exchange(part, "pw").reshape(PARTS, CHUNK, NB)
    own, kept = call(collect_kernel, (chunks, chunk), parts)
    whole = exchange(own.reshape(full, NB), "pw")
    whole, far, p_1 = lax.optimization_barrier((whole, far, p_1))

    y0 = inverse(whole)
    y_1 = shifted(y0, 1)
    y1 = shifted(y0, -1)
    g0, g1, p_1, part = call(
        orders_kernel,
        (grads, fields, fields, shape((PARTS, 5 * CHUNK, 128), BF16)),
        *(flags, y_1, y0, y1, p_1, state, p1, p2, near, far),
        smem=1,
        scratch=far_scratch,
    )
    y0, part = lax.optimization_barrier((y0, part))
    y_2 = shifted(y0, 2)
    parts = exchange(part, "pw")
    first, second, total = call(
        collect_orders_kernel, (chunk, chunk, shape((NK, 1, 128), F32)), parts
    )
    total = exchange(total, "kstr")
    own = call(combine_kernel, chunks, total, kept, first, second)
    whole = exchange(own.reshape(full, NB), "pw")
    q_1, q0, q1 = call(
        advance_kernel,
        (fields, fields, fields),
        *(flags, total, y_2, y_1, p_2, p_1, state, p1, far, g0, g1),
        smem=1,
        scratch=far_scratch,
    )

    y0 = inverse(whole)
    y_1 = shifted(y0, 1)
    g0, total = call(slope_kernel, (grads, shape((PARTS, 1, 128), F32)), y_1, y0, q_1, q1)
    total = whole_total(total)
    half = shape((NB, width), BF16)
    new_re, new_im = call(finish_kernel, (half, half), total, q0, g0)
    return new_re[None], new_im[None]


def solution(mesh):
    placed = (P("kstr", None, "pw"), P("kstr", None, "pw"), P("pw"))
    return jax.shard_map(
        body,
        mesh=mesh,
        in_specs=placed,
        out_specs=(P("kstr", None, "pw"), P("kstr", None, "pw")),
        check_vma=False,
    )
```
